32 devices in a mesh: dp: 2 (over x), space: 16 (over z, y, core).
Axes of the slice: x: 2, y: 2, z: 4, core: 2. Of those that a mesh axis runs over, the one named last changes fastest.
Arguments:
- features: bfloat16 [2, 16384, 256], P('dp', 'space'), may hold values from -6 to 6
- weight: bfloat16 [2048, 256], P(('dp', 'space')), may hold values from -0.125 to 0.125
- rulebook: int32 [2, 128, 3, 8], P('dp', 'space'), may hold values from 0 to 15, as said below
- rule_counts: int32 [2, 128], P('dp', 'space'), may hold values from 1 to 8, as said below
- cotangent: bfloat16 [2, 8192, 256], P('dp', 'space'), may hold values from -6 to 6
Outputs:
- activated: bfloat16 [2, 8192, 256], P('dp', 'space')
- grad_features: bfloat16 [2, 16384, 256], P('dp', 'space')
- grad_weight: float32 [2048, 256], P(('dp', 'space'))
The draws below stay inside these ranges and needn't reach their ends.
Inputs may be any that keep to these rules, and one draw needn't show every extreme that they name: `rulebook`: in the row of slab s the owner is s - 1, s or s + 1 and lies in 0 to 15; the input block lies in 0 to 7; the output block lies in 0 to 3, and in 2 to 3 when the owner is s - 1, in 0 to 1 when it is s + 1. Padded slots hold entries of the same kind. A block may appear in several rules. `rule_counts`: some slab and offset has 8 live rules in every draw.
All inputs are finite; a program needn't handle non-finite values.
Results may differ from the reference program's by a relative error of at most 0.0049.
Values may be sent and summed in bfloat16 or wider, within the bound.
No kernel may reach another device: no remote copies, remote signals or barrier semaphores. Data moves between devices by JAX's collectives and lax.ppermute only.
A program may use at most 64 MiB of HBM per device.

```python
import jax
import jax.numpy as jnp
from jax import lax

CI = 256
CO = 256
OFFS = 8
BR = 128
BND = 2
SLOTS = 8
IN_BLK = 8
OUT_BLK = 4
SCENES = 2
N_SPACE = 16


def draw_rulebook(key, part):
    key = jax.random.fold_in(key, 11)
    first, second, third, fourth = jax.random.split(key, 4)
    shape = (SCENES, N_SPACE * OFFS, SLOTS)
    device = lax.broadcasted_iota(jnp.int32, shape, 1) // OFFS
    in_index = jax.random.randint(first, shape, 0, IN_BLK)
    code = jax.random.randint(second, shape, 0, 4)
    relative = jnp.where(code == 0, -1, jnp.where(code == 3, 1, 0))
    relative = jnp.where(device + relative < 0, 0, relative)
    relative = jnp.where(device + relative > N_SPACE - 1, 0, relative)
    inner = jax.random.randint(third, shape, 0, OUT_BLK)
    rim = jax.random.randint(fourth, shape, 0, BND)
    out_index = jnp.where(relative == 0, inner, jnp.where(relative < 0, OUT_BLK - BND + rim, rim))
    return jnp.stack([in_index, out_index, device + relative], axis=2).astype(jnp.int32)


def draw_rule_counts(key, part):
    key = jax.random.fold_in(key, 23)
    first, second, third, fourth = jax.random.split(key, 4)
    heavy = jax.random.randint(first, (SCENES, N_SPACE, 1), 0, 4) == 0
    high = jax.random.randint(second, (SCENES, N_SPACE, OFFS), SLOTS // 2, SLOTS + 1)
    low = jax.random.randint(third, (SCENES, N_SPACE, OFFS), 1, SLOTS // 2 + 1)
    counts = jnp.where(heavy, high, low).reshape(SCENES, N_SPACE * OFFS)
    chosen = jax.random.randint(fourth, (), 0, SCENES * N_SPACE * OFFS)
    flat = lax.broadcasted_iota(jnp.int32, (SCENES, N_SPACE * OFFS), 0) * (N_SPACE * OFFS) + lax.broadcasted_iota(jnp.int32, (SCENES, N_SPACE * OFFS), 1)
    return jnp.where(flat == chosen, SLOTS, counts).astype(jnp.int32)


def shard_levels(rng, extent, pieces, low, largest):
    def one(position, blocks):
        draws = jax.random.uniform(jax.random.fold_in(jax.random.fold_in(rng, 6), position), (blocks,), jnp.float32, low / len(pieces), largest / len(pieces))
        return jnp.repeat(jnp.exp(draws), extent[position] // blocks).reshape((-1,) + (1,) * (len(extent) - position - 1))

    loudness = one(*pieces[0])
    for cut in pieces[1:]:
        loudness = loudness * one(*cut)
    return loudness


def noise(stream_key, shape, scale, most, cuts=(), kind=jnp.bfloat16):
    drawn = jax.random.normal(stream_key, shape, jnp.float32) * scale
    if len(cuts) > 0:
        drawn = shard_levels(stream_key, shape, cuts, -0.22, 0.18) * drawn
    return jnp.clip(drawn, min=-most, max=most).astype(kind)


def setup_inputs(seed: int = 0) -> dict:
    key_of = jax.random.split(jax.random.key(seed), 6)
    features = noise(key_of[0], (SCENES, N_SPACE * IN_BLK * BR, CI), 1.0, 6.0, ((0, 2), (1, 16)))
    weight = noise(key_of[1], (OFFS * CI, CO), (OFFS * CI) ** -0.5, 0.125, ((0, 32),))
    rulebook = draw_rulebook(jax.random.fold_in(key_of[5], 71), 0)
    rule_counts = draw_rule_counts(jax.random.fold_in(key_of[5], 71), 0)
    cotangent = noise(key_of[4], (SCENES, N_SPACE * OUT_BLK * BR, CO), 1.0, 6.0, ((0, 2), (1, 16)))
    return {"features": features, "weight": weight, "rulebook": rulebook, "rule_counts": rule_counts, "cotangent": cotangent}


grad_scale = 1.0 / 2048.0


def reference(features, weight, rulebook, rule_counts, cotangent):
    kernel = weight.reshape(OFFS, CI, CO)
    slot_ids = jnp.arange(SLOTS, dtype=jnp.int32)
    slab_ids = jnp.arange(N_SPACE, dtype=jnp.int32)
    total_in = N_SPACE * IN_BLK
    total_out = N_SPACE * OUT_BLK
    grad_total = jnp.zeros((OFFS, CI, CO), jnp.float32)
    outs_act = []
    outs_grad = []
    for scene in range(SCENES):
        blocks = features[scene].reshape(total_in, BR, CI)
        rules = rulebook[scene].reshape(N_SPACE, OFFS, 3, SLOTS)
        counts = rule_counts[scene].reshape(N_SPACE, OFFS)
        in_global = (rules[:, :, 0, :] + slab_ids[:, None, None] * IN_BLK).astype(jnp.int32)
        out_global = (rules[:, :, 2, :] * OUT_BLK + rules[:, :, 1, :]).astype(jnp.int32)
        live = slot_ids[None, None, :] < counts[:, :, None]
        in_off = jnp.transpose(in_global, (1, 0, 2)).reshape(OFFS, N_SPACE * SLOTS)
        out_off = jnp.transpose(out_global, (1, 0, 2)).reshape(OFFS, N_SPACE * SLOTS)
        live_off = jnp.transpose(live, (1, 0, 2)).reshape(OFFS, N_SPACE * SLOTS)

        def forward_step(carry, item):
            in_idx, out_idx, alive, kern = item
            picked = blocks[in_idx].reshape(N_SPACE * SLOTS * BR, CI)
            prod = jnp.dot(picked, kern, preferred_element_type=jnp.float32)
            prod = prod.reshape(N_SPACE * SLOTS, BR, CO) * alive.astype(jnp.float32)[:, None, None]
            return carry + jax.ops.segment_sum(prod, out_idx, num_segments=total_out), None

        pre, _ = lax.scan(forward_step, jnp.zeros((total_out, BR, CO), jnp.float32), (in_off, out_off, live_off, kernel))
        sigma = jax.nn.sigmoid(pre)
        activated = (pre * sigma).astype(jnp.bfloat16)
        upstream = cotangent[scene].reshape(total_out, BR, CO).astype(jnp.float32)
        grad_pre = (upstream * sigma * (1.0 + pre * (1.0 - sigma))).astype(jnp.bfloat16)

        def backward_step(carry, item):
            in_idx, out_idx, alive, kern = item
            rule_grads = grad_pre[out_idx] * alive.astype(jnp.bfloat16)[:, None, None]
            rule_flat = rule_grads.reshape(N_SPACE * SLOTS * BR, CO)
            back = jnp.dot(rule_flat, kern.T, preferred_element_type=jnp.float32)
            back = back.reshape(N_SPACE * SLOTS, BR, CI)
            picked = blocks[in_idx].reshape(N_SPACE * SLOTS * BR, CI)
            term = jnp.dot(picked.T, rule_flat, preferred_element_type=jnp.float32)
            return carry + jax.ops.segment_sum(back, in_idx, num_segments=total_in), term

        grad_in, terms = lax.scan(backward_step, jnp.zeros((total_in, BR, CI), jnp.float32), (in_off, out_off, live_off, kernel))
        grad_total = grad_total + terms
        outs_act.append(activated.reshape(total_out * BR, CO))
        outs_grad.append(grad_in.astype(jnp.bfloat16).reshape(total_in * BR, CI))
    grad_weight = (grad_total * grad_scale).reshape(OFFS * CI, CO)
    return jnp.stack(outs_act, 0), jnp.stack(outs_grad, 0), grad_weight
```

```python
import functools

import jax
import jax.numpy as jnp
from jax import lax
from jax.experimental import pallas as pl
from jax.experimental.pallas import tpu as pltpu
from jax.sharding import PartitionSpec as P

CI = 256
CO = 256
OFFS = 8
BR = 128
BND = 2
SLOTS = 8
IN_BLK = 8
OUT_BLK = 4
EXT = OUT_BLK + 2 * BND
AXES = ("dp", "space")

grad_scale = 1.0 / 2048.0

VMEM = pl.BlockSpec(memory_space=pltpu.VMEM)
SMEM = pl.BlockSpec(memory_space=pltpu.SMEM)


def phases_of(dp, space):
    space_bits = [1 << b for b in reversed(range(space.bit_length() - 1))]
    dp_bits = [space << b for b in reversed(range(dp.bit_length() - 1))]
    order = space_bits[:-1] + dp_bits
    return [order[i : i + 2] for i in range(0, len(order), 2)] + [space_bits[-1:]]


def masks_of(group):
    return [
        sum(bit for t, bit in enumerate(group) if r >> t & 1) for r in range(1, 1 << len(group))
    ]


def position_of(index, groups):
    place = 0
    for t, bit in enumerate([bit for group in groups for bit in group]):
        place = place | (jnp.where((index & bit) != 0, 1, 0) << t)
    return place


def exchange(value, mask, devices):
    return lax.ppermute(value, AXES, [(i, i ^ mask) for i in range(devices)])


def from_behind(value, steps):
    count = lax.axis_size("space")
    first, last = (max(0, -steps), min(count, count - steps))
    return lax.ppermute(value, "space", [(source, source + steps) for source in range(first, last)])


def rule_slots(rules_ref, counts_ref, offset, space_index):
    rules = []
    for j in range(SLOTS):
        in_index = rules_ref[offset, 0, j]
        out_index = rules_ref[offset, 1, j]
        relative = rules_ref[offset, 2, j] - space_index
        slot = BND + out_index + relative * OUT_BLK
        slot = jnp.where(j < counts_ref[offset], slot, EXT)
        rules.append((in_index, slot))
    return rules


def transpose_kernel(x_ref, xt_ref):
    for i in range(IN_BLK):
        xt_ref[i] = x_ref[i].T


def forward_kernel(rules_ref, counts_ref, place_ref, x_ref, *refs):
    w_refs, (lower_ref, upper_ref, own_ref, w_ref, acc) = refs[:-5], refs[-5:]
    space_index = place_ref[0]
    if len(w_refs) == 2:
        near, far = w_refs
        core = space_index & 1
        pairs, rows = near.shape[0], near.shape[1]
        for pair in range(pairs):
            place = place_ref[1 + pair]
            a, b = near[place], far[place]
            w_ref[pl.ds(2 * pair * rows, rows)] = jnp.where(core == 0, a, b)
            w_ref[pl.ds((2 * pair + 1) * rows, rows)] = jnp.where(core == 0, b, a)
    else:
        w_ref[...] = w_refs[0][...]
    acc[...] = jnp.zeros_like(acc)
    for offset in range(OFFS):
        rules = rule_slots(rules_ref, counts_ref, offset, space_index)
        picked = jnp.concatenate([x_ref[i] for i, _ in rules], 0)
        kernel = w_ref[pl.ds(offset * CI, CI)]
        product = jnp.dot(picked, kernel, preferred_element_type=jnp.float32)
        for j, (_, slot) in enumerate(rules):
            acc[slot] += product[j * BR : (j + 1) * BR]
    lower_ref[...] = acc[:BND].astype(jnp.bfloat16)
    upper_ref[...] = acc[BND + OUT_BLK : EXT].astype(jnp.bfloat16)
    own_ref[...] = acc[BND : BND + OUT_BLK]


def weight_grad_kernel(
    rules_ref, counts_ref, place_ref, xt_ref, low_ref, own_ref, high_ref, g_ref, *outs
):
    space_index = place_ref[0]
    g_ref[:BND] = low_ref[...]
    g_ref[BND : BND + OUT_BLK] = own_ref[...]
    g_ref[BND + OUT_BLK : EXT] = high_ref[...]
    g_ref[EXT] = jnp.zeros((BR, CO), jnp.bfloat16)
    core = space_index & 1
    for offset in range(OFFS):
        rules = rule_slots(rules_ref, counts_ref, offset, space_index)
        left = jnp.concatenate([xt_ref[i] for i, _ in rules], 1)
        right = jnp.concatenate([g_ref[slot] for _, slot in rules], 0)
        term = jnp.dot(left, right, preferred_element_type=jnp.float32)
        if len(outs) == 2:
            keep_ref, send_ref = outs
            rows = keep_ref.shape[1]
            pairs = CI // (2 * rows)
            for pair in range(pairs):
                place = place_ref[1 + offset * pairs + pair]
                a = term[2 * pair * rows : (2 * pair + 1) * rows]
                b = term[(2 * pair + 1) * rows : (2 * pair + 2) * rows]
                keep_ref[place] = jnp.where(core == 0, a, b)
                send_ref[place] = jnp.where(core == 0, b, a).astype(jnp.bfloat16)
        else:
            outs[0][pl.ds(offset * CI, CI)] = term


def feature_grad_kernel(rules_ref, counts_ref, place_ref, g_ref, w_ref, out_ref, acc):
    space_index = place_ref[0]
    acc[...] = jnp.zeros_like(acc)
    for offset in range(OFFS):
        rules = rule_slots(rules_ref, counts_ref, offset, space_index)
        grads = jnp.concatenate([g_ref[slot] for _, slot in rules], 0)
        kernel = w_ref[pl.ds(offset * CI, CI)]
        back = lax.dot_general(
            grads, kernel, (((1,), (1,)), ((), ())), preferred_element_type=jnp.float32
        )
        for j, (i, _) in enumerate(rules):
            acc[i] += back[j * BR : (j + 1) * BR]
    out_ref[...] = acc[...].astype(jnp.bfloat16)


def call(kernel, name, in_specs, out_shape, scratch=(), flops=0, moved=0):
    return pl.pallas_call(
        kernel,
        name=name,
        out_shape=out_shape,
        in_specs=in_specs,
        out_specs=jax.tree.map(lambda _: VMEM, out_shape),
        scratch_shapes=list(scratch),
        compiler_params=pltpu.CompilerParams(vmem_limit_bytes=24 * 1024 * 1024),
        cost_estimate=pl.CostEstimate(flops=flops, bytes_accessed=moved, transcendentals=0),
    )


def shape(dims, dtype):
    return jax.ShapeDtypeStruct(dims, dtype)


def local(features, weight, rulebook, rule_counts, cotangent):
    dp, space = lax.axis_size("dp"), lax.axis_size("space")
    devices = dp * space
    groups = phases_of(dp, space)
    rows = weight.shape[0]
    direct = rows % 16 == 0
    me = lax.axis_index("dp") * space + lax.axis_index("space")
    blocks = features[0].reshape(IN_BLK, BR, CI)
    rules, counts = rulebook[0], rule_counts[0]
    half = (1 << sum(len(group) for group in groups[:-1])) - 1
    pair_place = position_of(jnp.arange(devices // 2, dtype=jnp.int32) * 2 ^ (me & -2), groups) & half
    place = jnp.concatenate([lax.axis_index("space").astype(jnp.int32)[None], pair_place])
    if not direct:
        place = place[:1]

    xt = call(
        transpose_kernel, "transpose", [VMEM], shape((IN_BLK, CI, BR), jnp.bfloat16)
    )(blocks)

    parts = weight[None]
    for group in groups[:-1]:
        received = [exchange(parts, mask, devices) for mask in masks_of(group)]
        parts = jnp.concatenate([parts] + received, 0)
    far = exchange(parts, groups[-1][0], devices)
    if direct:
        gathered = (parts, far)
    else:
        order = position_of(jnp.arange(devices, dtype=jnp.int32) ^ me, groups)
        gathered = (jnp.concatenate([parts, far], 0)[order].reshape(OFFS * CI, CO),)

    rule_flops = 2 * OFFS * SLOTS * BR * CI * CO
    lower, upper, own, kernels = call(
        forward_kernel,
        "forward",
        [SMEM, SMEM, SMEM, VMEM] + [VMEM] * len(gathered),
        (
            shape((BND, BR, CO), jnp.bfloat16),
            shape((BND, BR, CO), jnp.bfloat16),
            shape((OUT_BLK, BR, CO), jnp.float32),
            shape((OFFS * CI, CO), jnp.bfloat16),
        ),
        [pltpu.VMEM((EXT + 1, BR, CO), jnp.float32)],
        rule_flops,
        1 << 22,
    )(rules, counts, place, blocks, *gathered)

    from_below = from_behind(upper, 1)
    from_above = from_behind(lower, -1)
    summed = own + jnp.concatenate([from_below, from_above], 0).astype(jnp.float32)
    sigma = jax.nn.sigmoid(summed)
    activated = (summed * sigma).astype(jnp.bfloat16)
    upstream = cotangent[0].reshape(OUT_BLK, BR, CO).astype(jnp.float32)
    grad_pre = (upstream * sigma * (1.0 + summed * (1.0 - sigma))).astype(jnp.bfloat16)
    grad_low = from_behind(grad_pre[OUT_BLK - BND :], 1)
    grad_high = from_behind(grad_pre[:BND], -1)

    if direct:
        grad_shapes = (
            shape((devices // 2, rows, CO), jnp.float32),
            shape((devices // 2, rows, CO), jnp.bfloat16),
        )
    else:
        grad_shapes = (shape((OFFS * CI, CO), jnp.float32),)
    wide, *grads = call(
        weight_grad_kernel,
        "weight_grad",
        [SMEM, SMEM, SMEM, VMEM, VMEM, VMEM, VMEM],
        (shape((EXT + 1, BR, CO), jnp.bfloat16),) + grad_shapes,
        (),
        rule_flops,
        1 << 22,
    )(rules, counts, place, xt, grad_low, grad_pre, grad_high)

    grad_in = call(
        feature_grad_kernel,
        "feature_grad",
        [SMEM, SMEM, SMEM, VMEM, VMEM],
        shape((IN_BLK, BR, CI), jnp.bfloat16),
        [pltpu.VMEM((IN_BLK, BR, CI), jnp.float32)],
        rule_flops,
        1 << 22,
    )(rules, counts, place, wide, kernels)

    if direct:
        keep, send = grads
    else:
        source = jnp.zeros((devices,), jnp.int32).at[order].set(jnp.arange(devices, dtype=jnp.int32))
        ordered = grads[0].reshape(devices, rows, CO)[source]
        keep, send = ordered[: devices // 2], ordered[devices // 2 :].astype(jnp.bfloat16)
    total = keep + exchange(send, groups[-1][0], devices).astype(jnp.float32)
    for group in reversed(groups[:-1]):
        masks = masks_of(group)
        count = total.shape[0] // (len(masks) + 1)
        received = [
            exchange(total[(r + 1) * count : (r + 2) * count].astype(jnp.bfloat16), mask, devices)
            for r, mask in enumerate(masks)
        ]
        total = total[:count]
        for piece in received:
            total = total + piece.astype(jnp.float32)
    grad_weight = total[0] * grad_scale
    return (
        activated.reshape(1, OUT_BLK * BR, CO),
        grad_in.reshape(1, IN_BLK * BR, CI),
        grad_weight,
    )


def solution(mesh):
    in_specs = (
        P("dp", "space", None),
        P(("dp", "space"), None),
        P("dp", "space", None, None),
        P("dp", "space"),
        P("dp", "space", None),
    )
    out_specs = (P("dp", "space", None), P("dp", "space", None), P(("dp", "space"), None))
    return jax.shard_map(local, mesh=mesh, in_specs=in_specs, out_specs=out_specs, check_vma=False)
```

```python
import jax
import jax.numpy as jnp
from jax import lax
from jax.experimental import pallas as pl
from jax.experimental.pallas import tpu as pltpu
from jax.sharding import Mesh
from jax.sharding import PartitionSpec as P

CI = 256
CO = 256
OFFS = 8
BR = 128
BND = 2
SLOTS = 8
IN_BLK = 8
OUT_BLK = 4
EXT = OUT_BLK + 2 * BND
SPACE = ("pair", "half")

grad_scale = 1.0 / 2048.0

VMEM = pl.BlockSpec(memory_space=pltpu.VMEM)
SMEM = pl.BlockSpec(memory_space=pltpu.SMEM)


def exchange(value):
    return lax.ppermute(value, "half", [(0, 1), (1, 0)])


def from_behind(value, steps):
    count = lax.axis_size(SPACE)
    first, last = (max(0, -steps), min(count, count - steps))
    return lax.ppermute(value, SPACE, [(source, source + steps) for source in range(first, last)])


def rule_slots(rules_ref, counts_ref, offset, space_index):
    rules = []
    for j in range(SLOTS):
        in_index = rules_ref[offset, 0, j]
        out_index = rules_ref[offset, 1, j]
        relative = rules_ref[offset, 2, j] - space_index
        slot = BND + out_index + relative * OUT_BLK
        slot = jnp.where(j < counts_ref[offset], slot, EXT)
        rules.append((in_index, slot))
    return rules


def transpose_kernel(x_ref, xt_ref):
    for i in range(IN_BLK):
        xt_ref[i] = x_ref[i].T


def forward_kernel(
    rules_ref, counts_ref, place_ref, x_ref, near_ref, far_ref, lower_ref, upper_ref, own_ref, w_ref, acc
):
    space_index = place_ref[0]
    core = space_index & 1
    pairs, rows = near_ref.shape[0], near_ref.shape[1]
    for pair in range(pairs):
        a, b = near_ref[pair], far_ref[pair]
        w_ref[pl.ds(2 * pair * rows, rows)] = jnp.where(core == 0, a, b)
        w_ref[pl.ds((2 * pair + 1) * rows, rows)] = jnp.where(core == 0, b, a)
    acc[...] = jnp.zeros_like(acc)
    for offset in range(OFFS):
        rules = rule_slots(rules_ref, counts_ref, offset, space_index)
        picked = jnp.concatenate([x_ref[i] for i, _ in rules], 0)
        kernel = w_ref[pl.ds(offset * CI, CI)]
        product = jnp.dot(picked, kernel, preferred_element_type=jnp.float32)
        for j, (_, slot) in enumerate(rules):
            acc[slot] += product[j * BR : (j + 1) * BR]
    lower_ref[...] = acc[:BND].astype(jnp.bfloat16)
    upper_ref[...] = acc[BND + OUT_BLK : EXT].astype(jnp.bfloat16)
    own_ref[...] = acc[BND : BND + OUT_BLK]


def weight_grad_kernel(
    rules_ref, counts_ref, place_ref, xt_ref, low_ref, own_ref, high_ref, g_ref, keep_ref, send_ref
):
    space_index = place_ref[0]
    g_ref[:BND] = low_ref[...]
    g_ref[BND : BND + OUT_BLK] = own_ref[...]
    g_ref[BND + OUT_BLK : EXT] = high_ref[...]
    g_ref[EXT] = jnp.zeros((BR, CO), jnp.bfloat16)
    core = space_index & 1
    for offset in range(OFFS):
        rules = rule_slots(rules_ref, counts_ref, offset, space_index)
        left = jnp.concatenate([xt_ref[i] for i, _ in rules], 1)
        right = jnp.concatenate([g_ref[slot] for _, slot in rules], 0)
        term = jnp.dot(left, right, preferred_element_type=jnp.float32)
        rows = keep_ref.shape[1]
        pairs = CI // (2 * rows)
        for pair in range(pairs):
            a = term[2 * pair * rows : (2 * pair + 1) * rows]
            b = term[(2 * pair + 1) * rows : (2 * pair + 2) * rows]
            keep_ref[offset * pairs + pair] = jnp.where(core == 0, a, b)
            send_ref[offset * pairs + pair] = jnp.where(core == 0, b, a).astype(jnp.bfloat16)


def feature_grad_kernel(rules_ref, counts_ref, place_ref, g_ref, w_ref, out_ref, acc):
    space_index = place_ref[0]
    acc[...] = jnp.zeros_like(acc)
    for offset in range(OFFS):
        rules = rule_slots(rules_ref, counts_ref, offset, space_index)
        grads = jnp.concatenate([g_ref[slot] for _, slot in rules], 0)
        kernel = w_ref[pl.ds(offset * CI, CI)]
        back = lax.dot_general(
            grads, kernel, (((1,), (1,)), ((), ())), preferred_element_type=jnp.float32
        )
        for j, (i, _) in enumerate(rules):
            acc[i] += back[j * BR : (j + 1) * BR]
    out_ref[...] = acc[...].astype(jnp.bfloat16)


def call(kernel, name, in_specs, out_shape, scratch=(), flops=0, moved=0):
    return pl.pallas_call(
        kernel,
        name=name,
        out_shape=out_shape,
        in_specs=in_specs,
        out_specs=jax.tree.map(lambda _: VMEM, out_shape),
        scratch_shapes=list(scratch),
        compiler_params=pltpu.CompilerParams(vmem_limit_bytes=24 * 1024 * 1024),
        cost_estimate=pl.CostEstimate(flops=flops, bytes_accessed=moved, transcendentals=0),
    )


def shape(dims, dtype):
    return jax.ShapeDtypeStruct(dims, dtype)


def local(features, weight, rulebook, rule_counts, cotangent):
    devices = lax.axis_size(("dp",) + SPACE)
    peers = devices // 2
    rows = weight.shape[0]
    blocks = features[0].reshape(IN_BLK, BR, CI)
    rules, counts = rulebook[0], rule_counts[0]
    place = lax.axis_index(SPACE).astype(jnp.int32)[None]

    xt = call(
        transpose_kernel, "transpose", [VMEM], shape((IN_BLK, CI, BR), jnp.bfloat16)
    )(blocks)

    near = lax.all_to_all(
        jnp.broadcast_to(weight[None], (peers, rows, CO)), ("dp", "pair"), 0, 0, tiled=True
    )
    far = exchange(near)

    rule_flops = 2 * OFFS * SLOTS * BR * CI * CO
    lower, upper, own, kernels = call(
        forward_kernel,
        "forward",
        [SMEM, SMEM, SMEM, VMEM, VMEM, VMEM],
        (
            shape((BND, BR, CO), jnp.bfloat16),
            shape((BND, BR, CO), jnp.bfloat16),
            shape((OUT_BLK, BR, CO), jnp.float32),
            shape((OFFS * CI, CO), jnp.bfloat16),
        ),
        [pltpu.VMEM((EXT + 1, BR, CO), jnp.float32)],
        rule_flops,
        1 << 22,
    )(rules, counts, place, blocks, near, far)

    from_below = from_behind(upper, 1)
    from_above = from_behind(lower, -1)
    summed = own + jnp.concatenate([from_below, from_above], 0).astype(jnp.float32)
    sigma = jax.nn.sigmoid(summed)
    activated = (summed * sigma).astype(jnp.bfloat16)
    upstream = cotangent[0].reshape(OUT_BLK, BR, CO).astype(jnp.float32)
    grad_pre = (upstream * sigma * (1.0 + summed * (1.0 - sigma))).astype(jnp.bfloat16)
    grad_low = from_behind(grad_pre[OUT_BLK - BND :], 1)
    grad_high = from_behind(grad_pre[:BND], -1)

    wide, keep, send = call(
        weight_grad_kernel,
        "weight_grad",
        [SMEM, SMEM, SMEM, VMEM, VMEM, VMEM, VMEM],
        (
            shape((EXT + 1, BR, CO), jnp.bfloat16),
            shape((peers, rows, CO), jnp.float32),
            shape((peers, rows, CO), jnp.bfloat16),
        ),
        (),
        rule_flops,
        1 << 22,
    )(rules, counts, place, xt, grad_low, grad_pre, grad_high)

    grad_in = call(
        feature_grad_kernel,
        "feature_grad",
        [SMEM, SMEM, SMEM, VMEM, VMEM],
        shape((IN_BLK, BR, CI), jnp.bfloat16),
        [pltpu.VMEM((IN_BLK, BR, CI), jnp.float32)],
        rule_flops,
        1 << 22,
    )(rules, counts, place, wide, kernels)

    total = (keep + exchange(send).astype(jnp.float32)).astype(jnp.bfloat16)
    terms = lax.all_to_all(total, ("dp", "pair"), 0, 0, tiled=True)
    grad_weight = jnp.sum(terms.astype(jnp.float32), 0) * grad_scale
    return (
        activated.reshape(1, OUT_BLK * BR, CO),
        grad_in.reshape(1, IN_BLK * BR, CI),
        grad_weight,
    )


def solution(mesh):
    devices = mesh.devices
    wide = Mesh(devices.reshape(devices.shape[0], -1, 2), ("dp",) + SPACE)
    in_specs = (
        P("dp", SPACE, None),
        P(("dp",) + SPACE, None),
        P("dp", SPACE, None, None),
        P("dp", SPACE),
        P("dp", SPACE, None),
    )
    out_specs = (P("dp", SPACE, None), P("dp", SPACE, None), P(("dp",) + SPACE, None))
    return jax.shard_map(local, mesh=wide, in_specs=in_specs, out_specs=out_specs, check_vma=False)
```

```python
import jax
import jax.numpy as jnp
import numpy as np
from jax import lax
from jax.experimental import pallas as pl
from jax.experimental.pallas import tpu as pltpu
from jax.sharding import PartitionSpec as P

CI = 256
CO = 256
OFFS = 8
BR = 128
BND = 2
SLOTS = 8
IN_BLK = 8
OUT_BLK = 4
EXT = OUT_BLK + 2 * BND
IN_ROWS = IN_BLK * BR
SLABS = 3
RULES = SLABS * SLOTS
AXES = ("dp", "space")
BACK = RULES
CHUNKS = RULES + SLOTS
CORE = CHUNKS + 1
FLIP = CHUNKS + 2
PAIRS = 16
ROWS = OFFS * CI // (2 * PAIRS)

grad_scale = 1.0 / 2048.0

VMEM = pl.BlockSpec(memory_space=pltpu.VMEM)
SMEM = pl.BlockSpec(memory_space=pltpu.SMEM)


def phases_of(dp, space):
    space_bits = [1 << b for b in reversed(range(space.bit_length() - 1))]
    dp_bits = [space << b for b in reversed(range(dp.bit_length() - 1))]
    order = space_bits[:-1:2] + space_bits[1:-1:2] + dp_bits
    return [order[i : i + 2] for i in range(0, len(order), 2)] + [space_bits[-1:]]


def masks_of(group):
    return [
        sum(bit for t, bit in enumerate(group) if r >> t & 1) for r in range(1, 1 << len(group))
    ]


def position_of(index, groups):
    place = 0
    for t, bit in enumerate([bit for group in groups for bit in group]):
        place = place | (((index // bit) & 1) << t)
    return place


def exchange(value, mask, devices):
    return lax.ppermute(value, AXES, [(i, i ^ mask) for i in range(devices)])


def swap_far(value):
    count = lax.axis_size("space")
    pairs = [(s, s + 1) for s in range(1, count - 1, 2)]
    return lax.ppermute(value, "space", pairs + [(t, s) for s, t in pairs])


def owner_rules(plan_ref, offset, first):
    codes = [plan_ref[offset, first + j] for j in range(SLOTS)]
    return [(code >> 3, code & 7) for code in codes]


def main_kernel(
    positions, plan_ref, x_ref, a_ref, b_ref, near_ref, far_ref, cot_ref,
    act_ref, grad_ref, near_grad_ref, far_grad_ref, keep_ref, send_ref, w_ref,
    x_all, xt_all, acc, g_all, term_ref,
):
    core, flip = plan_ref[0, CORE], plan_ref[0, FLIP]
    for slab, ref in enumerate((x_ref, a_ref, b_ref)):
        for i in range(IN_BLK):
            block = ref[i * BR : (i + 1) * BR]
            x_all[slab * IN_BLK + i] = block
            xt_all[slab * IN_BLK + i] = block.T
    for pair, position in enumerate(positions):
        place = position ^ flip
        a, b = near_ref[place], far_ref[place]
        w_ref[2 * pair * ROWS : (2 * pair + 1) * ROWS] = jnp.where(core == 0, a, b)
        w_ref[(2 * pair + 1) * ROWS : (2 * pair + 2) * ROWS] = jnp.where(core == 0, b, a)

    acc[...] = jnp.zeros_like(acc)
    for offset in range(OFFS):
        kernel = w_ref[offset * CI : (offset + 1) * CI]

        def add_products(chunk, offset=offset, kernel=kernel):
            rules = owner_rules(plan_ref, offset, chunk * SLOTS)
            picked = jnp.concatenate([x_all[i] for i, _ in rules], 0)
            product = jnp.dot(picked, kernel, preferred_element_type=jnp.float32)
            for j, (_, slot) in enumerate(rules):
                acc[slot] += product[j * BR : (j + 1) * BR]

        add_products(0)
        pl.loop(1, plan_ref[offset, CHUNKS])(add_products)

    for o in range(OUT_BLK):
        pre = acc[o]
        sigma = jax.nn.sigmoid(pre)
        act_ref[o] = (pre * sigma).astype(jnp.bfloat16)
        upstream = cot_ref[o].astype(jnp.float32)
        grad = (upstream * sigma * (1.0 + pre * (1.0 - sigma))).astype(jnp.bfloat16)
        grad_ref[o] = grad
        g_all[o] = grad
    g_all[OUT_BLK] = jnp.zeros((BR, CO), jnp.bfloat16)
    low, high = grad_ref[:BND], grad_ref[OUT_BLK - BND :]
    near_grad_ref[...] = jnp.where(core == 0, high, low)
    far_grad_ref[...] = jnp.where(core == 0, low, high)

    for offset in range(OFFS):

        def terms(chunk, offset=offset):
            rules = owner_rules(plan_ref, offset, chunk * SLOTS)
            left = jnp.concatenate([xt_all[i] for i, _ in rules], 1)
            right = jnp.concatenate([g_all[slot] for _, slot in rules], 0)
            return jnp.dot(left, right, preferred_element_type=jnp.float32)

        def add_terms(chunk):
            term_ref[...] += terms(chunk)

        term_ref[...] = terms(0)
        pl.loop(1, plan_ref[offset, CHUNKS])(add_terms)
        per = CI // (2 * ROWS)
        for pair in range(per):
            place = positions[offset * per + pair] ^ flip
            a = term_ref[2 * pair * ROWS : (2 * pair + 1) * ROWS]
            b = term_ref[(2 * pair + 1) * ROWS : (2 * pair + 2) * ROWS]
            keep_ref[place] = jnp.where(core == 0, a, b)
            send_ref[place] = jnp.where(core == 0, b, a).astype(jnp.bfloat16)


def feature_grad_kernel(plan_ref, grad_ref, near_ref, far_ref, w_ref, out_ref, g_all, acc):
    core = plan_ref[0, CORE]
    near, far = near_ref[...], far_ref[...]
    g_all[:BND] = jnp.where(core == 0, far, near)
    g_all[BND : BND + OUT_BLK] = grad_ref[...]
    g_all[BND + OUT_BLK : EXT] = jnp.where(core == 0, near, far)
    g_all[EXT] = jnp.zeros((BR, CO), jnp.bfloat16)
    acc[...] = jnp.zeros_like(acc)
    for offset in range(OFFS):
        codes = [plan_ref[offset, BACK + j] for j in range(SLOTS)]
        rules = [(code >> 4, code & 15) for code in codes]
        grads = jnp.concatenate([g_all[slot] for _, slot in rules], 0)
        kernel = w_ref[offset * CI : (offset + 1) * CI]
        back = lax.dot_general(
            grads, kernel, (((1,), (1,)), ((), ())), preferred_element_type=jnp.float32
        )
        for j, (i, _) in enumerate(rules):
            acc[i] += back[j * BR : (j + 1) * BR]
    out_ref[...] = acc[...].astype(jnp.bfloat16)


def call(kernel, name, in_specs, out_shape, scratch, flops, moved):
    return pl.pallas_call(
        kernel,
        name=name,
        out_shape=out_shape,
        in_specs=in_specs,
        out_specs=jax.tree.map(lambda _: VMEM, out_shape),
        scratch_shapes=scratch,
        compiler_params=pltpu.CompilerParams(vmem_limit_bytes=24 * 1024 * 1024),
        cost_estimate=pl.CostEstimate(flops=flops, bytes_accessed=moved, transcendentals=0),
    )


def shape(dims, dtype=jnp.bfloat16):
    return jax.ShapeDtypeStruct(dims, dtype)


def plan_of(tables, slab, flip):
    slots = jnp.arange(SLOTS, dtype=jnp.int32)
    in_index = tables[:, :, 0] + IN_BLK * jnp.arange(SLABS, dtype=jnp.int32)[:, None, None]
    out_index, owner = tables[:, :, 1], tables[:, :, 2]
    valid = slots < tables[:, :, 3]
    live = jnp.swapaxes(valid & (owner == slab), 0, 1).reshape(OFFS, RULES)
    code = jnp.swapaxes(in_index * 8 + out_index, 0, 1).reshape(OFFS, RULES)
    order = jnp.arange(RULES, dtype=jnp.int32)
    earlier = order[:, None] > order[None, :]
    rank = jnp.sum(jnp.where(live[:, None, :] & earlier, 1, 0), 2)
    count = jnp.sum(jnp.where(live, 1, 0), 1, keepdims=True)
    chosen = live[:, None, :] & (rank[:, None, :] == order[:, None])
    packed = jnp.sum(jnp.where(chosen, code[:, None, :], 0), 2)
    packed = jnp.where(order < count, packed, OUT_BLK)
    ext = jnp.where(valid[0], BND + out_index[0] + (owner[0] - slab) * OUT_BLK, EXT)
    back = tables[0, :, 0] * 16 + ext
    scalars = jnp.broadcast_to(jnp.stack([slab & 1, flip]), (OFFS, 2))
    return jnp.concatenate([packed, back, (count + SLOTS - 1) // SLOTS, scalars], 1)


def local(features, weight, rulebook, rule_counts, cotangent):
    dp, space = lax.axis_size("dp"), lax.axis_size("space")
    devices = dp * space
    groups = phases_of(dp, space)
    rows = weight.shape[0]
    slab = lax.axis_index("space").astype(jnp.int32)
    me = lax.axis_index("dp").astype(jnp.int32) * space + slab
    direct = rows == ROWS

    own_table = jnp.concatenate(
        [rulebook[0], jnp.broadcast_to(rule_counts[0][:, None, None], (OFFS, 1, SLOTS))], 1
    )
    coded = jnp.pad(own_table.astype(jnp.bfloat16).reshape(1, CI), ((0, 15), (0, 0)))
    halo = jnp.concatenate([features[0], coded], 0)

    parts = weight[None]
    beside = None
    for group in groups[:-1]:
        received = [exchange(parts, mask, devices) for mask in masks_of(group)]
        if beside is None:
            beside = (exchange(halo, 1, devices), swap_far(halo))
        parts = jnp.concatenate([parts] + received, 0)
    far = exchange(parts, groups[-1][0], devices)
    slab_a, slab_b = beside

    tables = [own_table] + [
        other[IN_ROWS].reshape(OFFS, 4, SLOTS).astype(jnp.int32) for other in beside
    ]
    flip = position_of(me & -2, groups) if direct else jnp.zeros((), jnp.int32)
    plan = plan_of(jnp.stack(tables), slab, flip)
    if direct:
        near = parts
        positions = [position_of(2 * pair, groups) for pair in range(PAIRS)]
    else:
        ids = np.arange(devices, dtype=np.int32)
        order = position_of(ids ^ me, groups)
        whole = jnp.concatenate([parts, far], 0)[order].reshape(PAIRS, 2, ROWS, CO)
        swapped = jnp.where((slab & 1) == 0, whole, whole[:, ::-1])
        near, far = swapped[:, 0], swapped[:, 1]
        positions = list(range(PAIRS))

    rule_flops = 2 * OFFS * SLOTS * BR * CI * CO
    activated, grad_pre, near_grad, far_grad, keep, send, kernels = call(
        lambda *refs: main_kernel(positions, *refs),
        "forward_and_weight_grad",
        [SMEM] + [VMEM] * 6,
        (
            shape((OUT_BLK, BR, CO)),
            shape((OUT_BLK, BR, CO)),
            shape((BND, BR, CO)),
            shape((BND, BR, CO)),
            shape((PAIRS, ROWS, CO), jnp.float32),
            shape((PAIRS, ROWS, CO)),
            shape((OFFS * CI, CO)),
        ),
        [
            pltpu.VMEM((SLABS * IN_BLK, BR, CI), jnp.bfloat16),
            pltpu.VMEM((SLABS * IN_BLK, CI, BR), jnp.bfloat16),
            pltpu.VMEM((OUT_BLK + 1, BR, CO), jnp.float32),
            pltpu.VMEM((OUT_BLK + 1, BR, CO), jnp.bfloat16),
            pltpu.VMEM((CI, CO), jnp.float32),
        ],
        2 * rule_flops,
        1 << 23,
    )(plan, features[0], slab_a, slab_b, near, far, cotangent[0].reshape(OUT_BLK, BR, CO))

    if not direct:
        terms = jnp.stack([keep, send.astype(jnp.float32)], 1)
        terms = jnp.where((slab & 1) == 0, terms, terms[:, ::-1]).reshape(devices, rows, CO)
        source = np.argsort(position_of(ids, groups)).astype(np.int32) ^ me
        ordered = terms[source]
        keep, send = ordered[: devices // 2], ordered[devices // 2 :].astype(jnp.bfloat16)
    total = keep + exchange(send, groups[-1][0], devices).astype(jnp.float32)

    near_rim = exchange(near_grad, 1, devices)
    far_rim = swap_far(far_grad)
    grad_in = call(
        feature_grad_kernel,
        "feature_grad",
        [SMEM] + [VMEM] * 4,
        shape((IN_BLK, BR, CI)),
        [
            pltpu.VMEM((EXT + 1, BR, CO), jnp.bfloat16),
            pltpu.VMEM((IN_BLK, BR, CI), jnp.float32),
        ],
        rule_flops,
        1 << 22,
    )(plan, grad_pre, near_rim, far_rim, kernels)

    for group in reversed(groups[:-1]):
        masks = masks_of(group)
        count = total.shape[0] // (len(masks) + 1)
        received = [
            exchange(total[(r + 1) * count : (r + 2) * count].astype(jnp.bfloat16), mask, devices)
            for r, mask in enumerate(masks)
        ]
        total = total[:count]
        for piece in received:
            total = total + piece.astype(jnp.float32)
    grad_weight = total[0] * grad_scale
    return (
        activated.reshape(1, OUT_BLK * BR, CO),
        grad_in.reshape(1, IN_ROWS, CI),
        grad_weight,
    )


def solution(mesh):
    in_specs = (
        P("dp", "space", None),
        P(("dp", "space"), None),
        P("dp", "space", None, None),
        P("dp", "space"),
        P("dp", "space", None),
    )
    out_specs = (P("dp", "space", None), P("dp", "space", None), P(("dp", "space"), None))
    return jax.shard_map(local, mesh=mesh, in_specs=in_specs, out_specs=out_specs, check_vma=False)
```

```python
import jax
import jax.numpy as jnp
import numpy as np
from jax import lax
from jax.experimental import pallas as pl
from jax.experimental.pallas import tpu as pltpu
from jax.sharding import PartitionSpec as P

CI = 256
CO = 256
OFFS = 8
BR = 128
BND = 2
SLOTS = 8
IN_BLK = 8
OUT_BLK = 4
EXT = OUT_BLK + 2 * BND
IN_ROWS = IN_BLK * BR
SLABS = 3
RULES = SLABS * SLOTS
AXES = ("dp", "space")
BACK = RULES
CHUNKS = RULES + SLOTS
CORE = CHUNKS + 1
FLIP = CHUNKS + 2
PAIRS = 16
ROWS = OFFS * CI // (2 * PAIRS)

grad_scale = 1.0 / 2048.0

VMEM = pl.BlockSpec(memory_space=pltpu.VMEM)
SMEM = pl.BlockSpec(memory_space=pltpu.SMEM)


def phases_of(dp, space):
    space_bits = [1 << b for b in reversed(range(space.bit_length() - 1))]
    dp_bits = [space << b for b in reversed(range(dp.bit_length() - 1))]
    order = space_bits[:-1:2] + space_bits[1:-1:2] + dp_bits
    return [order[i : i + 2] for i in range(0, len(order), 2)] + [space_bits[-1:]]


def masks_of(group):
    return [
        sum(bit for t, bit in enumerate(group) if r >> t & 1) for r in range(1, 1 << len(group))
    ]


def position_of(index, groups):
    place = 0
    for t, bit in enumerate([bit for group in groups for bit in group]):
        place = place | (((index >> (bit.bit_length() - 1)) & 1) << t)
    return place


def exchange(value, mask, devices):
    return lax.ppermute(value, AXES, [(i, i ^ mask) for i in range(devices)])


def swap_far(value):
    count = lax.axis_size("space")
    pairs = [(s, s + 1) for s in range(1, count - 1, 2)]
    return lax.ppermute(value, "space", pairs + [(t, s) for s, t in pairs])


def owner_rules(plan_ref, offset, first):
    codes = [plan_ref[offset, first + j] for j in range(SLOTS)]
    return [(code >> 3, code & 7) for code in codes]


def main_kernel(
    positions, plan_ref, x_ref, a_ref, b_ref, near_ref, far_ref, cot_ref,
    act_ref, grad_ref, near_grad_ref, far_grad_ref, keep_ref, send_ref, w_ref,
    x_all, xt_all, acc, g_all, term_ref,
):
    core, flip = plan_ref[0, CORE], plan_ref[0, FLIP]
    for slab, ref in enumerate((x_ref, a_ref, b_ref)):
        for i in range(IN_BLK):
            block = ref[i * BR : (i + 1) * BR]
            x_all[slab * IN_BLK + i] = block
            xt_all[slab * IN_BLK + i] = block.T
    for pair, position in enumerate(positions):
        place = position ^ flip
        a, b = near_ref[place], far_ref[place]
        w_ref[2 * pair * ROWS : (2 * pair + 1) * ROWS] = jnp.where(core == 0, a, b)
        w_ref[(2 * pair + 1) * ROWS : (2 * pair + 2) * ROWS] = jnp.where(core == 0, b, a)

    acc[...] = jnp.zeros_like(acc)
    for offset in range(OFFS):
        kernel = w_ref[offset * CI : (offset + 1) * CI]

        def add_products(chunk, offset=offset, kernel=kernel):
            rules = owner_rules(plan_ref, offset, chunk * SLOTS)
            picked = jnp.concatenate([x_all[i] for i, _ in rules], 0)
            product = jnp.dot(picked, kernel, preferred_element_type=jnp.float32)
            for j, (_, slot) in enumerate(rules):
                acc[slot] += product[j * BR : (j + 1) * BR]

        add_products(0)
        pl.loop(1, plan_ref[offset, CHUNKS])(add_products)

    for o in range(OUT_BLK):
        pre = acc[o]
        sigma = jax.nn.sigmoid(pre)
        act_ref[o] = (pre * sigma).astype(jnp.bfloat16)
        upstream = cot_ref[o].astype(jnp.float32)
        grad = (upstream * sigma * (1.0 + pre * (1.0 - sigma))).astype(jnp.bfloat16)
        grad_ref[o] = grad
        g_all[o] = grad
    g_all[OUT_BLK] = jnp.zeros((BR, CO), jnp.bfloat16)
    low, high = grad_ref[:BND], grad_ref[OUT_BLK - BND :]
    near_grad_ref[...] = jnp.where(core == 0, high, low)
    far_grad_ref[...] = jnp.where(core == 0, low, high)

    for offset in range(OFFS):

        def terms(chunk, offset=offset):
            rules = owner_rules(plan_ref, offset, chunk * SLOTS)
            left = jnp.concatenate([xt_all[i] for i, _ in rules], 1)
            right = jnp.concatenate([g_all[slot] for _, slot in rules], 0)
            return jnp.dot(left, right, preferred_element_type=jnp.float32)

        def add_terms(chunk):
            term_ref[...] += terms(chunk)

        term_ref[...] = terms(0)
        pl.loop(1, plan_ref[offset, CHUNKS])(add_terms)
        per = CI // (2 * ROWS)
        for pair in range(per):
            place = positions[offset * per + pair] ^ flip
            a = term_ref[2 * pair * ROWS : (2 * pair + 1) * ROWS]
            b = term_ref[(2 * pair + 1) * ROWS : (2 * pair + 2) * ROWS]
            keep_ref[place] = jnp.where(core == 0, a, b)
            send_ref[place] = jnp.where(core == 0, b, a).astype(jnp.bfloat16)


def feature_grad_kernel(plan_ref, grad_ref, near_ref, far_ref, w_ref, out_ref, g_all, acc):
    core = plan_ref[0, CORE]
    near, far = near_ref[...], far_ref[...]
    g_all[:BND] = jnp.where(core == 0, far, near)
    g_all[BND : BND + OUT_BLK] = grad_ref[...]
    g_all[BND + OUT_BLK : EXT] = jnp.where(core == 0, near, far)
    g_all[EXT] = jnp.zeros((BR, CO), jnp.bfloat16)
    acc[...] = jnp.zeros_like(acc)
    for offset in range(OFFS):
        codes = [plan_ref[offset, BACK + j] for j in range(SLOTS)]
        rules = [(code >> 4, code & 15) for code in codes]
        grads = jnp.concatenate([g_all[slot] for _, slot in rules], 0)
        kernel = w_ref[offset * CI : (offset + 1) * CI]
        back = lax.dot_general(
            grads, kernel, (((1,), (1,)), ((), ())), preferred_element_type=jnp.float32
        )
        for j, (i, _) in enumerate(rules):
            acc[i] += back[j * BR : (j + 1) * BR]
    out_ref[...] = acc[...].astype(jnp.bfloat16)


def call(kernel, name, in_specs, out_shape, scratch, flops, moved):
    return pl.pallas_call(
        kernel,
        name=name,
        out_shape=out_shape,
        in_specs=in_specs,
        out_specs=jax.tree.map(lambda _: VMEM, out_shape),
        scratch_shapes=scratch,
        compiler_params=pltpu.CompilerParams(vmem_limit_bytes=24 * 1024 * 1024),
        cost_estimate=pl.CostEstimate(flops=flops, bytes_accessed=moved, transcendentals=0),
    )


def shape(dims, dtype=jnp.bfloat16):
    return jax.ShapeDtypeStruct(dims, dtype)


def plan_of(tables, slab, flip):
    slots = jnp.arange(SLOTS, dtype=jnp.int32)
    in_index = tables[:, :, 0] + IN_BLK * jnp.arange(SLABS, dtype=jnp.int32)[:, None, None]
    out_index, owner = tables[:, :, 1], tables[:, :, 2]
    valid = slots < tables[:, :, 3]
    live = jnp.swapaxes(valid & (owner == slab), 0, 1).reshape(OFFS, RULES)
    code = jnp.swapaxes(in_index * 8 + out_index, 0, 1).reshape(OFFS, RULES)
    order = jnp.arange(RULES, dtype=jnp.int32)
    earlier = order[:, None] > order[None, :]
    rank = jnp.sum(jnp.where(live[:, None, :] & earlier, 1, 0), 2)
    count = jnp.sum(jnp.where(live, 1, 0), 1, keepdims=True)
    chosen = live[:, None, :] & (rank[:, None, :] == order[:, None])
    packed = jnp.sum(jnp.where(chosen, code[:, None, :], 0), 2)
    packed = jnp.where(order < count, packed, OUT_BLK)
    ext = jnp.where(valid[0], BND + out_index[0] + (owner[0] - slab) * OUT_BLK, EXT)
    back = tables[0, :, 0] * 16 + ext
    scalars = jnp.broadcast_to(jnp.stack([slab & 1, flip]), (OFFS, 2))
    return jnp.concatenate([packed, back, (count + SLOTS - 1) // SLOTS, scalars], 1)


def local(features, weight, rulebook, rule_counts, cotangent):
    dp, space = lax.axis_size("dp"), lax.axis_size("space")
    devices = dp * space
    groups = phases_of(dp, space)
    rows = weight.shape[0]
    slab = lax.axis_index("space").astype(jnp.int32)
    me = lax.axis_index("dp").astype(jnp.int32) * space + slab
    direct = rows == ROWS

    own_table = jnp.concatenate(
        [rulebook[0], jnp.broadcast_to(rule_counts[0][:, None, None], (OFFS, 1, SLOTS))], 1
    )
    slab_a, slab_b = exchange(features[0], 1, devices), swap_far(features[0])
    beside = (exchange(own_table, 1, devices), swap_far(own_table))

    parts = weight[None]
    for group in groups[:-1]:
        received = [exchange(parts, mask, devices) for mask in masks_of(group)]
        parts = jnp.concatenate([parts] + received, 0)
    far = exchange(parts, groups[-1][0], devices)

    flip = position_of(me & -2, groups) if direct else jnp.zeros((), jnp.int32)
    plan = plan_of(jnp.stack((own_table,) + beside), slab, flip)
    if direct:
        near = parts
        positions = [position_of(2 * pair, groups) for pair in range(PAIRS)]
    else:
        ids = np.arange(devices, dtype=np.int32)
        order = position_of(ids ^ me, groups)
        whole = jnp.concatenate([parts, far], 0)[order].reshape(PAIRS, 2, ROWS, CO)
        swapped = jnp.where((slab & 1) == 0, whole, whole[:, ::-1])
        near, far = swapped[:, 0], swapped[:, 1]
        positions = list(range(PAIRS))

    rule_flops = 2 * OFFS * SLOTS * BR * CI * CO
    activated, grad_pre, near_grad, far_grad, keep, send, kernels = call(
        lambda *refs: main_kernel(positions, *refs),
        "forward_and_weight_grad",
        [SMEM] + [VMEM] * 6,
        (
            shape((OUT_BLK, BR, CO)),
            shape((OUT_BLK, BR, CO)),
            shape((BND, BR, CO)),
            shape((BND, BR, CO)),
            shape((PAIRS, ROWS, CO), jnp.float32),
            shape((PAIRS, ROWS, CO)),
            shape((OFFS * CI, CO)),
        ),
        [
            pltpu.VMEM((SLABS * IN_BLK, BR, CI), jnp.bfloat16),
            pltpu.VMEM((SLABS * IN_BLK, CI, BR), jnp.bfloat16),
            pltpu.VMEM((OUT_BLK + 1, BR, CO), jnp.float32),
            pltpu.VMEM((OUT_BLK + 1, BR, CO), jnp.bfloat16),
            pltpu.VMEM((CI, CO), jnp.float32),
        ],
        2 * rule_flops,
        1 << 23,
    )(plan, features[0], slab_a, slab_b, near, far, cotangent[0].reshape(OUT_BLK, BR, CO))

    if not direct:
        terms = jnp.stack([keep, send.astype(jnp.float32)], 1)
        terms = jnp.where((slab & 1) == 0, terms, terms[:, ::-1]).reshape(devices, rows, CO)
        source = np.argsort(position_of(ids, groups)).astype(np.int32) ^ me
        ordered = terms[source]
        keep, send = ordered[: devices // 2], ordered[devices // 2 :].astype(jnp.bfloat16)
    total = keep + exchange(send, groups[-1][0], devices).astype(jnp.float32)

    near_rim = exchange(near_grad, 1, devices)
    far_rim = swap_far(far_grad)
    grad_in = call(
        feature_grad_kernel,
        "feature_grad",
        [SMEM] + [VMEM] * 4,
        shape((IN_BLK, BR, CI)),
        [
            pltpu.VMEM((EXT + 1, BR, CO), jnp.bfloat16),
            pltpu.VMEM((IN_BLK, BR, CI), jnp.float32),
        ],
        rule_flops,
        1 << 22,
    )(plan, grad_pre, near_rim, far_rim, kernels)

    for group in reversed(groups[:-1]):
        masks = masks_of(group)
        if group is groups[0]:
            total, grad_in = lax.optimization_barrier((total, grad_in))
        count = total.shape[0] // (len(masks) + 1)
        received = [
            exchange(total[(r + 1) * count : (r + 2) * count].astype(jnp.bfloat16), mask, devices)
            for r, mask in enumerate(masks)
        ]
        total = total[:count]
        for piece in received:
            total = total + piece.astype(jnp.float32)
    grad_weight = total[0] * grad_scale
    return (
        activated.reshape(1, OUT_BLK * BR, CO),
        grad_in.reshape(1, IN_ROWS, CI),
        grad_weight,
    )


def solution(mesh):
    in_specs = (
        P("dp", "space", None),
        P(("dp", "space"), None),
        P("dp", "space", None, None),
        P("dp", "space"),
        P("dp", "space", None),
    )
    out_specs = (P("dp", "space", None), P("dp", "space", None), P(("dp", "space"), None))
    return jax.shard_map(local, mesh=mesh, in_specs=in_specs, out_specs=out_specs, check_vma=False)
```

```python
import jax
import jax.numpy as jnp
import numpy as np
from jax import lax
from jax.experimental import pallas as pl
from jax.experimental.pallas import tpu as pltpu
from jax.sharding import PartitionSpec as P

CI = 256
CO = 256
OFFS = 8
BR = 128
BND = 2
SLOTS = 8
IN_BLK = 8
OUT_BLK = 4
EXT = OUT_BLK + 2 * BND
IN_ROWS = IN_BLK * BR
SLABS = 3
RULES = SLABS * SLOTS
STEP = 4
AXES = ("dp", "space")
BACK = RULES
COUNT = RULES + SLOTS
CORE = COUNT + 1
FLIP = COUNT + 2
PAIRS = 16
ROWS = OFFS * CI // (2 * PAIRS)

grad_scale = 1.0 / 2048.0

VMEM = pl.BlockSpec(memory_space=pltpu.VMEM)
SMEM = pl.BlockSpec(memory_space=pltpu.SMEM)


def phases_of(dp, space):
    space_bits = [1 << b for b in reversed(range(space.bit_length() - 1))]
    dp_bits = [space << b for b in reversed(range(dp.bit_length() - 1))]
    order = space_bits[:-1:2] + space_bits[1:-1:2] + dp_bits
    return [order[i : i + 2] for i in range(0, len(order), 2)] + [space_bits[-1:]]


def masks_of(group):
    return [
        sum(bit for t, bit in enumerate(group) if r >> t & 1) for r in range(1, 1 << len(group))
    ]


def position_of(index, groups):
    place = 0
    for t, bit in enumerate([bit for group in groups for bit in group]):
        place = place | (((index >> (bit.bit_length() - 1)) & 1) << t)
    return place


def exchange(value, mask, devices):
    return lax.ppermute(value, AXES, [(i, i ^ mask) for i in range(devices)])


def swap_far(value):
    count = lax.axis_size("space")
    pairs = [(s, s + 1) for s in range(1, count - 1, 2)]
    return lax.ppermute(value, "space", pairs + [(t, s) for s, t in pairs])


def owner_rules(plan_ref, offset, first, count):
    codes = [plan_ref[offset, first + j] for j in range(count)]
    return [(code >> 3, code & 7) for code in codes]


def lay_out(refs, first, x_all, xt_all):
    for slab, ref in enumerate(refs):
        for i in range(IN_BLK):
            block = ref[i * BR : (i + 1) * BR]
            x_all[first + slab * IN_BLK + i] = block
            xt_all[first + slab * IN_BLK + i] = block.T


def layout_kernel(x_ref, a_ref, x_all, xt_all):
    lay_out((x_ref, a_ref), 0, x_all, xt_all)


def main_kernel(
    positions, plan_ref, b_ref, near_ref, far_ref, cot_ref, _, __,
    act_ref, grad_ref, near_grad_ref, far_grad_ref, keep_ref, send_ref, w_ref, x_all, xt_all,
    acc, g_all, term_ref,
):
    core, flip = plan_ref[0, CORE], plan_ref[0, FLIP]
    lay_out((b_ref,), 2 * IN_BLK, x_all, xt_all)
    for pair, position in enumerate(positions):
        place = position ^ flip
        a, b = near_ref[place], far_ref[place]
        w_ref[2 * pair * ROWS : (2 * pair + 1) * ROWS] = jnp.where(core == 0, a, b)
        w_ref[(2 * pair + 1) * ROWS : (2 * pair + 2) * ROWS] = jnp.where(core == 0, b, a)

    acc[...] = jnp.zeros_like(acc)
    for offset in range(OFFS):
        kernel = w_ref[offset * CI : (offset + 1) * CI]

        def add_products(first, count=STEP, offset=offset, kernel=kernel):
            rules = owner_rules(plan_ref, offset, first, count)
            picked = jnp.concatenate([x_all[i] for i, _ in rules], 0)
            product = jnp.dot(picked, kernel, preferred_element_type=jnp.float32)
            for j, (_, slot) in enumerate(rules):
                acc[slot] += product[j * BR : (j + 1) * BR]

        add_products(0, SLOTS)
        pl.loop(SLOTS, plan_ref[offset, COUNT], step=STEP)(add_products)

    for o in range(OUT_BLK):
        pre = acc[o]
        sigma = jax.nn.sigmoid(pre)
        act_ref[o] = (pre * sigma).astype(jnp.bfloat16)
        upstream = cot_ref[o].astype(jnp.float32)
        grad = (upstream * sigma * (1.0 + pre * (1.0 - sigma))).astype(jnp.bfloat16)
        grad_ref[o] = grad
        g_all[o] = grad
    g_all[OUT_BLK] = jnp.zeros((BR, CO), jnp.bfloat16)
    low, high = grad_ref[:BND], grad_ref[OUT_BLK - BND :]
    near_grad_ref[...] = jnp.where(core == 0, high, low)
    far_grad_ref[...] = jnp.where(core == 0, low, high)

    for offset in range(OFFS):

        def terms(first, count=STEP, offset=offset):
            rules = owner_rules(plan_ref, offset, first, count)
            left = jnp.concatenate([xt_all[i] for i, _ in rules], 1)
            right = jnp.concatenate([g_all[slot] for _, slot in rules], 0)
            return jnp.dot(left, right, preferred_element_type=jnp.float32)

        def add_terms(first, terms=terms):
            term_ref[...] += terms(first)

        term_ref[...] = terms(0, SLOTS)
        pl.loop(SLOTS, plan_ref[offset, COUNT], step=STEP)(add_terms)
        per = CI // (2 * ROWS)
        for pair in range(per):
            place = positions[offset * per + pair] ^ flip
            a = term_ref[2 * pair * ROWS : (2 * pair + 1) * ROWS]
            b = term_ref[(2 * pair + 1) * ROWS : (2 * pair + 2) * ROWS]
            keep_ref[place] = jnp.where(core == 0, a, b)
            send_ref[place] = jnp.where(core == 0, b, a).astype(jnp.bfloat16)


def feature_grad_kernel(plan_ref, grad_ref, near_ref, far_ref, w_ref, out_ref, g_all, acc):
    core = plan_ref[0, CORE]
    near, far = near_ref[...], far_ref[...]
    g_all[:BND] = jnp.where(core == 0, far, near)
    g_all[BND : BND + OUT_BLK] = grad_ref[...]
    g_all[BND + OUT_BLK : EXT] = jnp.where(core == 0, near, far)
    g_all[EXT] = jnp.zeros((BR, CO), jnp.bfloat16)
    acc[...] = jnp.zeros_like(acc)
    for offset in range(OFFS):
        codes = [plan_ref[offset, BACK + j] for j in range(SLOTS)]
        rules = [(code >> 4, code & 15) for code in codes]
        grads = jnp.concatenate([g_all[slot] for _, slot in rules], 0)
        kernel = w_ref[offset * CI : (offset + 1) * CI]
        back = lax.dot_general(
            grads, kernel, (((1,), (1,)), ((), ())), preferred_element_type=jnp.float32
        )
        for j, (i, _) in enumerate(rules):
            acc[i] += back[j * BR : (j + 1) * BR]
    out_ref[...] = acc[...].astype(jnp.bfloat16)


def call(kernel, name, in_specs, out_shape, scratch, flops, moved, aliases={}):
    return pl.pallas_call(
        kernel,
        name=name,
        out_shape=out_shape,
        in_specs=in_specs,
        out_specs=jax.tree.map(lambda _: VMEM, out_shape),
        scratch_shapes=scratch,
        input_output_aliases=aliases,
        compiler_params=pltpu.CompilerParams(vmem_limit_bytes=24 * 1024 * 1024),
        cost_estimate=pl.CostEstimate(flops=flops, bytes_accessed=moved, transcendentals=0),
    )


def shape(dims, dtype=jnp.bfloat16):
    return jax.ShapeDtypeStruct(dims, dtype)


def plan_of(tables, slab, flip):
    slots = jnp.arange(SLOTS, dtype=jnp.int32)
    in_index = tables[:, :, 0] + IN_BLK * jnp.arange(SLABS, dtype=jnp.int32)[:, None, None]
    out_index, owner = tables[:, :, 1], tables[:, :, 2]
    valid = slots < tables[:, :, 3]
    live = jnp.swapaxes(valid & (owner == slab), 0, 1).reshape(OFFS, RULES)
    code = jnp.swapaxes(in_index * 8 + out_index, 0, 1).reshape(OFFS, RULES)
    order = jnp.arange(RULES, dtype=jnp.int32)
    earlier = order[:, None] > order[None, :]
    rank = jnp.sum(jnp.where(live[:, None, :] & earlier, 1, 0), 2)
    count = jnp.sum(jnp.where(live, 1, 0), 1, keepdims=True)
    chosen = live[:, None, :] & (rank[:, None, :] == order[:, None])
    packed = jnp.sum(jnp.where(chosen, code[:, None, :], 0), 2)
    packed = jnp.where(order < count, packed, OUT_BLK)
    ext = jnp.where(valid[0], BND + out_index[0] + (owner[0] - slab) * OUT_BLK, EXT)
    back = tables[0, :, 0] * 16 + ext
    scalars = jnp.broadcast_to(jnp.stack([slab & 1, flip]), (OFFS, 2))
    return jnp.concatenate([packed, back, count, scalars], 1)


def local(features, weight, rulebook, rule_counts, cotangent):
    dp, space = lax.axis_size("dp"), lax.axis_size("space")
    devices = dp * space
    groups = phases_of(dp, space)
    rows = weight.shape[0]
    slab = lax.axis_index("space").astype(jnp.int32)
    me = lax.axis_index("dp").astype(jnp.int32) * space + slab
    direct = rows == ROWS

    own_table = jnp.concatenate(
        [rulebook[0], jnp.broadcast_to(rule_counts[0][:, None, None], (OFFS, 1, SLOTS))], 1
    )
    slab_a, slab_b = exchange(features[0], 1, devices), swap_far(features[0])
    parts, slab_a = lax.optimization_barrier((weight[None], slab_a))
    for group in groups[:-1]:
        received = [exchange(parts, mask, devices) for mask in masks_of(group)]
        parts = jnp.concatenate([parts] + received, 0)
        if group is groups[0]:
            parts, own_table = lax.optimization_barrier((parts, own_table))
            beside = (exchange(own_table, 1, devices), swap_far(own_table))
    far = exchange(parts, groups[-1][0], devices)

    flip = position_of(me & -2, groups) if direct else jnp.zeros((), jnp.int32)
    plan = plan_of(jnp.stack((own_table,) + beside), slab, flip)
    if direct:
        near = parts
        positions = [position_of(2 * pair, groups) for pair in range(PAIRS)]
    else:
        ids = np.arange(devices, dtype=np.int32)
        order = position_of(ids ^ me, groups)
        whole = jnp.concatenate([parts, far], 0)[order].reshape(PAIRS, 2, ROWS, CO)
        swapped = jnp.where((slab & 1) == 0, whole, whole[:, ::-1])
        near, far = swapped[:, 0], swapped[:, 1]
        positions = list(range(PAIRS))

    rule_flops = 2 * OFFS * SLOTS * BR * CI * CO
    layouts = (
        shape((SLABS * IN_BLK, BR, CI)),
        shape((SLABS * IN_BLK, CI, BR)),
    )
    x_all, xt_all = call(
        layout_kernel, "layout", [VMEM] * 2, layouts, [], 0, 4 * IN_ROWS * CI * 4
    )(features[0], slab_a)
    activated, grad_pre, near_grad, far_grad, keep, send, kernels, _, _ = call(
        lambda *refs: main_kernel(positions, *refs),
        "forward_and_weight_grad",
        [SMEM] + [VMEM] * 6,
        (
            shape((OUT_BLK, BR, CO)),
            shape((OUT_BLK, BR, CO)),
            shape((BND, BR, CO)),
            shape((BND, BR, CO)),
            shape((PAIRS, ROWS, CO), jnp.float32),
            shape((PAIRS, ROWS, CO)),
            shape((OFFS * CI, CO)),
        )
        + layouts,
        [
            pltpu.VMEM((OUT_BLK + 1, BR, CO), jnp.float32),
            pltpu.VMEM((OUT_BLK + 1, BR, CO), jnp.bfloat16),
            pltpu.VMEM((CI, CO), jnp.float32),
        ],
        2 * rule_flops,
        1 << 23,
        {5: 7, 6: 8},
    )(plan, slab_b, near, far, cotangent[0].reshape(OUT_BLK, BR, CO), x_all, xt_all)

    if not direct:
        terms = jnp.stack([keep, send.astype(jnp.float32)], 1)
        terms = jnp.where((slab & 1) == 0, terms, terms[:, ::-1]).reshape(devices, rows, CO)
        source = np.argsort(position_of(ids, groups)).astype(np.int32) ^ me
        ordered = terms[source]
        keep, send = ordered[: devices // 2], ordered[devices // 2 :].astype(jnp.bfloat16)
    total = keep + exchange(send, groups[-1][0], devices).astype(jnp.float32)

    near_rim = exchange(near_grad, 1, devices)
    far_rim = swap_far(far_grad)
    grad_in = call(
        feature_grad_kernel,
        "feature_grad",
        [SMEM] + [VMEM] * 4,
        shape((IN_BLK, BR, CI)),
        [
            pltpu.VMEM((EXT + 1, BR, CO), jnp.bfloat16),
            pltpu.VMEM((IN_BLK, BR, CI), jnp.float32),
        ],
        rule_flops,
        1 << 22,
    )(plan, grad_pre, near_rim, far_rim, kernels)

    for group in reversed(groups[:-1]):
        masks = masks_of(group)
        count = total.shape[0] // (len(masks) + 1)
        received = [
            exchange(total[(r + 1) * count : (r + 2) * count].astype(jnp.bfloat16), mask, devices)
            for r, mask in enumerate(masks)
        ]
        total = total[:count]
        for piece in received:
            total = total + piece.astype(jnp.float32)
    grad_weight = total[0] * grad_scale
    return (
        activated.reshape(1, OUT_BLK * BR, CO),
        grad_in.reshape(1, IN_ROWS, CI),
        grad_weight,
    )


def solution(mesh):
    in_specs = (
        P("dp", "space", None),
        P(("dp", "space"), None),
        P("dp", "space", None, None),
        P("dp", "space"),
        P("dp", "space", None),
    )
    out_specs = (P("dp", "space", None), P("dp", "space", None), P(("dp", "space"), None))
    return jax.shard_map(local, mesh=mesh, in_specs=in_specs, out_specs=out_specs, check_vma=False)
```

```python
import functools

import jax
import jax.numpy as jnp
import numpy as np
from jax import lax
from jax.experimental import pallas as pl
from jax.experimental.pallas import tpu as pltpu
from jax.sharding import Mesh
from jax.sharding import PartitionSpec as P

CI = 256
CO = 256
OFFS = 8
BR = 128
BND = 2
SLOTS = 8
IN_BLK = 8
OUT_BLK = 4
EXT = OUT_BLK + 2 * BND
IN_ROWS = IN_BLK * BR
SLABS = 3
RULES = SLABS * SLOTS
STEP = 4
TAIL = 32
BACK = RULES
COUNT = RULES + SLOTS
CORE = COUNT + 1
PAIRS = 16
ROWS = OFFS * CI // (2 * PAIRS)

grad_scale = 1.0 / 2048.0

VMEM = pl.BlockSpec(memory_space=pltpu.VMEM)
SMEM = pl.BlockSpec(memory_space=pltpu.SMEM)


def phases_of(dp_bits, space_bits):
    order = space_bits[:-1:2] + dp_bits + space_bits[1:-1:2]
    return [order[i : i + 2] for i in range(0, len(order), 2)]


def positions_of(names, groups):
    places = []
    for pair in range(1 << (len(names) - 1)):
        bits = {name: pair >> (len(names) - 2 - i) & 1 for i, name in enumerate(names[:-1])}
        place = 0
        for group in reversed(groups):
            for name in group:
                place = 2 * place + bits[name]
        places.append(place)
    return places


def swap_near(value, core_axis):
    return lax.ppermute(value, core_axis, [(0, 1), (1, 0)])


def swap_far(value, space_axes):
    count = lax.axis_size(space_axes)
    pairs = [(s, s + 1) for s in range(1, count - 1, 2)]
    return lax.ppermute(value, space_axes, pairs + [(t, s) for s, t in pairs])


def pack_kernel(x_ref, rules_ref, counts_ref, halo_ref, tail):
    halo_ref[:IN_ROWS] = x_ref[...]
    tail[...] = jnp.zeros_like(tail)
    for offset in range(OFFS):
        tail[4 * offset : 4 * offset + 3, :SLOTS] = rules_ref[offset].astype(jnp.float32)
    tail[3:4, :OFFS] = counts_ref[...].astype(jnp.float32)
    halo_ref[IN_ROWS:] = tail[...].astype(jnp.bfloat16)


def owner_rules(plan_ref, offset, first, count):
    codes = [plan_ref[offset, first + j] for j in range(count)]
    return [(code >> 3, code & 7) for code in codes]


def main_kernel(
    positions, plan_ref, x_ref, a_ref, b_ref, near_ref, far_ref, cot_ref,
    act_ref, grad_ref, near_grad_ref, far_grad_ref, keep_ref, send_ref, w_ref,
    x_all, xt_all, acc, g_all, term_ref,
):
    core = plan_ref[0, CORE]
    for slab, ref in enumerate((x_ref, a_ref, b_ref)):
        for i in range(IN_BLK):
            block = ref[i * BR : (i + 1) * BR]
            x_all[slab * IN_BLK + i] = block
            xt_all[slab * IN_BLK + i] = block.T
    for pair, place in enumerate(positions):
        a, b = near_ref[place], far_ref[place]
        w_ref[2 * pair * ROWS : (2 * pair + 1) * ROWS] = jnp.where(core == 0, a, b)
        w_ref[(2 * pair + 1) * ROWS : (2 * pair + 2) * ROWS] = jnp.where(core == 0, b, a)

    acc[...] = jnp.zeros_like(acc)
    for offset in range(OFFS):
        kernel = w_ref[offset * CI : (offset + 1) * CI]

        def add_products(first, count=STEP, offset=offset, kernel=kernel):
            rules = owner_rules(plan_ref, offset, first, count)
            picked = jnp.concatenate([x_all[i] for i, _ in rules], 0)
            product = jnp.dot(picked, kernel, preferred_element_type=jnp.float32)
            for j, (_, slot) in enumerate(rules):
                acc[slot] += product[j * BR : (j + 1) * BR]

        add_products(0, SLOTS)
        pl.loop(SLOTS, plan_ref[offset, COUNT], step=STEP)(add_products)

    for o in range(OUT_BLK):
        pre = acc[o]
        sigma = jax.nn.sigmoid(pre)
        act_ref[o] = (pre * sigma).astype(jnp.bfloat16)
        upstream = cot_ref[o].astype(jnp.float32)
        grad = (upstream * sigma * (1.0 + pre * (1.0 - sigma))).astype(jnp.bfloat16)
        grad_ref[o] = grad
        g_all[o] = grad
    g_all[OUT_BLK] = jnp.zeros((BR, CO), jnp.bfloat16)
    low, high = grad_ref[:BND], grad_ref[OUT_BLK - BND :]
    near_grad_ref[...] = jnp.where(core == 0, high, low)
    far_grad_ref[...] = jnp.where(core == 0, low, high)

    for offset in range(OFFS):

        def terms(first, count=STEP, offset=offset):
            rules = owner_rules(plan_ref, offset, first, count)
            left = jnp.concatenate([xt_all[i] for i, _ in rules], 1)
            right = jnp.concatenate([g_all[slot] for _, slot in rules], 0)
            return jnp.dot(left, right, preferred_element_type=jnp.float32)

        def add_terms(first, terms=terms):
            term_ref[...] += terms(first)

        term_ref[...] = terms(0, SLOTS)
        pl.loop(SLOTS, plan_ref[offset, COUNT], step=STEP)(add_terms)
        per = CI // (2 * ROWS)
        for pair in range(per):
            place = positions[offset * per + pair]
            a = term_ref[2 * pair * ROWS : (2 * pair + 1) * ROWS]
            b = term_ref[(2 * pair + 1) * ROWS : (2 * pair + 2) * ROWS]
            keep_ref[place] = jnp.where(core == 0, a, b)
            send_ref[place] = jnp.where(core == 0, b, a).astype(jnp.bfloat16)


def feature_grad_kernel(plan_ref, grad_ref, near_ref, far_ref, w_ref, out_ref, g_all, acc):
    core = plan_ref[0, CORE]
    near, far = near_ref[...], far_ref[...]
    g_all[:BND] = jnp.where(core == 0, far, near)
    g_all[BND : BND + OUT_BLK] = grad_ref[...]
    g_all[BND + OUT_BLK : EXT] = jnp.where(core == 0, near, far)
    g_all[EXT] = jnp.zeros((BR, CO), jnp.bfloat16)
    acc[...] = jnp.zeros_like(acc)
    for offset in range(OFFS):
        codes = [plan_ref[offset, BACK + j] for j in range(SLOTS)]
        rules = [(code >> 4, code & 15) for code in codes]
        grads = jnp.concatenate([g_all[slot] for _, slot in rules], 0)
        kernel = w_ref[offset * CI : (offset + 1) * CI]
        back = lax.dot_general(
            grads, kernel, (((1,), (1,)), ((), ())), preferred_element_type=jnp.float32
        )
        for j, (i, _) in enumerate(rules):
            acc[i] += back[j * BR : (j + 1) * BR]
    out_ref[...] = acc[...].astype(jnp.bfloat16)


def call(kernel, name, in_specs, out_shape, scratch, flops, moved):
    return pl.pallas_call(
        kernel,
        name=name,
        out_shape=out_shape,
        in_specs=in_specs,
        out_specs=jax.tree.map(lambda _: VMEM, out_shape),
        scratch_shapes=scratch,
        compiler_params=pltpu.CompilerParams(vmem_limit_bytes=24 * 1024 * 1024),
        cost_estimate=pl.CostEstimate(flops=flops, bytes_accessed=moved, transcendentals=0),
    )


def shape(dims, dtype=jnp.bfloat16):
    return jax.ShapeDtypeStruct(dims, dtype)


def plan_of(tables, counts, slab):
    slots = jnp.arange(SLOTS, dtype=jnp.int32)
    in_index = tables[:, :, 0] + IN_BLK * jnp.arange(SLABS, dtype=jnp.int32)[:, None, None]
    out_index, owner = tables[:, :, 1], tables[:, :, 2]
    valid = slots < counts[:, :, None]
    live = jnp.swapaxes(valid & (owner == slab), 0, 1).reshape(OFFS, RULES)
    code = jnp.swapaxes(in_index * 8 + out_index, 0, 1).reshape(OFFS, RULES)
    order = jnp.arange(RULES, dtype=jnp.int32)
    earlier = order[:, None] > order[None, :]
    rank = jnp.sum(jnp.where(live[:, None, :] & earlier, 1, 0), 2)
    count = jnp.sum(jnp.where(live, 1, 0), 1, keepdims=True)
    chosen = live[:, None, :] & (rank[:, None, :] == order[:, None])
    packed = jnp.sum(jnp.where(chosen, code[:, None, :], 0), 2)
    packed = jnp.where(order < count, packed, OUT_BLK)
    ext = jnp.where(valid[0], BND + out_index[0] + (owner[0] - slab) * OUT_BLK, EXT)
    back = tables[0, :, 0] * 16 + ext
    core = jnp.broadcast_to(slab & 1, (OFFS, 1))
    return jnp.concatenate([packed, back, count, core], 1)


def local(dp_bits, space_bits, features, weight, rulebook, rule_counts, cotangent):
    groups = phases_of(dp_bits, space_bits)
    core_axis = space_bits[-1]
    pairs = lax.axis_size(dp_bits + space_bits) // 2
    places = positions_of(dp_bits + space_bits, groups)
    rows = weight.shape[0]
    slab = lax.axis_index(space_bits).astype(jnp.int32)
    core = slab & 1
    direct = rows == ROWS

    halo = call(
        pack_kernel,
        "pack",
        [VMEM] * 3,
        shape((IN_ROWS + TAIL, CI)),
        [pltpu.VMEM((TAIL, CI), jnp.float32)],
        0,
        1 << 20,
    )(features[0], rulebook[0], rule_counts)
    beside = (swap_near(halo, core_axis), swap_far(halo, space_bits))
    tails = [
        other[IN_ROWS:, :SLOTS].astype(jnp.int32).reshape(OFFS, 4, SLOTS) for other in beside
    ]

    near = weight[None]
    for group in groups:
        copies = jnp.broadcast_to(near[None], (1 << len(group),) + near.shape)
        near = lax.all_to_all(copies, group, 0, 0, tiled=True).reshape(-1, rows, CO)
    far = swap_near(near, core_axis)

    plan = plan_of(
        jnp.stack([rulebook[0]] + [tail[:, :3] for tail in tails]),
        jnp.stack([rule_counts[0]] + [tail[0, 3] for tail in tails]),
        slab,
    )
    positions = places
    if not direct:
        even, odd = jnp.where(core == 0, near, far), jnp.where(core == 0, far, near)
        whole = jnp.stack([even, odd], 1)[np.array(places)].reshape(PAIRS, 2, ROWS, CO)
        near = jnp.where(core == 0, whole[:, 0], whole[:, 1])
        far = jnp.where(core == 0, whole[:, 1], whole[:, 0])
        positions = list(range(PAIRS))

    rule_flops = 2 * OFFS * SLOTS * BR * CI * CO
    activated, grad_pre, near_grad, far_grad, keep, send, kernels = call(
        lambda *refs: main_kernel(positions, *refs),
        "forward_and_weight_grad",
        [SMEM] + [VMEM] * 6,
        (
            shape((OUT_BLK, BR, CO)),
            shape((OUT_BLK, BR, CO)),
            shape((BND, BR, CO)),
            shape((BND, BR, CO)),
            shape((PAIRS, ROWS, CO), jnp.float32),
            shape((PAIRS, ROWS, CO)),
            shape((OFFS * CI, CO)),
        ),
        [
            pltpu.VMEM((SLABS * IN_BLK, BR, CI), jnp.bfloat16),
            pltpu.VMEM((SLABS * IN_BLK, CI, BR), jnp.bfloat16),
            pltpu.VMEM((OUT_BLK + 1, BR, CO), jnp.float32),
            pltpu.VMEM((OUT_BLK + 1, BR, CO), jnp.bfloat16),
            pltpu.VMEM((CI, CO), jnp.float32),
        ],
        2 * rule_flops,
        1 << 23,
    )(plan, features[0], *beside, near, far, cotangent[0].reshape(OUT_BLK, BR, CO))

    if not direct:
        even, odd = jnp.where(core == 0, keep, send), jnp.where(core == 0, send, keep)
        whole = jnp.stack([even, odd], 1).reshape(pairs, 2, rows, CO)[np.argsort(places)]
        keep = jnp.where(core == 0, whole[:, 0], whole[:, 1])
        send = jnp.where(core == 0, whole[:, 1], whole[:, 0]).astype(jnp.bfloat16)
    total = keep + swap_near(send, core_axis).astype(jnp.float32)

    near_rim = swap_near(near_grad, core_axis)
    far_rim = swap_far(far_grad, space_bits)
    grad_in = call(
        feature_grad_kernel,
        "feature_grad",
        [SMEM] + [VMEM] * 4,
        shape((IN_BLK, BR, CI)),
        [
            pltpu.VMEM((EXT + 1, BR, CO), jnp.bfloat16),
            pltpu.VMEM((IN_BLK, BR, CI), jnp.float32),
        ],
        rule_flops,
        1 << 22,
    )(plan, grad_pre, near_rim, far_rim, kernels)

    for group in reversed(groups):
        split = total.astype(jnp.bfloat16).reshape((1 << len(group), -1, rows, CO))
        terms = lax.all_to_all(split, group, 0, 0, tiled=True)
        total = jnp.sum(terms.astype(jnp.float32), 0)
    grad_weight = total[0] * grad_scale
    return (
        activated.reshape(1, OUT_BLK * BR, CO),
        grad_in.reshape(1, IN_ROWS, CI),
        grad_weight,
    )


def solution(mesh):
    dp_bits = tuple("d%d" % b for b in reversed(range(mesh.shape["dp"].bit_length() - 1)))
    space_bits = tuple("s%d" % b for b in reversed(range(mesh.shape["space"].bit_length() - 1)))
    names = dp_bits + space_bits
    binary = Mesh(mesh.devices.reshape((2,) * len(names)), names)
    in_specs = (
        P(dp_bits, space_bits, None),
        P(names, None),
        P(dp_bits, space_bits, None, None),
        P(dp_bits, space_bits),
        P(dp_bits, space_bits, None),
    )
    out_specs = (P(dp_bits, space_bits, None), P(dp_bits, space_bits, None), P(names, None))
    return jax.shard_map(
        functools.partial(local, dp_bits, space_bits),
        mesh=binary,
        in_specs=in_specs,
        out_specs=out_specs,
        check_vma=False,
    )
```

```python
import jax
import jax.numpy as jnp
import numpy as np
from jax import lax
from jax.experimental import pallas as pl
from jax.experimental.pallas import tpu as pltpu
from jax.sharding import PartitionSpec as P

CI = 256
CO = 256
OFFS = 8
BR = 128
BND = 2
SLOTS = 8
IN_BLK = 8
OUT_BLK = 4
EXT = OUT_BLK + 2 * BND
IN_ROWS = IN_BLK * BR
SLABS = 3
RULES = SLABS * SLOTS
TAIL = 32
AXES = ("dp", "space")
BACK = RULES
CHUNKS = RULES + SLOTS
CORE = CHUNKS + 1
FLIP = CHUNKS + 2
PAIRS = 16
ROWS = OFFS * CI // (2 * PAIRS)

grad_scale = 1.0 / 2048.0

VMEM = pl.BlockSpec(memory_space=pltpu.VMEM)
SMEM = pl.BlockSpec(memory_space=pltpu.SMEM)


def phases_of(dp, space):
    space_bits = [1 << b for b in reversed(range(space.bit_length() - 1))]
    dp_bits = [space << b for b in reversed(range(dp.bit_length() - 1))]
    order = space_bits[:-1:2] + space_bits[1:-1:2] + dp_bits
    return [order[i : i + 2] for i in range(0, len(order), 2)] + [space_bits[-1:]]


def masks_of(group):
    return [
        sum(bit for t, bit in enumerate(group) if r >> t & 1) for r in range(1, 1 << len(group))
    ]


def position_of(index, groups):
    place = 0
    for t, bit in enumerate([bit for group in groups for bit in group]):
        place = place | (((index >> (bit.bit_length() - 1)) & 1) << t)
    return place


def exchange(value, mask, devices):
    return lax.ppermute(value, AXES, [(i, i ^ mask) for i in range(devices)])


def swap_far(value):
    count = lax.axis_size("space")
    pairs = [(s, s + 1) for s in range(1, count - 1, 2)]
    return lax.ppermute(value, "space", pairs + [(t, s) for s, t in pairs])


def owner_rules(plan_ref, offset, first):
    codes = [plan_ref[offset, first + j] for j in range(SLOTS)]
    return [(code >> 3, code & 7) for code in codes]


def pack_kernel(x_hbm, rules_hbm, counts_hbm, halo_ref, rules, counts, tail, sems):
    copies = [
        pltpu.make_async_copy(x_hbm, halo_ref.at[:IN_ROWS], sems.at[0]),
        pltpu.make_async_copy(rules_hbm, rules, sems.at[1]),
        pltpu.make_async_copy(counts_hbm, counts, sems.at[2]),
    ]
    for copy in copies:
        copy.start()
    tail[...] = jnp.zeros_like(tail)
    copies[1].wait()
    for part in range(3):
        tail[OFFS * part : OFFS * (part + 1), :SLOTS] = rules[part].astype(jnp.float32)
    copies[2].wait()
    tail[3 * OFFS : 3 * OFFS + 1, :OFFS] = counts[...].astype(jnp.float32)
    halo_ref[IN_ROWS:] = tail[...].astype(jnp.bfloat16)
    copies[0].wait()


def main_kernel(
    positions, plan_ref, x_ref, a_ref, b_ref, near_ref, far_ref, cot_ref,
    act_ref, grad_ref, near_grad_ref, far_grad_ref, keep_ref, send_ref, w_ref,
    x_all, xt_all, acc, g_all, term_ref,
):
    core, flip = plan_ref[0, CORE], plan_ref[0, FLIP]
    for slab, ref in enumerate((x_ref, a_ref, b_ref)):
        for i in range(IN_BLK):
            block = ref[i * BR : (i + 1) * BR]
            x_all[slab * IN_BLK + i] = block
            xt_all[slab * IN_BLK + i] = block.T
    for pair, position in enumerate(positions):
        place = position ^ flip
        a, b = near_ref[place], far_ref[place]
        w_ref[2 * pair * ROWS : (2 * pair + 1) * ROWS] = jnp.where(core == 0, a, b)
        w_ref[(2 * pair + 1) * ROWS : (2 * pair + 2) * ROWS] = jnp.where(core == 0, b, a)

    acc[...] = jnp.zeros_like(acc)
    for offset in range(OFFS):
        kernel = w_ref[offset * CI : (offset + 1) * CI]

        def add_products(chunk, offset=offset, kernel=kernel):
            rules = owner_rules(plan_ref, offset, chunk * SLOTS)
            picked = jnp.concatenate([x_all[i] for i, _ in rules], 0)
            product = jnp.dot(picked, kernel, preferred_element_type=jnp.float32)
            for j, (_, slot) in enumerate(rules):
                acc[slot] += product[j * BR : (j + 1) * BR]

        add_products(0)
        pl.loop(1, plan_ref[offset, CHUNKS])(add_products)

    for o in range(OUT_BLK):
        pre = acc[o]
        sigma = jax.nn.sigmoid(pre)
        act_ref[o] = (pre * sigma).astype(jnp.bfloat16)
        upstream = cot_ref[o].astype(jnp.float32)
        grad = (upstream * sigma * (1.0 + pre * (1.0 - sigma))).astype(jnp.bfloat16)
        grad_ref[o] = grad
        g_all[o] = grad
    g_all[OUT_BLK] = jnp.zeros((BR, CO), jnp.bfloat16)
    low, high = grad_ref[:BND], grad_ref[OUT_BLK - BND :]
    near_grad_ref[...] = jnp.where(core == 0, high, low)
    far_grad_ref[...] = jnp.where(core == 0, low, high)

    for offset in range(OFFS):

        def terms(chunk, offset=offset):
            rules = owner_rules(plan_ref, offset, chunk * SLOTS)
            left = jnp.concatenate([xt_all[i] for i, _ in rules], 1)
            right = jnp.concatenate([g_all[slot] for _, slot in rules], 0)
            return jnp.dot(left, right, preferred_element_type=jnp.float32)

        def add_terms(chunk):
            term_ref[...] += terms(chunk)

        term_ref[...] = terms(0)
        pl.loop(1, plan_ref[offset, CHUNKS])(add_terms)
        per = CI // (2 * ROWS)
        for pair in range(per):
            place = positions[offset * per + pair] ^ flip
            a = term_ref[2 * pair * ROWS : (2 * pair + 1) * ROWS]
            b = term_ref[(2 * pair + 1) * ROWS : (2 * pair + 2) * ROWS]
            keep_ref[place] = jnp.where(core == 0, a, b)
            send_ref[place] = jnp.where(core == 0, b, a).astype(jnp.bfloat16)


def feature_grad_kernel(plan_ref, grad_ref, near_ref, far_ref, w_ref, out_ref, g_all, acc):
    core = plan_ref[0, CORE]
    near, far = near_ref[...], far_ref[...]
    g_all[:BND] = jnp.where(core == 0, far, near)
    g_all[BND : BND + OUT_BLK] = grad_ref[...]
    g_all[BND + OUT_BLK : EXT] = jnp.where(core == 0, near, far)
    g_all[EXT] = jnp.zeros((BR, CO), jnp.bfloat16)
    acc[...] = jnp.zeros_like(acc)
    for offset in range(OFFS):
        codes = [plan_ref[offset, BACK + j] for j in range(SLOTS)]
        rules = [(code >> 4, code & 15) for code in codes]
        grads = jnp.concatenate([g_all[slot] for _, slot in rules], 0)
        kernel = w_ref[offset * CI : (offset + 1) * CI]
        back = lax.dot_general(
            grads, kernel, (((1,), (1,)), ((), ())), preferred_element_type=jnp.float32
        )
        for j, (i, _) in enumerate(rules):
            acc[i] += back[j * BR : (j + 1) * BR]
    out_ref[...] = acc[...].astype(jnp.bfloat16)


def call(kernel, name, in_specs, out_shape, scratch, flops, moved):
    return pl.pallas_call(
        kernel,
        name=name,
        out_shape=out_shape,
        in_specs=in_specs,
        out_specs=jax.tree.map(lambda _: VMEM, out_shape),
        scratch_shapes=scratch,
        compiler_params=pltpu.CompilerParams(vmem_limit_bytes=24 * 1024 * 1024),
        cost_estimate=pl.CostEstimate(flops=flops, bytes_accessed=moved, transcendentals=0),
    )


def shape(dims, dtype=jnp.bfloat16):
    return jax.ShapeDtypeStruct(dims, dtype)


def plan_of(tables, counts, slab, flip):
    slots = jnp.arange(SLOTS, dtype=jnp.int32)
    in_index = tables[:, 0] + IN_BLK * jnp.arange(SLABS, dtype=jnp.int32)[:, None, None]
    out_index, owner = tables[:, 1], tables[:, 2]
    valid = slots < counts[:, :, None]
    live = jnp.swapaxes(valid & (owner == slab), 0, 1).reshape(OFFS, RULES)
    code = jnp.swapaxes(in_index * 8 + out_index, 0, 1).reshape(OFFS, RULES)
    order = jnp.arange(RULES, dtype=jnp.int32)
    earlier = order[:, None] > order[None, :]
    rank = jnp.sum(jnp.where(live[:, None, :] & earlier, 1, 0), 2)
    count = jnp.sum(jnp.where(live, 1, 0), 1, keepdims=True)
    chosen = live[:, None, :] & (rank[:, None, :] == order[:, None])
    packed = jnp.sum(jnp.where(chosen, code[:, None, :], 0), 2)
    packed = jnp.where(order < count, packed, OUT_BLK)
    ext = jnp.where(valid[0], BND + out_index[0] + (owner[0] - slab) * OUT_BLK, EXT)
    back = tables[0, 0] * 16 + ext
    scalars = jnp.broadcast_to(jnp.stack([slab & 1, flip]), (OFFS, 2))
    return jnp.concatenate([packed, back, (count + SLOTS - 1) // SLOTS, scalars], 1)


def local(features, weight, rulebook, rule_counts, cotangent):
    dp, space = lax.axis_size("dp"), lax.axis_size("space")
    devices = dp * space
    groups = phases_of(dp, space)
    rows = weight.shape[0]
    slab = lax.axis_index("space").astype(jnp.int32)
    me = lax.axis_index("dp").astype(jnp.int32) * space + slab
    direct = rows == ROWS

    own_rules = jnp.swapaxes(rulebook[0], 0, 1)
    halo = pl.pallas_call(
        pack_kernel,
        name="pack",
        out_shape=shape((IN_ROWS + TAIL, CI)),
        in_specs=[pl.BlockSpec(memory_space=pl.ANY)] * 3,
        out_specs=VMEM,
        scratch_shapes=[
            pltpu.VMEM((3, OFFS, SLOTS), jnp.int32),
            pltpu.VMEM((1, OFFS), jnp.int32),
            pltpu.VMEM((TAIL, CI), jnp.float32),
            pltpu.SemaphoreType.DMA((3,)),
        ],
        cost_estimate=pl.CostEstimate(flops=0, bytes_accessed=1 << 20, transcendentals=0),
    )(features[0], own_rules, rule_counts)

    parts = weight[None]
    beside = None
    for group in groups[:-1]:
        received = [exchange(parts, bit, devices) for bit in group]
        if len(group) == 2 and beside is None:
            received.append(exchange(parts, group[0] | group[1], devices))
        elif len(group) == 2:
            received.append(exchange(received[0], group[1], devices))
        if beside is None:
            beside = (exchange(halo, 1, devices), swap_far(halo))
        parts = jnp.concatenate([parts] + received, 0)
    far = exchange(parts, groups[-1][0], devices)
    slab_a, slab_b = beside

    tails = [other[IN_ROWS:, :SLOTS].astype(jnp.int32) for other in beside]
    flip = position_of(me & -2, groups) if direct else jnp.zeros((), jnp.int32)
    plan = plan_of(
        jnp.stack([own_rules] + [t[: 3 * OFFS].reshape(3, OFFS, SLOTS) for t in tails]),
        jnp.stack([rule_counts[0]] + [t[3 * OFFS] for t in tails]),
        slab,
        flip,
    )
    if direct:
        near = parts
        positions = [position_of(2 * pair, groups) for pair in range(PAIRS)]
    else:
        ids = np.arange(devices, dtype=np.int32)
        order = position_of(ids ^ me, groups)
        whole = jnp.concatenate([parts, far], 0)[order].reshape(PAIRS, 2, ROWS, CO)
        swapped = jnp.where((slab & 1) == 0, whole, whole[:, ::-1])
        near, far = swapped[:, 0], swapped[:, 1]
        positions = list(range(PAIRS))

    rule_flops = 2 * OFFS * SLOTS * BR * CI * CO
    activated, grad_pre, near_grad, far_grad, keep, send, kernels = call(
        lambda *refs: main_kernel(positions, *refs),
        "forward_and_weight_grad",
        [SMEM] + [VMEM] * 6,
        (
            shape((OUT_BLK, BR, CO)),
            shape((OUT_BLK, BR, CO)),
            shape((BND, BR, CO)),
            shape((BND, BR, CO)),
            shape((PAIRS, ROWS, CO), jnp.float32),
            shape((PAIRS, ROWS, CO)),
            shape((OFFS * CI, CO)),
        ),
        [
            pltpu.VMEM((SLABS * IN_BLK, BR, CI), jnp.bfloat16),
            pltpu.VMEM((SLABS * IN_BLK, CI, BR), jnp.bfloat16),
            pltpu.VMEM((OUT_BLK + 1, BR, CO), jnp.float32),
            pltpu.VMEM((OUT_BLK + 1, BR, CO), jnp.bfloat16),
            pltpu.VMEM((CI, CO), jnp.float32),
        ],
        2 * rule_flops,
        1 << 23,
    )(plan, features[0], slab_a, slab_b, near, far, cotangent[0].reshape(OUT_BLK, BR, CO))

    if not direct:
        terms = jnp.stack([keep, send.astype(jnp.float32)], 1)
        terms = jnp.where((slab & 1) == 0, terms, terms[:, ::-1]).reshape(devices, rows, CO)
        source = np.argsort(position_of(ids, groups)).astype(np.int32) ^ me
        ordered = terms[source]
        keep, send = ordered[: devices // 2], ordered[devices // 2 :].astype(jnp.bfloat16)
    total = keep + exchange(send, groups[-1][0], devices).astype(jnp.float32)

    near_rim = exchange(near_grad, 1, devices)
    far_rim = swap_far(far_grad)
    grad_in = call(
        feature_grad_kernel,
        "feature_grad",
        [SMEM] + [VMEM] * 4,
        shape((IN_BLK, BR, CI)),
        [
            pltpu.VMEM((EXT + 1, BR, CO), jnp.bfloat16),
            pltpu.VMEM((IN_BLK, BR, CI), jnp.float32),
        ],
        rule_flops,
        1 << 22,
    )(plan, grad_pre, near_rim, far_rim, kernels)

    for group in reversed(groups[:-1]):
        masks = masks_of(group)
        count = total.shape[0] // (len(masks) + 1)
        received = [
            exchange(total[(r + 1) * count : (r + 2) * count].astype(jnp.bfloat16), mask, devices)
            for r, mask in enumerate(masks)
        ]
        total = total[:count]
        for piece in received:
            total = total + piece.astype(jnp.float32)
    grad_weight = total[0] * grad_scale
    return (
        activated.reshape(1, OUT_BLK * BR, CO),
        grad_in.reshape(1, IN_ROWS, CI),
        grad_weight,
    )


def solution(mesh):
    in_specs = (
        P("dp", "space", None),
        P(("dp", "space"), None),
        P("dp", "space", None, None),
        P("dp", "space"),
        P("dp", "space", None),
    )
    out_specs = (P("dp", "space", None), P("dp", "space", None), P(("dp", "space"), None))
    return jax.shard_map(local, mesh=mesh, in_specs=in_specs, out_specs=out_specs, check_vma=False)
```

```python
import functools

import jax
import jax.numpy as jnp
import numpy as np
from jax import lax
from jax.experimental import pallas as pl
from jax.experimental.pallas import tpu as pltpu
from jax.sharding import PartitionSpec as P

CI = 256
CO = 256
OFFS = 8
BR = 128
BND = 2
SLOTS = 8
IN_BLK = 8
OUT_BLK = 4
EXT = OUT_BLK + 2 * BND
IN_ROWS = IN_BLK * BR
SLABS = 3
SLABS_HERE = 2
RULES = SLABS_HERE * SLOTS
STEP = 4
TAIL = 32
AXES = ("dp", "space")
BACK = RULES
COUNT = RULES + SLOTS
CORE = COUNT + 1
FLIP = COUNT + 2
PAIRS = 16
ROWS = OFFS * CI // (2 * PAIRS)

grad_scale = 1.0 / 2048.0

VMEM = pl.BlockSpec(memory_space=pltpu.VMEM)
SMEM = pl.BlockSpec(memory_space=pltpu.SMEM)


def phases_of(dp, space):
    space_bits = [1 << b for b in reversed(range(space.bit_length() - 1))]
    dp_bits = [space << b for b in reversed(range(dp.bit_length() - 1))]
    order = space_bits[:-1:2] + space_bits[1:-1:2] + dp_bits
    return [order[i : i + 2] for i in range(0, len(order), 2)] + [space_bits[-1:]]


def masks_of(group):
    return [
        sum(bit for t, bit in enumerate(group) if r >> t & 1) for r in range(1, 1 << len(group))
    ]


def position_of(index, groups):
    place = 0
    for t, bit in enumerate([bit for group in groups for bit in group]):
        place = place | (((index >> (bit.bit_length() - 1)) & 1) << t)
    return place


def exchange(value, mask, devices):
    return lax.ppermute(value, AXES, [(i, i ^ mask) for i in range(devices)])


def swap_far(value):
    count = lax.axis_size("space")
    pairs = [(s, s + 1) for s in range(1, count - 1, 2)]
    return lax.ppermute(value, "space", pairs + [(t, s) for s, t in pairs])


def rules_at(plan_ref, offset, first, count):
    codes = [plan_ref[offset, first + j] for j in range(count)]
    return [(code >> 3, code & 7) for code in codes]


def when_live(far_ref, offset, run):
    for first in range(0, SLOTS, STEP):
        rules = rules_at(far_ref, offset, first, STEP)
        live = functools.reduce(jnp.logical_or, [slot != OUT_BLK for _, slot in rules])
        pl.when(live)(functools.partial(run, far_ref, first, STEP))


def lay_out(ref, first, x_all, xt_all):
    for i in range(IN_BLK):
        block = ref[i * BR : (i + 1) * BR]
        x_all[first + i] = block
        xt_all[first + i] = block.T


def add_products(x_all, kernel, acc, offset, plan_ref, first, count):
    rules = rules_at(plan_ref, offset, first, count)
    picked = jnp.concatenate([x_all[i] for i, _ in rules], 0)
    product = jnp.dot(picked, kernel, preferred_element_type=jnp.float32)
    for j, (_, slot) in enumerate(rules):
        acc[slot] += product[j * BR : (j + 1) * BR]


def pack_kernel(x_hbm, rules_hbm, counts_hbm, halo_ref, rules, counts, tail, sems):
    copies = [
        pltpu.make_async_copy(x_hbm, halo_ref.at[:IN_ROWS], sems.at[0]),
        pltpu.make_async_copy(rules_hbm, rules, sems.at[1]),
        pltpu.make_async_copy(counts_hbm, counts, sems.at[2]),
    ]
    for copy in copies:
        copy.start()
    tail[...] = jnp.zeros_like(tail)
    copies[1].wait()
    for part in range(3):
        tail[OFFS * part : OFFS * (part + 1), :SLOTS] = rules[part].astype(jnp.float32)
    copies[2].wait()
    tail[3 * OFFS : 3 * OFFS + 1, :OFFS] = counts[...].astype(jnp.float32)
    halo_ref[IN_ROWS:] = tail[...].astype(jnp.bfloat16)
    copies[0].wait()


def forward_kernel(
    positions, plan_ref, x_ref, a_ref, near_ref, far_ref, w_ref, x_all, xt_all, acc
):
    core, flip = plan_ref[0, CORE], plan_ref[0, FLIP]
    lay_out(x_ref, 0, x_all, xt_all)
    lay_out(a_ref, IN_BLK, x_all, xt_all)
    for pair, position in enumerate(positions):
        place = position ^ flip
        a, b = near_ref[place], far_ref[place]
        w_ref[2 * pair * ROWS : (2 * pair + 1) * ROWS] = jnp.where(core == 0, a, b)
        w_ref[(2 * pair + 1) * ROWS : (2 * pair + 2) * ROWS] = jnp.where(core == 0, b, a)
    acc[...] = jnp.zeros_like(acc)
    for offset in range(OFFS):
        kernel = w_ref[offset * CI : (offset + 1) * CI]
        add = functools.partial(add_products, x_all, kernel, acc, offset, plan_ref)
        add(0, SLOTS)
        pl.loop(SLOTS, plan_ref[offset, COUNT], step=STEP)(functools.partial(add, count=STEP))


def weight_grad_kernel(
    positions, plan_ref, far_ref, b_ref, w_ref, cot_ref, _, __, ___,
    act_ref, grad_ref, near_grad_ref, far_grad_ref, keep_ref, send_ref, x_all, xt_all, acc,
    g_all, term_ref,
):
    core, flip = plan_ref[0, CORE], plan_ref[0, FLIP]
    lay_out(b_ref, 2 * IN_BLK, x_all, xt_all)
    for offset in range(OFFS):
        kernel = w_ref[offset * CI : (offset + 1) * CI]
        when_live(far_ref, offset, functools.partial(add_products, x_all, kernel, acc, offset))

    for o in range(OUT_BLK):
        pre = acc[o]
        sigma = jax.nn.sigmoid(pre)
        act_ref[o] = (pre * sigma).astype(jnp.bfloat16)
        upstream = cot_ref[o].astype(jnp.float32)
        grad = (upstream * sigma * (1.0 + pre * (1.0 - sigma))).astype(jnp.bfloat16)
        grad_ref[o] = grad
        g_all[o] = grad
    g_all[OUT_BLK] = jnp.zeros((BR, CO), jnp.bfloat16)
    low, high = grad_ref[:BND], grad_ref[OUT_BLK - BND :]
    near_grad_ref[...] = jnp.where(core == 0, high, low)
    far_grad_ref[...] = jnp.where(core == 0, low, high)

    for offset in range(OFFS):

        def terms(ref, first, count, offset=offset):
            rules = rules_at(ref, offset, first, count)
            left = jnp.concatenate([xt_all[i] for i, _ in rules], 1)
            right = jnp.concatenate([g_all[slot] for _, slot in rules], 0)
            return jnp.dot(left, right, preferred_element_type=jnp.float32)

        def add_terms(ref, first, count, terms=terms):
            term_ref[...] += terms(ref, first, count)

        term_ref[...] = terms(plan_ref, 0, SLOTS)
        pl.loop(SLOTS, plan_ref[offset, COUNT], step=STEP)(
            functools.partial(add_terms, plan_ref, count=STEP)
        )
        when_live(far_ref, offset, add_terms)
        per = CI // (2 * ROWS)
        for pair in range(per):
            place = positions[offset * per + pair] ^ flip
            a = term_ref[2 * pair * ROWS : (2 * pair + 1) * ROWS]
            b = term_ref[(2 * pair + 1) * ROWS : (2 * pair + 2) * ROWS]
            keep_ref[place] = jnp.where(core == 0, a, b)
            send_ref[place] = jnp.where(core == 0, b, a).astype(jnp.bfloat16)


def feature_grad_kernel(plan_ref, grad_ref, near_ref, far_ref, w_ref, out_ref, g_all, acc):
    core = plan_ref[0, CORE]
    near, far = near_ref[...], far_ref[...]
    g_all[:BND] = jnp.where(core == 0, far, near)
    g_all[BND : BND + OUT_BLK] = grad_ref[...]
    g_all[BND + OUT_BLK : EXT] = jnp.where(core == 0, near, far)
    g_all[EXT] = jnp.zeros((BR, CO), jnp.bfloat16)
    acc[...] = jnp.zeros_like(acc)
    for offset in range(OFFS):
        codes = [plan_ref[offset, BACK + j] for j in range(SLOTS)]
        rules = [(code >> 4, code & 15) for code in codes]
        grads = jnp.concatenate([g_all[slot] for _, slot in rules], 0)
        kernel = w_ref[offset * CI : (offset + 1) * CI]
        back = lax.dot_general(
            grads, kernel, (((1,), (1,)), ((), ())), preferred_element_type=jnp.float32
        )
        for j, (i, _) in enumerate(rules):
            acc[i] += back[j * BR : (j + 1) * BR]
    out_ref[...] = acc[...].astype(jnp.bfloat16)


def call(kernel, name, in_specs, out_shape, scratch, flops, moved, aliases={}):
    return pl.pallas_call(
        kernel,
        name=name,
        out_shape=out_shape,
        in_specs=in_specs,
        out_specs=jax.tree.map(lambda _: VMEM, out_shape),
        scratch_shapes=scratch,
        input_output_aliases=aliases,
        compiler_params=pltpu.CompilerParams(vmem_limit_bytes=24 * 1024 * 1024),
        cost_estimate=pl.CostEstimate(flops=flops, bytes_accessed=moved, transcendentals=0),
    )


def shape(dims, dtype=jnp.bfloat16):
    return jax.ShapeDtypeStruct(dims, dtype)


def plan_of(tables, counts, slab, flip):
    slots = jnp.arange(SLOTS, dtype=jnp.int32)
    in_index = tables[:, 0] + IN_BLK * jnp.arange(SLABS_HERE, dtype=jnp.int32)[:, None, None]
    out_index, owner = tables[:, 1], tables[:, 2]
    valid = slots < counts[:, :, None]
    live = jnp.swapaxes(valid & (owner == slab), 0, 1).reshape(OFFS, RULES)
    code = jnp.swapaxes(in_index * 8 + out_index, 0, 1).reshape(OFFS, RULES)
    order = jnp.arange(RULES, dtype=jnp.int32)
    earlier = order[:, None] > order[None, :]
    rank = jnp.sum(jnp.where(live[:, None, :] & earlier, 1, 0), 2)
    count = jnp.sum(jnp.where(live, 1, 0), 1, keepdims=True)
    chosen = live[:, None, :] & (rank[:, None, :] == order[:, None])
    packed = jnp.sum(jnp.where(chosen, code[:, None, :], 0), 2)
    packed = jnp.where(order < count, packed, OUT_BLK)
    ext = jnp.where(valid[0], BND + out_index[0] + (owner[0] - slab) * OUT_BLK, EXT)
    back = tables[0, 0] * 16 + ext
    scalars = jnp.broadcast_to(jnp.stack([slab & 1, flip]), (OFFS, 2))
    return jnp.concatenate([packed, back, count, scalars], 1)


def tail_of(halo):
    tail = halo[IN_ROWS:, :SLOTS].astype(jnp.int32)
    return tail[: 3 * OFFS].reshape(3, OFFS, SLOTS), tail[3 * OFFS]


def far_plan_of(tables, counts, slab):
    valid = jnp.arange(SLOTS, dtype=jnp.int32) < counts[:, None]
    live = valid & (tables[2] == slab)
    return jnp.where(live, (tables[0] + SLABS_HERE * IN_BLK) * 8 + tables[1], OUT_BLK)


def local(features, weight, rulebook, rule_counts, cotangent):
    dp, space = lax.axis_size("dp"), lax.axis_size("space")
    devices = dp * space
    groups = phases_of(dp, space)
    rows = weight.shape[0]
    slab = lax.axis_index("space").astype(jnp.int32)
    me = lax.axis_index("dp").astype(jnp.int32) * space + slab
    direct = rows == ROWS

    own_rules = jnp.swapaxes(rulebook[0], 0, 1)
    halo = pl.pallas_call(
        pack_kernel,
        name="pack",
        out_shape=shape((IN_ROWS + TAIL, CI)),
        in_specs=[pl.BlockSpec(memory_space=pl.ANY)] * 3,
        out_specs=VMEM,
        scratch_shapes=[
            pltpu.VMEM((3, OFFS, SLOTS), jnp.int32),
            pltpu.VMEM((1, OFFS), jnp.int32),
            pltpu.VMEM((TAIL, CI), jnp.float32),
            pltpu.SemaphoreType.DMA((3,)),
        ],
        cost_estimate=pl.CostEstimate(flops=0, bytes_accessed=1 << 20, transcendentals=0),
    )(features[0], own_rules, rule_counts)

    parts = weight[None]
    for group in groups[:-1]:
        received = [exchange(parts, mask, devices) for mask in masks_of(group)]
        if group is groups[0]:
            near_slab = exchange(halo, 1, devices)
        parts = jnp.concatenate([parts] + received, 0)
        if group is groups[0]:
            parts, halo = lax.optimization_barrier((parts, halo))
            far_slab = swap_far(halo)
    far = exchange(parts, groups[-1][0], devices)

    flip = position_of(me & -2, groups) if direct else jnp.zeros((), jnp.int32)
    rules, counts = own_rules, rule_counts[0]
    near_rules, near_counts = tail_of(near_slab)
    plan = plan_of(
        jnp.stack([rules, near_rules]), jnp.stack([counts, near_counts]), slab, flip
    )
    if direct:
        near = parts
        positions = [position_of(2 * pair, groups) for pair in range(PAIRS)]
    else:
        ids = np.arange(devices, dtype=np.int32)
        order = position_of(ids ^ me, groups)
        whole = jnp.concatenate([parts, far], 0)[order].reshape(PAIRS, 2, ROWS, CO)
        swapped = jnp.where((slab & 1) == 0, whole, whole[:, ::-1])
        near, far = swapped[:, 0], swapped[:, 1]
        positions = list(range(PAIRS))

    rule_flops = 2 * OFFS * SLOTS * BR * CI * CO
    carried = (
        shape((SLABS * IN_BLK, BR, CI)),
        shape((SLABS * IN_BLK, CI, BR)),
        shape((OUT_BLK + 1, BR, CO), jnp.float32),
    )
    kernels, *state = call(
        functools.partial(forward_kernel, positions),
        "forward",
        [SMEM] + [VMEM] * 4,
        (shape((OFFS * CI, CO)),) + carried,
        [],
        rule_flops,
        1 << 22,
    )(plan, features[0], near_slab, near, far)
    far_slab, kernels = lax.optimization_barrier((far_slab, kernels))
    far_plan = far_plan_of(*tail_of(far_slab), slab)
    activated, grad_pre, near_grad, far_grad, keep, send, *_ = call(
        functools.partial(weight_grad_kernel, positions),
        "weight_grad",
        [SMEM] * 2 + [VMEM] * 6,
        (
            shape((OUT_BLK, BR, CO)),
            shape((OUT_BLK, BR, CO)),
            shape((BND, BR, CO)),
            shape((BND, BR, CO)),
            shape((PAIRS, ROWS, CO), jnp.float32),
            shape((PAIRS, ROWS, CO)),
        )
        + carried,
        [
            pltpu.VMEM((OUT_BLK + 1, BR, CO), jnp.bfloat16),
            pltpu.VMEM((CI, CO), jnp.float32),
        ],
        2 * rule_flops,
        1 << 22,
        {5: 6, 6: 7, 7: 8},
    )(plan, far_plan, far_slab, kernels, cotangent[0].reshape(OUT_BLK, BR, CO), *state)

    if not direct:
        terms = jnp.stack([keep, send.astype(jnp.float32)], 1)
        terms = jnp.where((slab & 1) == 0, terms, terms[:, ::-1]).reshape(devices, rows, CO)
        source = np.argsort(position_of(ids, groups)).astype(np.int32) ^ me
        ordered = terms[source]
        keep, send = ordered[: devices // 2], ordered[devices // 2 :].astype(jnp.bfloat16)
    total = keep + exchange(send, groups[-1][0], devices).astype(jnp.float32)

    near_rim = exchange(near_grad, 1, devices)
    far_rim = swap_far(far_grad)
    grad_in = call(
        feature_grad_kernel,
        "feature_grad",
        [SMEM] + [VMEM] * 4,
        shape((IN_BLK, BR, CI)),
        [
            pltpu.VMEM((EXT + 1, BR, CO), jnp.bfloat16),
            pltpu.VMEM((IN_BLK, BR, CI), jnp.float32),
        ],
        rule_flops,
        1 << 22,
    )(plan, grad_pre, near_rim, far_rim, kernels)

    for group in reversed(groups[:-1]):
        masks = masks_of(group)
        count = total.shape[0] // (len(masks) + 1)
        received = [
            exchange(total[(r + 1) * count : (r + 2) * count].astype(jnp.bfloat16), mask, devices)
            for r, mask in enumerate(masks)
        ]
        total = total[:count]
        for piece in received:
            total = total + piece.astype(jnp.float32)
    grad_weight = total[0] * grad_scale
    return (
        activated.reshape(1, OUT_BLK * BR, CO),
        grad_in.reshape(1, IN_ROWS, CI),
        grad_weight,
    )


def solution(mesh):
    in_specs = (
        P("dp", "space", None),
        P(("dp", "space"), None),
        P("dp", "space", None, None),
        P("dp", "space"),
        P("dp", "space", None),
    )
    out_specs = (P("dp", "space", None), P("dp", "space", None), P(("dp", "space"), None))
    return jax.shard_map(local, mesh=mesh, in_specs=in_specs, out_specs=out_specs, check_vma=False)
```

```python
import functools

import jax
import jax.numpy as jnp
import numpy as np
from jax import lax
from jax.experimental import pallas as pl
from jax.experimental.pallas import tpu as pltpu
from jax.sharding import PartitionSpec as P

CI = 256
CO = 256
OFFS = 8
BR = 128
BND = 2
SLOTS = 8
IN_BLK = 8
OUT_BLK = 4
EXT = OUT_BLK + 2 * BND
IN_ROWS = IN_BLK * BR
TAIL = 32
AXES = ("dp", "space")
BACK = 2 * SLOTS
CORE = BACK + SLOTS
FLIP = CORE + 1
PAIRS = 16
ROWS = OFFS * CI // (2 * PAIRS)

grad_scale = 1.0 / 2048.0

VMEM = pl.BlockSpec(memory_space=pltpu.VMEM)
SMEM = pl.BlockSpec(memory_space=pltpu.SMEM)


def phases_of(dp, space):
    space_bits = [1 << b for b in reversed(range(space.bit_length() - 1))]
    dp_bits = [space << b for b in reversed(range(dp.bit_length() - 1))]
    order = space_bits[:-1:2] + space_bits[1:-1:2] + dp_bits
    return [order[i : i + 2] for i in range(0, len(order), 2)] + [space_bits[-1:]]


def masks_of(group):
    return [
        sum(bit for t, bit in enumerate(group) if r >> t & 1) for r in range(1, 1 << len(group))
    ]


def position_of(index, groups):
    place = 0
    for t, bit in enumerate([bit for group in groups for bit in group]):
        place = place | (((index >> (bit.bit_length() - 1)) & 1) << t)
    return place


def exchange(value, mask, devices):
    return lax.ppermute(value, AXES, [(i, i ^ mask) for i in range(devices)])


def swap_far(value):
    count = lax.axis_size("space")
    pairs = [(s, s + 1) for s in range(1, count - 1, 2)]
    return lax.ppermute(value, "space", pairs + [(t, s) for s, t in pairs])


def pack_kernel(x_hbm, rules_hbm, counts_hbm, halo_ref, rules, counts, tail, sems):
    copies = [
        pltpu.make_async_copy(x_hbm, halo_ref.at[:IN_ROWS], sems.at[0]),
        pltpu.make_async_copy(rules_hbm, rules, sems.at[1]),
        pltpu.make_async_copy(counts_hbm, counts, sems.at[2]),
    ]
    for copy in copies:
        copy.start()
    tail[...] = jnp.zeros_like(tail)
    copies[1].wait()
    for part in range(3):
        tail[OFFS * part : OFFS * (part + 1), :SLOTS] = rules[part].astype(jnp.float32)
    copies[2].wait()
    tail[3 * OFFS : 3 * OFFS + 1, :OFFS] = counts[...].astype(jnp.float32)
    halo_ref[IN_ROWS:] = tail[...].astype(jnp.bfloat16)
    copies[0].wait()


def block_at(ref, index):
    return ref[pl.ds(pl.multiple_of(index * BR, BR), BR)]


def sum_kernel(plan_ref, x_ref, a_ref, s_ref, st_ref, acc):
    for offset in range(OFFS):
        acc[...] = jnp.zeros_like(acc)
        for ref, first in ((x_ref, 0), (a_ref, SLOTS)):

            @pl.loop(0, SLOTS)
            def _(j, ref=ref, first=first, offset=offset):
                code = plan_ref[offset, first + j]

                @pl.when((code & 7) != OUT_BLK)
                def _():
                    acc[code & 7] += block_at(ref, code >> 3).astype(jnp.float32)

        for t in range(OUT_BLK):
            block = acc[t].astype(jnp.bfloat16)
            s_ref[offset, t] = block
            st_ref[offset, t] = block.T


def far_sum_kernel(far_plan_ref, b_ref, _, __, s_ref, st_ref):
    for offset in range(OFFS):

        @pl.loop(0, SLOTS)
        def _(j, offset=offset):
            code = far_plan_ref[offset, j]

            @pl.when((code & 7) != OUT_BLK)
            def _():
                t = code & 7
                extra = block_at(b_ref, code >> 3).astype(jnp.float32)
                block = (s_ref[offset, t].astype(jnp.float32) + extra).astype(jnp.bfloat16)
                s_ref[offset, t] = block
                st_ref[offset, t] = block.T


def main_kernel(
    positions, plan_ref, s_ref, st_ref, near_ref, far_ref, cot_ref,
    act_ref, grad_ref, near_grad_ref, far_grad_ref, keep_ref, send_ref, w_ref,
):
    core, flip = plan_ref[0, CORE], plan_ref[0, FLIP]
    for pair, position in enumerate(positions):
        place = position ^ flip
        a, b = near_ref[place], far_ref[place]
        w_ref[2 * pair * ROWS : (2 * pair + 1) * ROWS] = jnp.where(core == 0, a, b)
        w_ref[(2 * pair + 1) * ROWS : (2 * pair + 2) * ROWS] = jnp.where(core == 0, b, a)
    sums = jnp.concatenate([s_ref[k].reshape(OUT_BLK * BR, CI) for k in range(OFFS)], 1)
    pre = jnp.dot(sums, w_ref[...], preferred_element_type=jnp.float32)
    pre = pre.reshape(OUT_BLK, BR, CO)
    sigma = jax.nn.sigmoid(pre)
    act_ref[...] = (pre * sigma).astype(jnp.bfloat16)
    upstream = cot_ref[...].astype(jnp.float32)
    grad = (upstream * sigma * (1.0 + pre * (1.0 - sigma))).astype(jnp.bfloat16)
    grad_ref[...] = grad
    low, high = grad[:BND], grad[OUT_BLK - BND :]
    near_grad_ref[...] = jnp.where(core == 0, high, low)
    far_grad_ref[...] = jnp.where(core == 0, low, high)
    grads = grad_ref[...].reshape(OUT_BLK * BR, CO)
    per = CI // (2 * ROWS)
    for offset in range(OFFS):
        left = jnp.concatenate([st_ref[offset, t] for t in range(OUT_BLK)], 1)
        term = jnp.dot(left, grads, preferred_element_type=jnp.float32)
        for pair in range(per):
            place = positions[offset * per + pair] ^ flip
            a = term[2 * pair * ROWS : (2 * pair + 1) * ROWS]
            b = term[(2 * pair + 1) * ROWS : (2 * pair + 2) * ROWS]
            keep_ref[place] = jnp.where(core == 0, a, b)
            send_ref[place] = jnp.where(core == 0, b, a).astype(jnp.bfloat16)


def feature_grad_kernel(plan_ref, grad_ref, near_ref, far_ref, w_ref, out_ref, g_all, acc):
    core = plan_ref[0, CORE]
    near, far = near_ref[...], far_ref[...]
    g_all[:BND] = jnp.where(core == 0, far, near)
    g_all[BND : BND + OUT_BLK] = grad_ref[...]
    g_all[BND + OUT_BLK : EXT] = jnp.where(core == 0, near, far)
    g_all[EXT] = jnp.zeros((BR, CO), jnp.bfloat16)
    acc[...] = jnp.zeros_like(acc)
    for offset in range(OFFS):
        codes = [plan_ref[offset, BACK + j] for j in range(SLOTS)]
        rules = [(code >> 4, code & 15) for code in codes]
        grads = jnp.concatenate([g_all[slot] for _, slot in rules], 0)
        kernel = w_ref[offset * CI : (offset + 1) * CI]
        back = lax.dot_general(
            grads, kernel, (((1,), (1,)), ((), ())), preferred_element_type=jnp.float32
        )
        for j, (i, _) in enumerate(rules):
            acc[i] += back[j * BR : (j + 1) * BR]
    out_ref[...] = acc[...].astype(jnp.bfloat16)


def call(kernel, name, in_specs, out_shape, scratch, flops, moved, aliases={}):
    return pl.pallas_call(
        kernel,
        name=name,
        out_shape=out_shape,
        in_specs=in_specs,
        out_specs=jax.tree.map(lambda _: VMEM, out_shape),
        scratch_shapes=scratch,
        input_output_aliases=aliases,
        compiler_params=pltpu.CompilerParams(vmem_limit_bytes=24 * 1024 * 1024),
        cost_estimate=pl.CostEstimate(flops=flops, bytes_accessed=moved, transcendentals=0),
    )


def shape(dims, dtype=jnp.bfloat16):
    return jax.ShapeDtypeStruct(dims, dtype)


def codes_of(tables, counts, slab):
    valid = jnp.arange(SLOTS, dtype=jnp.int32) < counts[:, None]
    return jnp.where(valid & (tables[2] == slab), tables[0] * 8 + tables[1], OUT_BLK)


def back_codes_of(tables, counts, slab):
    valid = jnp.arange(SLOTS, dtype=jnp.int32) < counts[:, None]
    slot = BND + tables[1] + (tables[2] - slab) * OUT_BLK
    return tables[0] * 16 + jnp.where(valid, slot, EXT)


def tail_of(halo):
    tail = halo[IN_ROWS:, :SLOTS].astype(jnp.int32)
    return tail[: 3 * OFFS].reshape(3, OFFS, SLOTS), tail[3 * OFFS]


def local(features, weight, rulebook, rule_counts, cotangent):
    dp, space = lax.axis_size("dp"), lax.axis_size("space")
    devices = dp * space
    groups = phases_of(dp, space)
    rows = weight.shape[0]
    slab = lax.axis_index("space").astype(jnp.int32)
    me = lax.axis_index("dp").astype(jnp.int32) * space + slab
    direct = rows == ROWS

    own_rules = jnp.swapaxes(rulebook[0], 0, 1)
    halo = pl.pallas_call(
        pack_kernel,
        name="pack",
        out_shape=shape((IN_ROWS + TAIL, CI)),
        in_specs=[pl.BlockSpec(memory_space=pl.ANY)] * 3,
        out_specs=VMEM,
        scratch_shapes=[
            pltpu.VMEM((3, OFFS, SLOTS), jnp.int32),
            pltpu.VMEM((1, OFFS), jnp.int32),
            pltpu.VMEM((TAIL, CI), jnp.float32),
            pltpu.SemaphoreType.DMA((3,)),
        ],
        cost_estimate=pl.CostEstimate(flops=0, bytes_accessed=1 << 20, transcendentals=0),
    )(features[0], own_rules, rule_counts)

    parts = weight[None]
    for group in groups[:-1]:
        received = [exchange(parts, mask, devices) for mask in masks_of(group)]
        if group is groups[0]:
            near_slab, far_slab = exchange(halo, 1, devices), swap_far(halo)
        if group is groups[1]:
            flip = position_of(me & -2, groups) if direct else jnp.zeros((), jnp.int32)
            own = (own_rules, rule_counts[0], slab)
            scalars = jnp.broadcast_to(jnp.stack([slab & 1, flip]), (OFFS, 2))
            plan = jnp.concatenate(
                [codes_of(*own), codes_of(*tail_of(near_slab), slab), back_codes_of(*own), scalars], 1
            )
            sum_shapes = (shape((OFFS, OUT_BLK, BR, CI)), shape((OFFS, OUT_BLK, CI, BR)))
            sums = call(
                sum_kernel,
                "block_sums",
                [SMEM] + [VMEM] * 2,
                sum_shapes,
                [pltpu.VMEM((OUT_BLK + 1, BR, CI), jnp.float32)],
                0,
                1 << 23,
            )(plan, features[0], near_slab)
            parts, sums = lax.optimization_barrier((parts, sums))
        parts = jnp.concatenate([parts] + received, 0)
    far = exchange(parts, groups[-1][0], devices)
    far_plan = codes_of(*tail_of(far_slab), slab)

    if direct:
        near = parts
        positions = [position_of(2 * pair, groups) for pair in range(PAIRS)]
    else:
        ids = np.arange(devices, dtype=np.int32)
        order = position_of(ids ^ me, groups)
        whole = jnp.concatenate([parts, far], 0)[order].reshape(PAIRS, 2, ROWS, CO)
        swapped = jnp.where((slab & 1) == 0, whole, whole[:, ::-1])
        near, far = swapped[:, 0], swapped[:, 1]
        positions = list(range(PAIRS))

    rule_flops = 2 * OFFS * SLOTS * BR * CI * CO
    sums = call(
        far_sum_kernel,
        "far_sums",
        [SMEM] + [VMEM] * 3,
        sum_shapes,
        [],
        0,
        1 << 20,
        {2: 0, 3: 1},
    )(far_plan, far_slab, *sums)
    activated, grad_pre, near_grad, far_grad, keep, send, kernels = call(
        functools.partial(main_kernel, positions),
        "forward_and_weight_grad",
        [SMEM] + [VMEM] * 5,
        (
            shape((OUT_BLK, BR, CO)),
            shape((OUT_BLK, BR, CO)),
            shape((BND, BR, CO)),
            shape((BND, BR, CO)),
            shape((PAIRS, ROWS, CO), jnp.float32),
            shape((PAIRS, ROWS, CO)),
            shape((OFFS * CI, CO)),
        ),
        [],
        rule_flops,
        1 << 22,
    )(plan, *sums, near, far, cotangent[0].reshape(OUT_BLK, BR, CO))

    if not direct:
        terms = jnp.stack([keep, send.astype(jnp.float32)], 1)
        terms = jnp.where((slab & 1) == 0, terms, terms[:, ::-1]).reshape(devices, rows, CO)
        source = np.argsort(position_of(ids, groups)).astype(np.int32) ^ me
        ordered = terms[source]
        keep, send = ordered[: devices // 2], ordered[devices // 2 :].astype(jnp.bfloat16)
    total = keep + exchange(send, groups[-1][0], devices).astype(jnp.float32)

    near_rim = exchange(near_grad, 1, devices)
    far_rim = swap_far(far_grad)
    grad_in = call(
        feature_grad_kernel,
        "feature_grad",
        [SMEM] + [VMEM] * 4,
        shape((IN_BLK, BR, CI)),
        [
            pltpu.VMEM((EXT + 1, BR, CO), jnp.bfloat16),
            pltpu.VMEM((IN_BLK, BR, CI), jnp.float32),
        ],
        rule_flops,
        1 << 22,
    )(plan, grad_pre, near_rim, far_rim, kernels)

    for group in reversed(groups[:-1]):
        masks = masks_of(group)
        count = total.shape[0] // (len(masks) + 1)
        received = [
            exchange(total[(r + 1) * count : (r + 2) * count].astype(jnp.bfloat16), mask, devices)
            for r, mask in enumerate(masks)
        ]
        total = total[:count]
        for piece in received:
            total = total + piece.astype(jnp.float32)
    grad_weight = total[0] * grad_scale
    return (
        activated.reshape(1, OUT_BLK * BR, CO),
        grad_in.reshape(1, IN_ROWS, CI),
        grad_weight,
    )


def solution(mesh):
    in_specs = (
        P("dp", "space", None),
        P(("dp", "space"), None),
        P("dp", "space", None, None),
        P("dp", "space"),
        P("dp", "space", None),
    )
    out_specs = (P("dp", "space", None), P("dp", "space", None), P(("dp", "space"), None))
    return jax.shard_map(local, mesh=mesh, in_specs=in_specs, out_specs=out_specs, check_vma=False)
```

```python
import functools

import jax
import jax.numpy as jnp
import numpy as np
from jax import lax
from jax.experimental import pallas as pl
from jax.experimental.pallas import tpu as pltpu
from jax.sharding import PartitionSpec as P

CI = 256
CO = 256
OFFS = 8
BR = 128
BND = 2
SLOTS = 8
IN_BLK = 8
OUT_BLK = 4
EXT = OUT_BLK + 2 * BND
IN_ROWS = IN_BLK * BR
TAIL = 32
AXES = ("dp", "space")
BACK = 2 * SLOTS
CORE = BACK + SLOTS
FLIP = CORE + 1
PAIRS = 16
ROWS = OFFS * CI // (2 * PAIRS)

grad_scale = 1.0 / 2048.0

VMEM = pl.BlockSpec(memory_space=pltpu.VMEM)
SMEM = pl.BlockSpec(memory_space=pltpu.SMEM)


def phases_of(dp, space):
    space_bits = [1 << b for b in reversed(range(space.bit_length() - 1))]
    dp_bits = [space << b for b in reversed(range(dp.bit_length() - 1))]
    order = space_bits[:-1:2] + space_bits[1:-1:2] + dp_bits
    return [order[i : i + 2] for i in range(0, len(order), 2)] + [space_bits[-1:]]


def masks_of(group):
    return [
        sum(bit for t, bit in enumerate(group) if r >> t & 1) for r in range(1, 1 << len(group))
    ]


def position_of(index, groups):
    place = 0
    for t, bit in enumerate([bit for group in groups for bit in group]):
        place = place | (((index >> (bit.bit_length() - 1)) & 1) << t)
    return place


def exchange(value, mask, devices):
    return lax.ppermute(value, AXES, [(i, i ^ mask) for i in range(devices)])


def swap_far(value):
    count = lax.axis_size("space")
    pairs = [(s, s + 1) for s in range(1, count - 1, 2)]
    return lax.ppermute(value, "space", pairs + [(t, s) for s, t in pairs])


def pack_kernel(
    x_hbm, rules_hbm, counts_hbm, weight_hbm, halo_ref, rules, counts, weight, tail, sems
):
    copies = [
        pltpu.make_async_copy(x_hbm, halo_ref.at[:IN_ROWS], sems.at[0]),
        pltpu.make_async_copy(rules_hbm, rules, sems.at[1]),
        pltpu.make_async_copy(counts_hbm, counts, sems.at[2]),
        pltpu.make_async_copy(weight_hbm, weight, sems.at[3]),
    ]
    for copy in copies:
        copy.start()
    tail[...] = jnp.zeros_like(tail)
    copies[1].wait()
    for part in range(3):
        tail[OFFS * part : OFFS * (part + 1), :SLOTS] = rules[part].astype(jnp.float32)
    copies[2].wait()
    tail[3 * OFFS : 3 * OFFS + 1, :OFFS] = counts[...].astype(jnp.float32)
    halo_ref[IN_ROWS:] = tail[...].astype(jnp.bfloat16)
    copies[3].wait()
    copies[0].wait()


def block_at(ref, index):
    return ref[pl.ds(pl.multiple_of(index * BR, BR), BR)]


def sum_kernel(plan_ref, x_ref, a_ref, s_ref, st_ref, acc):
    for offset in range(OFFS):
        acc[...] = jnp.zeros_like(acc)
        for ref, first in ((x_ref, 0), (a_ref, SLOTS)):

            @pl.loop(0, SLOTS)
            def _(j, ref=ref, first=first, offset=offset):
                code = plan_ref[offset, first + j]

                @pl.when((code & 7) != OUT_BLK)
                def _():
                    acc[code & 7] += block_at(ref, code >> 3).astype(jnp.float32)

        for t in range(OUT_BLK):
            block = acc[t].astype(jnp.bfloat16)
            s_ref[offset, t] = block
            st_ref[offset, t] = block.T


def far_sum_kernel(far_plan_ref, b_ref, _, __, s_ref, st_ref):
    for offset in range(OFFS):

        @pl.loop(0, SLOTS)
        def _(j, offset=offset):
            code = far_plan_ref[offset, j]

            @pl.when((code & 7) != OUT_BLK)
            def _():
                t = code & 7
                extra = block_at(b_ref, code >> 3).astype(jnp.float32)
                block = (s_ref[offset, t].astype(jnp.float32) + extra).astype(jnp.bfloat16)
                s_ref[offset, t] = block
                st_ref[offset, t] = block.T


def main_kernel(
    positions, plan_ref, s_ref, st_ref, near_ref, far_ref, cot_ref,
    act_ref, grad_ref, near_grad_ref, far_grad_ref, keep_ref, send_ref, w_ref,
):
    core, flip = plan_ref[0, CORE], plan_ref[0, FLIP]
    for pair, position in enumerate(positions):
        place = position ^ flip
        a, b = near_ref[place], far_ref[place]
        w_ref[2 * pair * ROWS : (2 * pair + 1) * ROWS] = jnp.where(core == 0, a, b)
        w_ref[(2 * pair + 1) * ROWS : (2 * pair + 2) * ROWS] = jnp.where(core == 0, b, a)
    sums = jnp.concatenate([s_ref[k].reshape(OUT_BLK * BR, CI) for k in range(OFFS)], 1)
    pre = jnp.dot(sums, w_ref[...], preferred_element_type=jnp.float32)
    pre = pre.reshape(OUT_BLK, BR, CO)
    sigma = jax.nn.sigmoid(pre)
    act_ref[...] = (pre * sigma).astype(jnp.bfloat16)
    upstream = cot_ref[...].astype(jnp.float32)
    grad = (upstream * sigma * (1.0 + pre * (1.0 - sigma))).astype(jnp.bfloat16)
    grad_ref[...] = grad
    low, high = grad[:BND], grad[OUT_BLK - BND :]
    near_grad_ref[...] = jnp.where(core == 0, high, low)
    far_grad_ref[...] = jnp.where(core == 0, low, high)
    grads = grad_ref[...].reshape(OUT_BLK * BR, CO)
    per = CI // (2 * ROWS)
    for offset in range(OFFS):
        left = jnp.concatenate([st_ref[offset, t] for t in range(OUT_BLK)], 1)
        term = jnp.dot(left, grads, preferred_element_type=jnp.float32)
        for pair in range(per):
            place = positions[offset * per + pair] ^ flip
            a = term[2 * pair * ROWS : (2 * pair + 1) * ROWS]
            b = term[(2 * pair + 1) * ROWS : (2 * pair + 2) * ROWS]
            keep_ref[place] = jnp.where(core == 0, a, b)
            send_ref[place] = jnp.where(core == 0, b, a).astype(jnp.bfloat16)


def feature_grad_kernel(plan_ref, grad_ref, near_ref, far_ref, w_ref, out_ref, g_all, acc):
    core = plan_ref[0, CORE]
    near, far = near_ref[...], far_ref[...]
    g_all[:BND] = jnp.where(core == 0, far, near)
    g_all[BND : BND + OUT_BLK] = grad_ref[...]
    g_all[BND + OUT_BLK : EXT] = jnp.where(core == 0, near, far)
    g_all[EXT] = jnp.zeros((BR, CO), jnp.bfloat16)
    acc[...] = jnp.zeros_like(acc)
    for offset in range(OFFS):
        codes = [plan_ref[offset, BACK + j] for j in range(SLOTS)]
        rules = [(code >> 4, code & 15) for code in codes]
        grads = jnp.concatenate([g_all[slot] for _, slot in rules], 0)
        kernel = w_ref[offset * CI : (offset + 1) * CI]
        back = lax.dot_general(
            grads, kernel, (((1,), (1,)), ((), ())), preferred_element_type=jnp.float32
        )
        for j, (i, _) in enumerate(rules):
            acc[i] += back[j * BR : (j + 1) * BR]
    out_ref[...] = acc[...].astype(jnp.bfloat16)


def call(kernel, name, in_specs, out_shape, scratch, flops, moved, aliases={}):
    return pl.pallas_call(
        kernel,
        name=name,
        out_shape=out_shape,
        in_specs=in_specs,
        out_specs=jax.tree.map(lambda _: VMEM, out_shape),
        scratch_shapes=scratch,
        input_output_aliases=aliases,
        compiler_params=pltpu.CompilerParams(vmem_limit_bytes=24 * 1024 * 1024),
        cost_estimate=pl.CostEstimate(flops=flops, bytes_accessed=moved, transcendentals=0),
    )


def shape(dims, dtype=jnp.bfloat16):
    return jax.ShapeDtypeStruct(dims, dtype)


def codes_of(tables, counts, slab):
    valid = jnp.arange(SLOTS, dtype=jnp.int32) < counts[:, None]
    return jnp.where(valid & (tables[2] == slab), tables[0] * 8 + tables[1], OUT_BLK)


def back_codes_of(tables, counts, slab):
    valid = jnp.arange(SLOTS, dtype=jnp.int32) < counts[:, None]
    slot = BND + tables[1] + (tables[2] - slab) * OUT_BLK
    return tables[0] * 16 + jnp.where(valid, slot, EXT)


def tail_of(halo):
    tail = halo[IN_ROWS:, :SLOTS].astype(jnp.int32)
    return tail[: 3 * OFFS].reshape(3, OFFS, SLOTS), tail[3 * OFFS]


def local(features, weight, rulebook, rule_counts, cotangent):
    dp, space = lax.axis_size("dp"), lax.axis_size("space")
    devices = dp * space
    groups = phases_of(dp, space)
    rows = weight.shape[0]
    slab = lax.axis_index("space").astype(jnp.int32)
    me = lax.axis_index("dp").astype(jnp.int32) * space + slab
    direct = rows == ROWS

    halo, own_rules, own_counts, own_weight = pl.pallas_call(
        pack_kernel,
        name="pack",
        out_shape=(
            shape((IN_ROWS + TAIL, CI)),
            shape((3, OFFS, SLOTS), jnp.int32),
            shape((1, OFFS), jnp.int32),
            shape((rows, CO)),
        ),
        in_specs=[pl.BlockSpec(memory_space=pl.ANY)] * 4,
        out_specs=(VMEM,) * 4,
        scratch_shapes=[
            pltpu.VMEM((TAIL, CI), jnp.float32),
            pltpu.SemaphoreType.DMA((4,)),
        ],
        cost_estimate=pl.CostEstimate(flops=0, bytes_accessed=1 << 20, transcendentals=0),
    )(features[0], jnp.swapaxes(rulebook[0], 0, 1), rule_counts, weight)

    parts = weight[None]
    for group in groups[:-1]:
        received = [exchange(parts, mask, devices) for mask in masks_of(group)]
        if group is groups[0]:
            far_slab = swap_far(halo)
        if group is groups[1]:
            near_slab = exchange(halo, 1, devices)
            flip = position_of(me & -2, groups) if direct else jnp.zeros((), jnp.int32)
            own = (own_rules, own_counts[0], slab)
            scalars = jnp.broadcast_to(jnp.stack([slab & 1, flip]), (OFFS, 2))
            plan = jnp.concatenate(
                [codes_of(*own), codes_of(*tail_of(near_slab), slab), back_codes_of(*own), scalars], 1
            )
            sum_shapes = (shape((OFFS, OUT_BLK, BR, CI)), shape((OFFS, OUT_BLK, CI, BR)))
            sums = call(
                sum_kernel,
                "block_sums",
                [SMEM] + [VMEM] * 2,
                sum_shapes,
                [pltpu.VMEM((OUT_BLK + 1, BR, CI), jnp.float32)],
                0,
                1 << 23,
            )(plan, halo, near_slab)
            parts, sums = lax.optimization_barrier((parts, sums))
        if group is groups[0]:
            parts = own_weight[None]
        parts = jnp.concatenate([parts] + received, 0)
        if group is groups[0]:
            parts, halo = lax.optimization_barrier((parts, halo))
    far = exchange(parts, groups[-1][0], devices)
    far_plan = codes_of(*tail_of(far_slab), slab)

    if direct:
        near = parts
        positions = [position_of(2 * pair, groups) for pair in range(PAIRS)]
    else:
        ids = np.arange(devices, dtype=np.int32)
        order = position_of(ids ^ me, groups)
        whole = jnp.concatenate([parts, far], 0)[order].reshape(PAIRS, 2, ROWS, CO)
        swapped = jnp.where((slab & 1) == 0, whole, whole[:, ::-1])
        near, far = swapped[:, 0], swapped[:, 1]
        positions = list(range(PAIRS))

    rule_flops = 2 * OFFS * SLOTS * BR * CI * CO
    sums = call(
        far_sum_kernel,
        "far_sums",
        [SMEM] + [VMEM] * 3,
        sum_shapes,
        [],
        0,
        1 << 20,
        {2: 0, 3: 1},
    )(far_plan, far_slab, *sums)
    activated, grad_pre, near_grad, far_grad, keep, send, kernels = call(
        functools.partial(main_kernel, positions),
        "forward_and_weight_grad",
        [SMEM] + [VMEM] * 5,
        (
            shape((OUT_BLK, BR, CO)),
            shape((OUT_BLK, BR, CO)),
            shape((BND, BR, CO)),
            shape((BND, BR, CO)),
            shape((PAIRS, ROWS, CO), jnp.float32),
            shape((PAIRS, ROWS, CO)),
            shape((OFFS * CI, CO)),
        ),
        [],
        rule_flops,
        1 << 22,
    )(plan, *sums, near, far, cotangent[0].reshape(OUT_BLK, BR, CO))

    if not direct:
        terms = jnp.stack([keep, send.astype(jnp.float32)], 1)
        terms = jnp.where((slab & 1) == 0, terms, terms[:, ::-1]).reshape(devices, rows, CO)
        source = np.argsort(position_of(ids, groups)).astype(np.int32) ^ me
        ordered = terms[source]
        keep, send = ordered[: devices // 2], ordered[devices // 2 :].astype(jnp.bfloat16)
    total = keep + exchange(send, groups[-1][0], devices).astype(jnp.float32)

    near_rim = exchange(near_grad, 1, devices)
    far_rim = swap_far(far_grad)
    grad_in = call(
        feature_grad_kernel,
        "feature_grad",
        [SMEM] + [VMEM] * 4,
        shape((IN_BLK, BR, CI)),
        [
            pltpu.VMEM((EXT + 1, BR, CO), jnp.bfloat16),
            pltpu.VMEM((IN_BLK, BR, CI), jnp.float32),
        ],
        rule_flops,
        1 << 22,
    )(plan, grad_pre, near_rim, far_rim, kernels)

    for group in reversed(groups[:-1]):
        masks = masks_of(group)
        count = total.shape[0] // (len(masks) + 1)
        received = [
            exchange(total[(r + 1) * count : (r + 2) * count].astype(jnp.bfloat16), mask, devices)
            for r, mask in enumerate(masks)
        ]
        total = total[:count]
        for piece in received:
            total = total + piece.astype(jnp.float32)
    grad_weight = total[0] * grad_scale
    return (
        activated.reshape(1, OUT_BLK * BR, CO),
        grad_in.reshape(1, IN_ROWS, CI),
        grad_weight,
    )


def solution(mesh):
    in_specs = (
        P("dp", "space", None),
        P(("dp", "space"), None),
        P("dp", "space", None, None),
        P("dp", "space"),
        P("dp", "space", None),
    )
    out_specs = (P("dp", "space", None), P("dp", "space", None), P(("dp", "space"), None))
    return jax.shard_map(local, mesh=mesh, in_specs=in_specs, out_specs=out_specs, check_vma=False)
```

```python
import functools

import jax
import jax.numpy as jnp
import numpy as np
from jax import lax
from jax.experimental import pallas as pl
from jax.experimental.pallas import tpu as pltpu
from jax.sharding import PartitionSpec as P

CI = 256
CO = 256
OFFS = 8
BR = 128
BND = 2
SLOTS = 8
IN_BLK = 8
OUT_BLK = 4
EXT = OUT_BLK + 2 * BND
IN_ROWS = IN_BLK * BR
TAIL = 32
AXES = ("dp", "space")
BACK = 2 * SLOTS
CORE = BACK + SLOTS
FLIP = CORE + 1
PAIRS = 16
ROWS = OFFS * CI // (2 * PAIRS)

grad_scale = 1.0 / 2048.0

VMEM = pl.BlockSpec(memory_space=pltpu.VMEM)
SMEM = pl.BlockSpec(memory_space=pltpu.SMEM)


def phases_of(dp, space):
    space_bits = [1 << b for b in reversed(range(space.bit_length() - 1))]
    dp_bits = [space << b for b in reversed(range(dp.bit_length() - 1))]
    order = space_bits[:-1:2] + space_bits[1:-1:2] + dp_bits
    return [order[i : i + 2] for i in range(0, len(order), 2)] + [space_bits[-1:]]


def masks_of(group):
    return [
        sum(bit for t, bit in enumerate(group) if r >> t & 1) for r in range(1, 1 << len(group))
    ]


def position_of(index, groups):
    place = 0
    for t, bit in enumerate([bit for group in groups for bit in group]):
        place = place | (((index >> (bit.bit_length() - 1)) & 1) << t)
    return place


def exchange(value, mask, devices):
    return lax.ppermute(value, AXES, [(i, i ^ mask) for i in range(devices)])


def swap_far(value):
    count = lax.axis_size("space")
    pairs = [(s, s + 1) for s in range(1, count - 1, 2)]
    return lax.ppermute(value, "space", pairs + [(t, s) for s, t in pairs])


def pack_kernel(x_hbm, rules_hbm, counts_hbm, halo_ref, rules, counts, tail, sems):
    copies = [
        pltpu.make_async_copy(x_hbm, halo_ref.at[:IN_ROWS], sems.at[0]),
        pltpu.make_async_copy(rules_hbm, rules, sems.at[1]),
        pltpu.make_async_copy(counts_hbm, counts, sems.at[2]),
    ]
    for copy in copies:
        copy.start()
    tail[...] = jnp.zeros_like(tail)
    copies[1].wait()
    for part in range(3):
        tail[OFFS * part : OFFS * (part + 1), :SLOTS] = rules[part].astype(jnp.float32)
    copies[2].wait()
    tail[3 * OFFS : 3 * OFFS + 1, :OFFS] = counts[...].astype(jnp.float32)
    halo_ref[IN_ROWS:] = tail[...].astype(jnp.bfloat16)
    copies[0].wait()


def block_at(ref, index):
    return ref[pl.ds(pl.multiple_of(index * BR, BR), BR)]


def sum_kernel(plan_ref, x_ref, a_ref, s_ref, st_ref, acc):
    for offset in range(OFFS):
        acc[...] = jnp.zeros_like(acc)
        for ref, first in ((x_ref, 0), (a_ref, SLOTS)):

            @pl.loop(0, SLOTS)
            def _(j, ref=ref, first=first, offset=offset):
                code = plan_ref[offset, first + j]

                @pl.when((code & 7) != OUT_BLK)
                def _():
                    acc[code & 7] += block_at(ref, code >> 3).astype(jnp.float32)

        for t in range(OUT_BLK):
            block = acc[t].astype(jnp.bfloat16)
            s_ref[offset, t] = block
            st_ref[offset, t] = block.T


def far_sum_kernel(far_plan_ref, b_ref, _, __, s_ref, st_ref):
    for offset in range(OFFS):

        @pl.loop(0, SLOTS)
        def _(j, offset=offset):
            code = far_plan_ref[offset, j]

            @pl.when((code & 7) != OUT_BLK)
            def _():
                t = code & 7
                extra = block_at(b_ref, code >> 3).astype(jnp.float32)
                block = (s_ref[offset, t].astype(jnp.float32) + extra).astype(jnp.bfloat16)
                s_ref[offset, t] = block
                st_ref[offset, t] = block.T


def main_kernel(
    positions, plan_ref, s_ref, st_ref, near_ref, far_ref, cot_ref,
    act_ref, grad_ref, near_grad_ref, far_grad_ref, keep_ref, send_ref, w_ref,
):
    core, flip = plan_ref[0, CORE], plan_ref[0, FLIP]
    for pair, position in enumerate(positions):
        place = position ^ flip
        a, b = near_ref[place], far_ref[place]
        w_ref[2 * pair * ROWS : (2 * pair + 1) * ROWS] = jnp.where(core == 0, a, b)
        w_ref[(2 * pair + 1) * ROWS : (2 * pair + 2) * ROWS] = jnp.where(core == 0, b, a)
    sums = jnp.concatenate([s_ref[k].reshape(OUT_BLK * BR, CI) for k in range(OFFS)], 1)
    pre = jnp.dot(sums, w_ref[...], preferred_element_type=jnp.float32)
    pre = pre.reshape(OUT_BLK, BR, CO)
    sigma = jax.nn.sigmoid(pre)
    act_ref[...] = (pre * sigma).astype(jnp.bfloat16)
    upstream = cot_ref[...].astype(jnp.float32)
    grad = (upstream * sigma * (1.0 + pre * (1.0 - sigma))).astype(jnp.bfloat16)
    grad_ref[...] = grad
    low, high = grad[:BND], grad[OUT_BLK - BND :]
    near_grad_ref[...] = jnp.where(core == 0, high, low)
    far_grad_ref[...] = jnp.where(core == 0, low, high)
    grads = grad_ref[...].reshape(OUT_BLK * BR, CO)
    per = CI // (2 * ROWS)
    for offset in range(OFFS):
        left = jnp.concatenate([st_ref[offset, t] for t in range(OUT_BLK)], 1)
        term = jnp.dot(left, grads, preferred_element_type=jnp.float32)
        for pair in range(per):
            place = positions[offset * per + pair] ^ flip
            a = term[2 * pair * ROWS : (2 * pair + 1) * ROWS]
            b = term[(2 * pair + 1) * ROWS : (2 * pair + 2) * ROWS]
            keep_ref[place] = jnp.where(core == 0, a, b)
            send_ref[place] = jnp.where(core == 0, b, a).astype(jnp.bfloat16)


def feature_grad_kernel(plan_ref, grad_ref, near_ref, far_ref, w_ref, out_ref, g_all, acc):
    core = plan_ref[0, CORE]
    near, far = near_ref[...], far_ref[...]
    g_all[:BND] = jnp.where(core == 0, far, near)
    g_all[BND : BND + OUT_BLK] = grad_ref[...]
    g_all[BND + OUT_BLK : EXT] = jnp.where(core == 0, near, far)
    g_all[EXT] = jnp.zeros((BR, CO), jnp.bfloat16)
    acc[...] = jnp.zeros_like(acc)
    for offset in range(OFFS):
        codes = [plan_ref[offset, BACK + j] for j in range(SLOTS)]
        rules = [(code >> 4, code & 15) for code in codes]
        grads = jnp.concatenate([g_all[slot] for _, slot in rules], 0)
        kernel = w_ref[offset * CI : (offset + 1) * CI]
        back = lax.dot_general(
            grads, kernel, (((1,), (1,)), ((), ())), preferred_element_type=jnp.float32
        )
        for j, (i, _) in enumerate(rules):
            acc[i] += back[j * BR : (j + 1) * BR]
    out_ref[...] = acc[...].astype(jnp.bfloat16)


def call(kernel, name, in_specs, out_shape, scratch, flops, moved, aliases={}):
    return pl.pallas_call(
        kernel,
        name=name,
        out_shape=out_shape,
        in_specs=in_specs,
        out_specs=jax.tree.map(lambda _: VMEM, out_shape),
        scratch_shapes=scratch,
        input_output_aliases=aliases,
        compiler_params=pltpu.CompilerParams(vmem_limit_bytes=24 * 1024 * 1024),
        cost_estimate=pl.CostEstimate(flops=flops, bytes_accessed=moved, transcendentals=0),
    )


def shape(dims, dtype=jnp.bfloat16):
    return jax.ShapeDtypeStruct(dims, dtype)


def codes_of(tables, counts, slab):
    valid = jnp.arange(SLOTS, dtype=jnp.int32) < counts[:, None]
    return jnp.where(valid & (tables[2] == slab), tables[0] * 8 + tables[1], OUT_BLK)


def back_codes_of(tables, counts, slab):
    valid = jnp.arange(SLOTS, dtype=jnp.int32) < counts[:, None]
    slot = BND + tables[1] + (tables[2] - slab) * OUT_BLK
    return tables[0] * 16 + jnp.where(valid, slot, EXT)


def tail_of(halo):
    tail = halo[IN_ROWS:, :SLOTS].astype(jnp.int32)
    return tail[: 3 * OFFS].reshape(3, OFFS, SLOTS), tail[3 * OFFS]


def local(features, weight, rulebook, rule_counts, cotangent):
    dp, space = lax.axis_size("dp"), lax.axis_size("space")
    devices = dp * space
    groups = phases_of(dp, space)
    rows = weight.shape[0]
    slab = lax.axis_index("space").astype(jnp.int32)
    me = lax.axis_index("dp").astype(jnp.int32) * space + slab
    direct = rows == ROWS

    own_rules = jnp.swapaxes(rulebook[0], 0, 1)
    halo = pl.pallas_call(
        pack_kernel,
        name="pack",
        out_shape=pltpu.VMEM((IN_ROWS + TAIL, CI), jnp.bfloat16),
        in_specs=[pl.BlockSpec(memory_space=pltpu.HBM)] * 3,
        out_specs=VMEM,
        scratch_shapes=[
            pltpu.VMEM((3, OFFS, SLOTS), jnp.int32),
            pltpu.VMEM((1, OFFS), jnp.int32),
            pltpu.VMEM((TAIL, CI), jnp.float32),
            pltpu.SemaphoreType.DMA((3,)),
        ],
        cost_estimate=pl.CostEstimate(flops=0, bytes_accessed=1 << 20, transcendentals=0),
    )(*[pltpu.with_memory_space_constraint(v, pltpu.HBM) for v in (features[0], own_rules, rule_counts)])

    parts = weight[None]
    for group in groups[:-1]:
        received = [exchange(parts, mask, devices) for mask in masks_of(group)]
        if group is groups[0]:
            near_slab, far_slab = exchange(halo, 1, devices), swap_far(halo)
        if group is groups[1]:
            flip = position_of(me & -2, groups) if direct else jnp.zeros((), jnp.int32)
            own = (own_rules, rule_counts[0], slab)
            scalars = jnp.broadcast_to(jnp.stack([slab & 1, flip]), (OFFS, 2))
            plan = jnp.concatenate(
                [codes_of(*own), codes_of(*tail_of(near_slab), slab), back_codes_of(*own), scalars], 1
            )
            sum_shapes = (shape((OFFS, OUT_BLK, BR, CI)), shape((OFFS, OUT_BLK, CI, BR)))
            sums = call(
                sum_kernel,
                "block_sums",
                [SMEM] + [VMEM] * 2,
                sum_shapes,
                [pltpu.VMEM((OUT_BLK + 1, BR, CI), jnp.float32)],
                0,
                1 << 23,
            )(plan, halo, near_slab)
            parts, sums = lax.optimization_barrier((parts, sums))
        parts = jnp.concatenate([parts] + received, 0)
    far = exchange(parts, groups[-1][0], devices)
    far_plan = codes_of(*tail_of(far_slab), slab)

    if direct:
        near = parts
        positions = [position_of(2 * pair, groups) for pair in range(PAIRS)]
    else:
        ids = np.arange(devices, dtype=np.int32)
        order = position_of(ids ^ me, groups)
        whole = jnp.concatenate([parts, far], 0)[order].reshape(PAIRS, 2, ROWS, CO)
        swapped = jnp.where((slab & 1) == 0, whole, whole[:, ::-1])
        near, far = swapped[:, 0], swapped[:, 1]
        positions = list(range(PAIRS))

    rule_flops = 2 * OFFS * SLOTS * BR * CI * CO
    sums = call(
        far_sum_kernel,
        "far_sums",
        [SMEM] + [VMEM] * 3,
        sum_shapes,
        [],
        0,
        1 << 20,
        {2: 0, 3: 1},
    )(far_plan, far_slab, *sums)
    activated, grad_pre, near_grad, far_grad, keep, send, kernels = call(
        functools.partial(main_kernel, positions),
        "forward_and_weight_grad",
        [SMEM] + [VMEM] * 5,
        (
            shape((OUT_BLK, BR, CO)),
            shape((OUT_BLK, BR, CO)),
            shape((BND, BR, CO)),
            shape((BND, BR, CO)),
            shape((PAIRS, ROWS, CO), jnp.float32),
            shape((PAIRS, ROWS, CO)),
            shape((OFFS * CI, CO)),
        ),
        [],
        rule_flops,
        1 << 22,
    )(plan, *sums, near, far, cotangent[0].reshape(OUT_BLK, BR, CO))

    if not direct:
        terms = jnp.stack([keep, send.astype(jnp.float32)], 1)
        terms = jnp.where((slab & 1) == 0, terms, terms[:, ::-1]).reshape(devices, rows, CO)
        source = np.argsort(position_of(ids, groups)).astype(np.int32) ^ me
        ordered = terms[source]
        keep, send = ordered[: devices // 2], ordered[devices // 2 :].astype(jnp.bfloat16)
    total = keep + exchange(send, groups[-1][0], devices).astype(jnp.float32)

    near_rim = exchange(near_grad, 1, devices)
    far_rim = swap_far(far_grad)
    grad_in = call(
        feature_grad_kernel,
        "feature_grad",
        [SMEM] + [VMEM] * 4,
        shape((IN_BLK, BR, CI)),
        [
            pltpu.VMEM((EXT + 1, BR, CO), jnp.bfloat16),
            pltpu.VMEM((IN_BLK, BR, CI), jnp.float32),
        ],
        rule_flops,
        1 << 22,
    )(plan, grad_pre, near_rim, far_rim, kernels)

    for group in reversed(groups[:-1]):
        masks = masks_of(group)
        count = total.shape[0] // (len(masks) + 1)
        received = [
            exchange(total[(r + 1) * count : (r + 2) * count].astype(jnp.bfloat16), mask, devices)
            for r, mask in enumerate(masks)
        ]
        total = total[:count]
        for piece in received:
            total = total + piece.astype(jnp.float32)
    grad_weight = total[0] * grad_scale
    return (
        activated.reshape(1, OUT_BLK * BR, CO),
        grad_in.reshape(1, IN_ROWS, CI),
        grad_weight,
    )


def solution(mesh):
    in_specs = (
        P("dp", "space", None),
        P(("dp", "space"), None),
        P("dp", "space", None, None),
        P("dp", "space"),
        P("dp", "space", None),
    )
    out_specs = (P("dp", "space", None), P("dp", "space", None), P(("dp", "space"), None))
    return jax.shard_map(local, mesh=mesh, in_specs=in_specs, out_specs=out_specs, check_vma=False)
```

```python
import functools

import jax
import jax.numpy as jnp
import numpy as np
from jax import lax
from jax.experimental import pallas as pl
from jax.experimental.pallas import tpu as pltpu
from jax.sharding import PartitionSpec as P

CI = 256
CO = 256
OFFS = 8
BR = 128
BND = 2
SLOTS = 8
IN_BLK = 8
OUT_BLK = 4
EXT = OUT_BLK + 2 * BND
IN_ROWS = IN_BLK * BR
TAIL = 32
AXES = ("dp", "space")
BACK = 2 * SLOTS
CORE = BACK + SLOTS
FLIP = CORE + 1
PAIRS = 16
ROWS = OFFS * CI // (2 * PAIRS)

grad_scale = 1.0 / 2048.0

VMEM = pl.BlockSpec(memory_space=pltpu.VMEM)
SMEM = pl.BlockSpec(memory_space=pltpu.SMEM)


def phases_of(dp, space):
    space_bits = [1 << b for b in reversed(range(space.bit_length() - 1))]
    dp_bits = [space << b for b in reversed(range(dp.bit_length() - 1))]
    order = space_bits[:-1:2] + space_bits[1:-1:2] + dp_bits
    return [order[i : i + 2] for i in range(0, len(order), 2)] + [space_bits[-1:]]


def masks_of(group):
    if len(group) == 1:
        return list(group)
    return [group[0] | group[1], group[1], group[0]]


def position_of(index, groups):
    place, t = 0, 0
    for group in groups:
        bits = [(index >> (bit.bit_length() - 1)) & 1 for bit in group]
        digit = bits[0] if len(group) == 1 else bits[0] | ((bits[0] ^ bits[1]) << 1)
        place = place | (digit << t)
        t += len(group)
    return place


def exchange(value, mask, devices):
    return lax.ppermute(value, AXES, [(i, i ^ mask) for i in range(devices)])


def swap_far(value):
    count = lax.axis_size("space")
    pairs = [(s, s + 1) for s in range(1, count - 1, 2)]
    return lax.ppermute(value, "space", pairs + [(t, s) for s, t in pairs])


def pack_kernel(x_hbm, rules_hbm, counts_hbm, halo_ref, rules, counts, tail, sems):
    copies = [
        pltpu.make_async_copy(x_hbm, halo_ref.at[:IN_ROWS], sems.at[0]),
        pltpu.make_async_copy(rules_hbm, rules, sems.at[1]),
        pltpu.make_async_copy(counts_hbm, counts, sems.at[2]),
    ]
    for copy in copies:
        copy.start()
    tail[...] = jnp.zeros_like(tail)
    copies[1].wait()
    for part in range(3):
        tail[OFFS * part : OFFS * (part + 1), :SLOTS] = rules[part].astype(jnp.float32)
    copies[2].wait()
    tail[3 * OFFS : 3 * OFFS + 1, :OFFS] = counts[...].astype(jnp.float32)
    halo_ref[IN_ROWS:] = tail[...].astype(jnp.bfloat16)
    copies[0].wait()


def block_at(ref, index):
    return ref[pl.ds(pl.multiple_of(index * BR, BR), BR)]


def sum_kernel(plan_ref, x_ref, a_ref, s_ref, st_ref, acc):
    for offset in range(OFFS):
        acc[...] = jnp.zeros_like(acc)
        for ref, first in ((x_ref, 0), (a_ref, SLOTS)):

            @pl.loop(0, SLOTS)
            def _(j, ref=ref, first=first, offset=offset):
                code = plan_ref[offset, first + j]

                @pl.when((code & 7) != OUT_BLK)
                def _():
                    acc[code & 7] += block_at(ref, code >> 3).astype(jnp.float32)

        for t in range(OUT_BLK):
            block = acc[t].astype(jnp.bfloat16)
            s_ref[offset, t] = block
            st_ref[offset, t] = block.T


def far_sum_kernel(far_plan_ref, b_ref, _, __, s_ref, st_ref):
    for offset in range(OFFS):

        @pl.loop(0, SLOTS)
        def _(j, offset=offset):
            code = far_plan_ref[offset, j]

            @pl.when((code & 7) != OUT_BLK)
            def _():
                t = code & 7
                extra = block_at(b_ref, code >> 3).astype(jnp.float32)
                block = (s_ref[offset, t].astype(jnp.float32) + extra).astype(jnp.bfloat16)
                s_ref[offset, t] = block
                st_ref[offset, t] = block.T


def main_kernel(
    positions, plan_ref, s_ref, st_ref, near_ref, far_ref, cot_ref,
    act_ref, grad_ref, near_grad_ref, far_grad_ref, keep_ref, send_ref, w_ref,
):
    core, flip = plan_ref[0, CORE], plan_ref[0, FLIP]
    for pair, position in enumerate(positions):
        place = position ^ flip
        a, b = near_ref[place], far_ref[place]
        w_ref[2 * pair * ROWS : (2 * pair + 1) * ROWS] = jnp.where(core == 0, a, b)
        w_ref[(2 * pair + 1) * ROWS : (2 * pair + 2) * ROWS] = jnp.where(core == 0, b, a)
    sums = jnp.concatenate([s_ref[k].reshape(OUT_BLK * BR, CI) for k in range(OFFS)], 1)
    pre = jnp.dot(sums, w_ref[...], preferred_element_type=jnp.float32)
    pre = pre.reshape(OUT_BLK, BR, CO)
    sigma = jax.nn.sigmoid(pre)
    act_ref[...] = (pre * sigma).astype(jnp.bfloat16)
    upstream = cot_ref[...].astype(jnp.float32)
    grad = (upstream * sigma * (1.0 + pre * (1.0 - sigma))).astype(jnp.bfloat16)
    grad_ref[...] = grad
    low, high = grad[:BND], grad[OUT_BLK - BND :]
    near_grad_ref[...] = jnp.where(core == 0, high, low)
    far_grad_ref[...] = jnp.where(core == 0, low, high)
    grads = grad_ref[...].reshape(OUT_BLK * BR, CO)
    per = CI // (2 * ROWS)
    for offset in range(OFFS):
        left = jnp.concatenate([st_ref[offset, t] for t in range(OUT_BLK)], 1)
        term = jnp.dot(left, grads, preferred_element_type=jnp.float32)
        for pair in range(per):
            place = positions[offset * per + pair] ^ flip
            a = term[2 * pair * ROWS : (2 * pair + 1) * ROWS]
            b = term[(2 * pair + 1) * ROWS : (2 * pair + 2) * ROWS]
            keep_ref[place] = jnp.where(core == 0, a, b)
            send_ref[place] = jnp.where(core == 0, b, a).astype(jnp.bfloat16)


def feature_grad_kernel(plan_ref, grad_ref, near_ref, far_ref, w_ref, out_ref, g_all, acc):
    core = plan_ref[0, CORE]
    near, far = near_ref[...], far_ref[...]
    g_all[:BND] = jnp.where(core == 0, far, near)
    g_all[BND : BND + OUT_BLK] = grad_ref[...]
    g_all[BND + OUT_BLK : EXT] = jnp.where(core == 0, near, far)
    g_all[EXT] = jnp.zeros((BR, CO), jnp.bfloat16)
    acc[...] = jnp.zeros_like(acc)
    for offset in range(OFFS):
        codes = [plan_ref[offset, BACK + j] for j in range(SLOTS)]
        rules = [(code >> 4, code & 15) for code in codes]
        grads = jnp.concatenate([g_all[slot] for _, slot in rules], 0)
        kernel = w_ref[offset * CI : (offset + 1) * CI]
        back = lax.dot_general(
            grads, kernel, (((1,), (1,)), ((), ())), preferred_element_type=jnp.float32
        )
        for j, (i, _) in enumerate(rules):
            acc[i] += back[j * BR : (j + 1) * BR]
    out_ref[...] = acc[...].astype(jnp.bfloat16)


def call(kernel, name, in_specs, out_shape, scratch, flops, moved, aliases={}):
    return pl.pallas_call(
        kernel,
        name=name,
        out_shape=out_shape,
        in_specs=in_specs,
        out_specs=jax.tree.map(lambda _: VMEM, out_shape),
        scratch_shapes=scratch,
        input_output_aliases=aliases,
        compiler_params=pltpu.CompilerParams(vmem_limit_bytes=24 * 1024 * 1024),
        cost_estimate=pl.CostEstimate(flops=flops, bytes_accessed=moved, transcendentals=0),
    )


def shape(dims, dtype=jnp.bfloat16):
    return jax.ShapeDtypeStruct(dims, dtype)


def codes_of(tables, counts, slab):
    valid = jnp.arange(SLOTS, dtype=jnp.int32) < counts[:, None]
    return jnp.where(valid & (tables[2] == slab), tables[0] * 8 + tables[1], OUT_BLK)


def back_codes_of(tables, counts, slab):
    valid = jnp.arange(SLOTS, dtype=jnp.int32) < counts[:, None]
    slot = BND + tables[1] + (tables[2] - slab) * OUT_BLK
    return tables[0] * 16 + jnp.where(valid, slot, EXT)


def tail_of(halo):
    tail = halo[IN_ROWS:, :SLOTS].astype(jnp.int32)
    return tail[: 3 * OFFS].reshape(3, OFFS, SLOTS), tail[3 * OFFS]


def local(features, weight, rulebook, rule_counts, cotangent):
    dp, space = lax.axis_size("dp"), lax.axis_size("space")
    devices = dp * space
    groups = phases_of(dp, space)
    rows = weight.shape[0]
    slab = lax.axis_index("space").astype(jnp.int32)
    me = lax.axis_index("dp").astype(jnp.int32) * space + slab
    direct = rows == ROWS

    own_rules = jnp.swapaxes(rulebook[0], 0, 1)
    halo = pl.pallas_call(
        pack_kernel,
        name="pack",
        out_shape=pltpu.VMEM((IN_ROWS + TAIL, CI), jnp.bfloat16),
        in_specs=[pl.BlockSpec(memory_space=pltpu.HBM)] * 3,
        out_specs=VMEM,
        scratch_shapes=[
            pltpu.VMEM((3, OFFS, SLOTS), jnp.int32),
            pltpu.VMEM((1, OFFS), jnp.int32),
            pltpu.VMEM((TAIL, CI), jnp.float32),
            pltpu.SemaphoreType.DMA((3,)),
        ],
        cost_estimate=pl.CostEstimate(flops=0, bytes_accessed=1 << 20, transcendentals=0),
    )(*[pltpu.with_memory_space_constraint(v, pltpu.HBM) for v in (features[0], own_rules, rule_counts)])

    parts = weight[None]
    for group in groups[:-1]:
        received = [exchange(parts, mask, devices) for mask in masks_of(group)]
        if group is groups[0]:
            near_slab, far_slab = exchange(halo, 1, devices), swap_far(halo)
        if group is groups[1]:
            flip = position_of(me & -2, groups) if direct else jnp.zeros((), jnp.int32)
            own = (own_rules, rule_counts[0], slab)
            scalars = jnp.broadcast_to(jnp.stack([slab & 1, flip]), (OFFS, 2))
            plan = jnp.concatenate(
                [codes_of(*own), codes_of(*tail_of(near_slab), slab), back_codes_of(*own), scalars], 1
            )
            sum_shapes = (shape((OFFS, OUT_BLK, BR, CI)), shape((OFFS, OUT_BLK, CI, BR)))
            sums = call(
                sum_kernel,
                "block_sums",
                [SMEM] + [VMEM] * 2,
                sum_shapes,
                [pltpu.VMEM((OUT_BLK + 1, BR, CI), jnp.float32)],
                0,
                1 << 23,
            )(plan, halo, near_slab)
            parts, sums = lax.optimization_barrier((parts, sums))
        parts = jnp.concatenate([parts] + received, 0)
    far = exchange(parts, groups[-1][0], devices)
    far_plan = codes_of(*tail_of(far_slab), slab)

    if direct:
        near = parts
        positions = [position_of(2 * pair, groups) for pair in range(PAIRS)]
    else:
        ids = np.arange(devices, dtype=np.int32)
        order = position_of(ids ^ me, groups)
        whole = jnp.concatenate([parts, far], 0)[order].reshape(PAIRS, 2, ROWS, CO)
        swapped = jnp.where((slab & 1) == 0, whole, whole[:, ::-1])
        near, far = swapped[:, 0], swapped[:, 1]
        positions = list(range(PAIRS))

    rule_flops = 2 * OFFS * SLOTS * BR * CI * CO
    sums = call(
        far_sum_kernel,
        "far_sums",
        [SMEM] + [VMEM] * 3,
        sum_shapes,
        [],
        0,
        1 << 20,
        {2: 0, 3: 1},
    )(far_plan, far_slab, *sums)
    activated, grad_pre, near_grad, far_grad, keep, send, kernels = call(
        functools.partial(main_kernel, positions),
        "forward_and_weight_grad",
        [SMEM] + [VMEM] * 5,
        (
            shape((OUT_BLK, BR, CO)),
            shape((OUT_BLK, BR, CO)),
            shape((BND, BR, CO)),
            shape((BND, BR, CO)),
            shape((PAIRS, ROWS, CO), jnp.float32),
            shape((PAIRS, ROWS, CO)),
            shape((OFFS * CI, CO)),
        ),
        [],
        rule_flops,
        1 << 22,
    )(plan, *sums, near, far, cotangent[0].reshape(OUT_BLK, BR, CO))

    if not direct:
        terms = jnp.stack([keep, send.astype(jnp.float32)], 1)
        terms = jnp.where((slab & 1) == 0, terms, terms[:, ::-1]).reshape(devices, rows, CO)
        source = np.argsort(position_of(ids, groups)).astype(np.int32) ^ me
        ordered = terms[source]
        keep, send = ordered[: devices // 2], ordered[devices // 2 :].astype(jnp.bfloat16)
    total = keep + exchange(send, groups[-1][0], devices).astype(jnp.float32)

    near_rim = exchange(near_grad, 1, devices)
    far_rim = swap_far(far_grad)
    grad_in = call(
        feature_grad_kernel,
        "feature_grad",
        [SMEM] + [VMEM] * 4,
        shape((IN_BLK, BR, CI)),
        [
            pltpu.VMEM((EXT + 1, BR, CO), jnp.bfloat16),
            pltpu.VMEM((IN_BLK, BR, CI), jnp.float32),
        ],
        rule_flops,
        1 << 22,
    )(plan, grad_pre, near_rim, far_rim, kernels)

    for group in reversed(groups[:-1]):
        masks = masks_of(group)
        count = total.shape[0] // (len(masks) + 1)
        received = [
            exchange(total[(r + 1) * count : (r + 2) * count].astype(jnp.bfloat16), mask, devices)
            for r, mask in enumerate(masks)
        ]
        total = total[:count]
        for piece in received:
            total = total + piece.astype(jnp.float32)
    grad_weight = total[0] * grad_scale
    return (
        activated.reshape(1, OUT_BLK * BR, CO),
        grad_in.reshape(1, IN_ROWS, CI),
        grad_weight,
    )


def solution(mesh):
    in_specs = (
        P("dp", "space", None),
        P(("dp", "space"), None),
        P("dp", "space", None, None),
        P("dp", "space"),
        P("dp", "space", None),
    )
    out_specs = (P("dp", "space", None), P("dp", "space", None), P(("dp", "space"), None))
    return jax.shard_map(local, mesh=mesh, in_specs=in_specs, out_specs=out_specs, check_vma=False)
```

```python
import functools

import jax
import jax.numpy as jnp
import numpy as np
from jax import lax
from jax.experimental import pallas as pl
from jax.experimental.pallas import tpu as pltpu
from jax.sharding import PartitionSpec as P

CI = 256
CO = 256
OFFS = 8
BR = 128
BND = 2
SLOTS = 8
IN_BLK = 8
OUT_BLK = 4
EXT = OUT_BLK + 2 * BND
IN_ROWS = IN_BLK * BR
TAIL = 32
TOGETHER = 4
AXES = ("dp", "space")
BACK = 2 * SLOTS
CORE = BACK + SLOTS
FLIP = CORE + 1
PAIRS = 16
ROWS = OFFS * CI // (2 * PAIRS)

grad_scale = 1.0 / 2048.0

VMEM = pl.BlockSpec(memory_space=pltpu.VMEM)
SMEM = pl.BlockSpec(memory_space=pltpu.SMEM)


def phases_of(dp, space):
    space_bits = [1 << b for b in reversed(range(space.bit_length() - 1))]
    dp_bits = [space << b for b in reversed(range(dp.bit_length() - 1))]
    order = space_bits[:-1:2] + space_bits[1:-1:2] + dp_bits
    return [order[i : i + 2] for i in range(0, len(order), 2)] + [space_bits[-1:]]


def masks_of(group):
    if len(group) == 1:
        return list(group)
    return [group[0] | group[1], group[1], group[0]]


def position_of(index, groups):
    place, t = 0, 0
    for group in groups:
        bits = [(index >> (bit.bit_length() - 1)) & 1 for bit in group]
        digit = bits[0] if len(group) == 1 else bits[0] | ((bits[0] ^ bits[1]) << 1)
        place = place | (digit << t)
        t += len(group)
    return place


def exchange(value, mask, devices):
    return lax.ppermute(value, AXES, [(i, i ^ mask) for i in range(devices)])


def swap_far(value):
    count = lax.axis_size("space")
    pairs = [(s, s + 1) for s in range(1, count - 1, 2)]
    return lax.ppermute(value, "space", pairs + [(t, s) for s, t in pairs])


def pack_kernel(x_hbm, rules_hbm, counts_hbm, halo_ref, rules, counts, tail, sems):
    copies = [
        pltpu.make_async_copy(x_hbm, halo_ref.at[:IN_ROWS], sems.at[0]),
        pltpu.make_async_copy(rules_hbm, rules, sems.at[1]),
        pltpu.make_async_copy(counts_hbm, counts, sems.at[2]),
    ]
    for copy in copies:
        copy.start()
    tail[...] = jnp.zeros_like(tail)
    copies[1].wait()
    for part in range(3):
        tail[OFFS * part : OFFS * (part + 1), :SLOTS] = rules[part].astype(jnp.float32)
    copies[2].wait()
    tail[3 * OFFS : 3 * OFFS + 1, :OFFS] = counts[...].astype(jnp.float32)
    halo_ref[IN_ROWS:] = tail[...].astype(jnp.bfloat16)
    copies[0].wait()


def block_at(ref, index):
    return ref[pl.ds(pl.multiple_of(index * BR, BR), BR)]


def sum_kernel(plan_ref, x_ref, a_ref, s_ref, st_ref, acc):
    for offset in range(OFFS):
        acc[...] = jnp.zeros_like(acc)
        for ref, first in ((x_ref, 0), (a_ref, SLOTS)):

            @pl.loop(0, SLOTS)
            def _(j, ref=ref, first=first, offset=offset):
                code = plan_ref[offset, first + j]

                @pl.when((code & 7) != OUT_BLK)
                def _():
                    acc[code & 7] += block_at(ref, code >> 3).astype(jnp.float32)

        for t in range(OUT_BLK):
            block = acc[t].astype(jnp.bfloat16)
            s_ref[offset, t] = block
            st_ref[offset, t] = block.T


def far_sum_kernel(far_plan_ref, b_ref, _, __, s_ref, st_ref):
    for offset in range(OFFS):

        @pl.loop(0, SLOTS)
        def _(j, offset=offset):
            code = far_plan_ref[offset, j]

            @pl.when((code & 7) != OUT_BLK)
            def _():
                t = code & 7
                extra = block_at(b_ref, code >> 3).astype(jnp.float32)
                block = (s_ref[offset, t].astype(jnp.float32) + extra).astype(jnp.bfloat16)
                s_ref[offset, t] = block
                st_ref[offset, t] = block.T


def main_kernel(
    positions, plan_ref, s_ref, st_ref, near_ref, far_ref, cot_ref,
    act_ref, grad_ref, near_grad_ref, far_grad_ref, keep_ref, send_ref, w_ref,
):
    core, flip = plan_ref[0, CORE], plan_ref[0, FLIP]
    for pair, position in enumerate(positions):
        place = position ^ flip
        a, b = near_ref[place], far_ref[place]
        w_ref[2 * pair * ROWS : (2 * pair + 1) * ROWS] = jnp.where(core == 0, a, b)
        w_ref[(2 * pair + 1) * ROWS : (2 * pair + 2) * ROWS] = jnp.where(core == 0, b, a)
    sums = jnp.concatenate([s_ref[k].reshape(OUT_BLK * BR, CI) for k in range(OFFS)], 1)
    pre = jnp.dot(sums, w_ref[...], preferred_element_type=jnp.float32)
    pre = pre.reshape(OUT_BLK, BR, CO)
    sigma = jax.nn.sigmoid(pre)
    act_ref[...] = (pre * sigma).astype(jnp.bfloat16)
    upstream = cot_ref[...].astype(jnp.float32)
    grad = (upstream * sigma * (1.0 + pre * (1.0 - sigma))).astype(jnp.bfloat16)
    grad_ref[...] = grad
    low, high = grad[:BND], grad[OUT_BLK - BND :]
    near_grad_ref[...] = jnp.where(core == 0, high, low)
    far_grad_ref[...] = jnp.where(core == 0, low, high)
    grads = grad_ref[...].reshape(OUT_BLK * BR, CO)
    per = CI // (2 * ROWS)
    for first in range(0, OFFS, TOGETHER):
        left = [
            jnp.concatenate([st_ref[offset, t] for t in range(OUT_BLK)], 1)
            for offset in range(first, first + TOGETHER)
        ]
        term = jnp.dot(jnp.concatenate(left, 0), grads, preferred_element_type=jnp.float32)
        for pair in range(TOGETHER * per):
            place = positions[first * per + pair] ^ flip
            a = term[2 * pair * ROWS : (2 * pair + 1) * ROWS]
            b = term[(2 * pair + 1) * ROWS : (2 * pair + 2) * ROWS]
            keep_ref[place] = jnp.where(core == 0, a, b)
            send_ref[place] = jnp.where(core == 0, b, a).astype(jnp.bfloat16)


def feature_grad_kernel(plan_ref, grad_ref, near_ref, far_ref, w_ref, out_ref, g_all, acc):
    core = plan_ref[0, CORE]
    near, far = near_ref[...], far_ref[...]
    g_all[:BND] = jnp.where(core == 0, far, near)
    g_all[BND : BND + OUT_BLK] = grad_ref[...]
    g_all[BND + OUT_BLK : EXT] = jnp.where(core == 0, near, far)
    g_all[EXT] = jnp.zeros((BR, CO), jnp.bfloat16)
    acc[...] = jnp.zeros_like(acc)
    for offset in range(OFFS):
        codes = [plan_ref[offset, BACK + j] for j in range(SLOTS)]
        rules = [(code >> 4, code & 15) for code in codes]
        grads = jnp.concatenate([g_all[slot] for _, slot in rules], 0)
        kernel = w_ref[offset * CI : (offset + 1) * CI]
        back = lax.dot_general(
            grads, kernel, (((1,), (1,)), ((), ())), preferred_element_type=jnp.float32
        )
        for j, (i, _) in enumerate(rules):
            acc[i] += back[j * BR : (j + 1) * BR]
    out_ref[...] = acc[...].astype(jnp.bfloat16)


def call(kernel, name, in_specs, out_shape, scratch, flops, moved, aliases={}):
    return pl.pallas_call(
        kernel,
        name=name,
        out_shape=out_shape,
        in_specs=in_specs,
        out_specs=jax.tree.map(lambda _: VMEM, out_shape),
        scratch_shapes=scratch,
        input_output_aliases=aliases,
        compiler_params=pltpu.CompilerParams(vmem_limit_bytes=24 * 1024 * 1024),
        cost_estimate=pl.CostEstimate(flops=flops, bytes_accessed=moved, transcendentals=0),
    )


def shape(dims, dtype=jnp.bfloat16):
    return jax.ShapeDtypeStruct(dims, dtype)


def codes_of(tables, counts, slab):
    valid = jnp.arange(SLOTS, dtype=jnp.int32) < counts[:, None]
    return jnp.where(valid & (tables[2] == slab), tables[0] * 8 + tables[1], OUT_BLK)


def back_codes_of(tables, counts, slab):
    valid = jnp.arange(SLOTS, dtype=jnp.int32) < counts[:, None]
    slot = BND + tables[1] + (tables[2] - slab) * OUT_BLK
    return tables[0] * 16 + jnp.where(valid, slot, EXT)


def tail_of(halo):
    tail = halo[IN_ROWS:, :SLOTS].astype(jnp.int32)
    return tail[: 3 * OFFS].reshape(3, OFFS, SLOTS), tail[3 * OFFS]


def local(features, weight, rulebook, rule_counts, cotangent):
    dp, space = lax.axis_size("dp"), lax.axis_size("space")
    devices = dp * space
    groups = phases_of(dp, space)
    rows = weight.shape[0]
    slab = lax.axis_index("space").astype(jnp.int32)
    me = lax.axis_index("dp").astype(jnp.int32) * space + slab
    direct = rows == ROWS

    own_rules = jnp.swapaxes(rulebook[0], 0, 1)
    halo = pl.pallas_call(
        pack_kernel,
        name="pack",
        out_shape=pltpu.VMEM((IN_ROWS + TAIL, CI), jnp.bfloat16),
        in_specs=[pl.BlockSpec(memory_space=pltpu.HBM)] * 3,
        out_specs=VMEM,
        scratch_shapes=[
            pltpu.VMEM((3, OFFS, SLOTS), jnp.int32),
            pltpu.VMEM((1, OFFS), jnp.int32),
            pltpu.VMEM((TAIL, CI), jnp.float32),
            pltpu.SemaphoreType.DMA((3,)),
        ],
        cost_estimate=pl.CostEstimate(flops=0, bytes_accessed=1 << 20, transcendentals=0),
    )(*[pltpu.with_memory_space_constraint(v, pltpu.HBM) for v in (features[0], own_rules, rule_counts)])

    parts = weight[None]
    for group in groups[:-1]:
        received = [exchange(parts, mask, devices) for mask in masks_of(group)]
        if group is groups[0]:
            near_slab, far_slab = exchange(halo, 1, devices), swap_far(halo)
        if group is groups[1]:
            flip = position_of(me & -2, groups) if direct else jnp.zeros((), jnp.int32)
            own = (own_rules, rule_counts[0], slab)
            scalars = jnp.broadcast_to(jnp.stack([slab & 1, flip]), (OFFS, 2))
            plan = jnp.concatenate(
                [codes_of(*own), codes_of(*tail_of(near_slab), slab), back_codes_of(*own), scalars], 1
            )
            sum_shapes = (shape((OFFS, OUT_BLK, BR, CI)), shape((OFFS, OUT_BLK, CI, BR)))
            sums = call(
                sum_kernel,
                "block_sums",
                [SMEM] + [VMEM] * 2,
                sum_shapes,
                [pltpu.VMEM((OUT_BLK + 1, BR, CI), jnp.float32)],
                0,
                1 << 23,
            )(plan, halo, near_slab)
            parts, sums = lax.optimization_barrier((parts, sums))
        parts = jnp.concatenate([parts] + received, 0)
    far = exchange(parts, groups[-1][0], devices)
    far_plan = codes_of(*tail_of(far_slab), slab)

    if direct:
        near = parts
        positions = [position_of(2 * pair, groups) for pair in range(PAIRS)]
    else:
        ids = np.arange(devices, dtype=np.int32)
        order = position_of(ids ^ me, groups)
        whole = jnp.concatenate([parts, far], 0)[order].reshape(PAIRS, 2, ROWS, CO)
        swapped = jnp.where((slab & 1) == 0, whole, whole[:, ::-1])
        near, far = swapped[:, 0], swapped[:, 1]
        positions = list(range(PAIRS))

    rule_flops = 2 * OFFS * SLOTS * BR * CI * CO
    sums = call(
        far_sum_kernel,
        "far_sums",
        [SMEM] + [VMEM] * 3,
        sum_shapes,
        [],
        0,
        1 << 20,
        {2: 0, 3: 1},
    )(far_plan, far_slab, *sums)
    activated, grad_pre, near_grad, far_grad, keep, send, kernels = call(
        functools.partial(main_kernel, positions),
        "forward_and_weight_grad",
        [SMEM] + [VMEM] * 5,
        (
            pltpu.VMEM((OUT_BLK, BR, CO), jnp.bfloat16),
            shape((OUT_BLK, BR, CO)),
            shape((BND, BR, CO)),
            shape((BND, BR, CO)),
            shape((PAIRS, ROWS, CO), jnp.float32),
            shape((PAIRS, ROWS, CO)),
            shape((OFFS * CI, CO)),
        ),
        [],
        rule_flops,
        1 << 22,
    )(plan, *sums, near, far, cotangent[0].reshape(OUT_BLK, BR, CO))

    if not direct:
        terms = jnp.stack([keep, send.astype(jnp.float32)], 1)
        terms = jnp.where((slab & 1) == 0, terms, terms[:, ::-1]).reshape(devices, rows, CO)
        source = np.argsort(position_of(ids, groups)).astype(np.int32) ^ me
        ordered = terms[source]
        keep, send = ordered[: devices // 2], ordered[devices // 2 :].astype(jnp.bfloat16)
    total = keep + exchange(send, groups[-1][0], devices).astype(jnp.float32)

    near_rim = exchange(near_grad, 1, devices)
    far_rim = swap_far(far_grad)
    grad_in = call(
        feature_grad_kernel,
        "feature_grad",
        [SMEM] + [VMEM] * 4,
        shape((IN_BLK, BR, CI)),
        [
            pltpu.VMEM((EXT + 1, BR, CO), jnp.bfloat16),
            pltpu.VMEM((IN_BLK, BR, CI), jnp.float32),
        ],
        rule_flops,
        1 << 22,
    )(plan, grad_pre, near_rim, far_rim, kernels)

    for group in reversed(groups[:-1]):
        masks = masks_of(group)
        count = total.shape[0] // (len(masks) + 1)
        received = [
            exchange(total[(r + 1) * count : (r + 2) * count].astype(jnp.bfloat16), mask, devices)
            for r, mask in enumerate(masks)
        ]
        total = total[:count]
        for piece in received:
            total = total + piece.astype(jnp.float32)
    grad_weight = total[0] * grad_scale
    return (
        activated.reshape(1, OUT_BLK * BR, CO),
        grad_in.reshape(1, IN_ROWS, CI),
        grad_weight,
    )


def solution(mesh):
    in_specs = (
        P("dp", "space", None),
        P(("dp", "space"), None),
        P("dp", "space", None, None),
        P("dp", "space"),
        P("dp", "space", None),
    )
    out_specs = (P("dp", "space", None), P("dp", "space", None), P(("dp", "space"), None))
    return jax.shard_map(local, mesh=mesh, in_specs=in_specs, out_specs=out_specs, check_vma=False)
```

```python
import functools

import jax
import jax.numpy as jnp
import numpy as np
from jax import lax
from jax.experimental import pallas as pl
from jax.experimental.pallas import tpu as pltpu
from jax.sharding import PartitionSpec as P

CI = 256
CO = 256
OFFS = 8
BR = 128
BND = 2
SLOTS = 8
IN_BLK = 8
OUT_BLK = 4
EXT = OUT_BLK + 2 * BND
IN_ROWS = IN_BLK * BR
TAIL = 32
TOGETHER = 4
AXES = ("dp", "space")
BACK = 2 * SLOTS
CORE = BACK + SLOTS
FLIP = CORE + 1
PAIRS = 16
ROWS = OFFS * CI // (2 * PAIRS)

grad_scale = 1.0 / 2048.0

VMEM = pl.BlockSpec(memory_space=pltpu.VMEM)
SMEM = pl.BlockSpec(memory_space=pltpu.SMEM)


def phases_of(dp, space):
    space_bits = [1 << b for b in reversed(range(space.bit_length() - 1))]
    dp_bits = [space << b for b in reversed(range(dp.bit_length() - 1))]
    order = space_bits[:-1:2] + space_bits[1:-1:2] + dp_bits
    return [order[i : i + 2] for i in range(0, len(order), 2)] + [space_bits[-1:]]


def masks_of(group):
    if len(group) == 1:
        return list(group)
    return [group[0] | group[1], group[1], group[0]]


def position_of(index, groups):
    place, t = 0, 0
    for group in groups:
        bits = [(index >> (bit.bit_length() - 1)) & 1 for bit in group]
        digit = bits[0] if len(group) == 1 else bits[0] | ((bits[0] ^ bits[1]) << 1)
        place = place | (digit << t)
        t += len(group)
    return place


def exchange(value, mask, devices):
    return lax.ppermute(value, AXES, [(i, i ^ mask) for i in range(devices)])


def swap_far(value):
    count = lax.axis_size("space")
    pairs = [(s, s + 1) for s in range(1, count - 1, 2)]
    return lax.ppermute(value, "space", pairs + [(t, s) for s, t in pairs])


def pack_kernel(x_hbm, rules_hbm, counts_hbm, halo_ref, rules, counts, tail, sems):
    copies = [
        pltpu.make_async_copy(x_hbm, halo_ref.at[:IN_ROWS], sems.at[0]),
        pltpu.make_async_copy(rules_hbm, rules, sems.at[1]),
        pltpu.make_async_copy(counts_hbm, counts, sems.at[2]),
    ]
    for copy in copies:
        copy.start()
    tail[...] = jnp.zeros_like(tail)
    copies[1].wait()
    for part in range(3):
        tail[OFFS * part : OFFS * (part + 1), :SLOTS] = rules[part].astype(jnp.float32)
    copies[2].wait()
    tail[3 * OFFS : 3 * OFFS + 1, :OFFS] = counts[...].astype(jnp.float32)
    halo_ref[IN_ROWS:] = tail[...].astype(jnp.bfloat16)
    copies[0].wait()


def fetch_kernel(weight_hbm, weight_ref, sem):
    copy = pltpu.make_async_copy(weight_hbm, weight_ref, sem)
    copy.start()
    copy.wait()


def block_at(ref, index):
    return ref[pl.ds(pl.multiple_of(index * BR, BR), BR)]


def sum_kernel(plan_ref, x_ref, a_ref, s_ref, st_ref, acc):
    for offset in range(OFFS):
        acc[...] = jnp.zeros_like(acc)
        for ref, first in ((x_ref, 0), (a_ref, SLOTS)):

            @pl.loop(0, SLOTS)
            def _(j, ref=ref, first=first, offset=offset):
                code = plan_ref[offset, first + j]

                @pl.when((code & 7) != OUT_BLK)
                def _():
                    acc[code & 7] += block_at(ref, code >> 3).astype(jnp.float32)

        for t in range(OUT_BLK):
            block = acc[t].astype(jnp.bfloat16)
            s_ref[offset, t] = block
            st_ref[offset, t] = block.T


def far_sum_kernel(far_plan_ref, b_ref, _, __, s_ref, st_ref):
    for offset in range(OFFS):

        @pl.loop(0, SLOTS)
        def _(j, offset=offset):
            code = far_plan_ref[offset, j]

            @pl.when((code & 7) != OUT_BLK)
            def _():
                t = code & 7
                extra = block_at(b_ref, code >> 3).astype(jnp.float32)
                block = (s_ref[offset, t].astype(jnp.float32) + extra).astype(jnp.bfloat16)
                s_ref[offset, t] = block
                st_ref[offset, t] = block.T


def main_kernel(
    positions, plan_ref, s_ref, st_ref, near_ref, far_ref, cot_ref,
    act_ref, grad_ref, near_grad_ref, far_grad_ref, keep_ref, send_ref, w_ref,
):
    core, flip = plan_ref[0, CORE], plan_ref[0, FLIP]
    for pair, position in enumerate(positions):
        place = position ^ flip
        a, b = near_ref[place], far_ref[place]
        w_ref[2 * pair * ROWS : (2 * pair + 1) * ROWS] = jnp.where(core == 0, a, b)
        w_ref[(2 * pair + 1) * ROWS : (2 * pair + 2) * ROWS] = jnp.where(core == 0, b, a)
    sums = jnp.concatenate([s_ref[k].reshape(OUT_BLK * BR, CI) for k in range(OFFS)], 1)
    pre = jnp.dot(sums, w_ref[...], preferred_element_type=jnp.float32)
    pre = pre.reshape(OUT_BLK, BR, CO)
    sigma = jax.nn.sigmoid(pre)
    act_ref[...] = (pre * sigma).astype(jnp.bfloat16)
    upstream = cot_ref[...].astype(jnp.float32)
    grad = (upstream * sigma * (1.0 + pre * (1.0 - sigma))).astype(jnp.bfloat16)
    grad_ref[...] = grad
    low, high = grad[:BND], grad[OUT_BLK - BND :]
    near_grad_ref[...] = jnp.where(core == 0, high, low)
    far_grad_ref[...] = jnp.where(core == 0, low, high)
    grads = grad_ref[...].reshape(OUT_BLK * BR, CO)
    per = CI // (2 * ROWS)
    for first in range(0, OFFS, TOGETHER):
        left = [
            jnp.concatenate([st_ref[offset, t] for t in range(OUT_BLK)], 1)
            for offset in range(first, first + TOGETHER)
        ]
        term = jnp.dot(jnp.concatenate(left, 0), grads, preferred_element_type=jnp.float32)
        for pair in range(TOGETHER * per):
            place = positions[first * per + pair] ^ flip
            a = term[2 * pair * ROWS : (2 * pair + 1) * ROWS]
            b = term[(2 * pair + 1) * ROWS : (2 * pair + 2) * ROWS]
            keep_ref[place] = jnp.where(core == 0, a, b)
            send_ref[place] = jnp.where(core == 0, b, a).astype(jnp.bfloat16)


def feature_grad_kernel(plan_ref, grad_ref, near_ref, far_ref, w_ref, out_ref, g_all, acc):
    core = plan_ref[0, CORE]
    near, far = near_ref[...], far_ref[...]
    g_all[:BND] = jnp.where(core == 0, far, near)
    g_all[BND : BND + OUT_BLK] = grad_ref[...]
    g_all[BND + OUT_BLK : EXT] = jnp.where(core == 0, near, far)
    g_all[EXT] = jnp.zeros((BR, CO), jnp.bfloat16)
    acc[...] = jnp.zeros_like(acc)
    for offset in range(OFFS):
        codes = [plan_ref[offset, BACK + j] for j in range(SLOTS)]
        rules = [(code >> 4, code & 15) for code in codes]
        grads = jnp.concatenate([g_all[slot] for _, slot in rules], 0)
        kernel = w_ref[offset * CI : (offset + 1) * CI]
        back = lax.dot_general(
            grads, kernel, (((1,), (1,)), ((), ())), preferred_element_type=jnp.float32
        )
        for j, (i, _) in enumerate(rules):
            acc[i] += back[j * BR : (j + 1) * BR]
    out_ref[...] = acc[...].astype(jnp.bfloat16)


def call(kernel, name, in_specs, out_shape, scratch, flops, moved, aliases={}):
    return pl.pallas_call(
        kernel,
        name=name,
        out_shape=out_shape,
        in_specs=in_specs,
        out_specs=jax.tree.map(lambda _: VMEM, out_shape),
        scratch_shapes=scratch,
        input_output_aliases=aliases,
        compiler_params=pltpu.CompilerParams(vmem_limit_bytes=24 * 1024 * 1024),
        cost_estimate=pl.CostEstimate(flops=flops, bytes_accessed=moved, transcendentals=0),
    )


def shape(dims, dtype=jnp.bfloat16):
    return jax.ShapeDtypeStruct(dims, dtype)


def codes_of(tables, counts, slab):
    valid = jnp.arange(SLOTS, dtype=jnp.int32) < counts[:, None]
    return jnp.where(valid & (tables[2] == slab), tables[0] * 8 + tables[1], OUT_BLK)


def back_codes_of(tables, counts, slab):
    valid = jnp.arange(SLOTS, dtype=jnp.int32) < counts[:, None]
    slot = BND + tables[1] + (tables[2] - slab) * OUT_BLK
    return tables[0] * 16 + jnp.where(valid, slot, EXT)


def tail_of(halo):
    tail = halo[IN_ROWS:, :SLOTS].astype(jnp.int32)
    return tail[: 3 * OFFS].reshape(3, OFFS, SLOTS), tail[3 * OFFS]


def local(features, weight, rulebook, rule_counts, cotangent):
    dp, space = lax.axis_size("dp"), lax.axis_size("space")
    devices = dp * space
    groups = phases_of(dp, space)
    rows = weight.shape[0]
    slab = lax.axis_index("space").astype(jnp.int32)
    me = lax.axis_index("dp").astype(jnp.int32) * space + slab
    direct = rows == ROWS

    own_rules = jnp.swapaxes(rulebook[0], 0, 1)
    halo = pl.pallas_call(
        pack_kernel,
        name="pack",
        out_shape=pltpu.VMEM((IN_ROWS + TAIL, CI), jnp.bfloat16),
        in_specs=[pl.BlockSpec(memory_space=pltpu.HBM)] * 3,
        out_specs=VMEM,
        scratch_shapes=[
            pltpu.VMEM((3, OFFS, SLOTS), jnp.int32),
            pltpu.VMEM((1, OFFS), jnp.int32),
            pltpu.VMEM((TAIL, CI), jnp.float32),
            pltpu.SemaphoreType.DMA((3,)),
        ],
        cost_estimate=pl.CostEstimate(flops=0, bytes_accessed=1 << 20, transcendentals=0),
    )(*[pltpu.with_memory_space_constraint(v, pltpu.HBM) for v in (features[0], own_rules, rule_counts)])

    own_weight = pl.pallas_call(
        fetch_kernel,
        name="fetch",
        out_shape=pltpu.VMEM((rows, CO), jnp.bfloat16),
        in_specs=[pl.BlockSpec(memory_space=pltpu.HBM)],
        out_specs=VMEM,
        scratch_shapes=[pltpu.SemaphoreType.DMA],
        cost_estimate=pl.CostEstimate(flops=0, bytes_accessed=1 << 16, transcendentals=0),
    )(pltpu.with_memory_space_constraint(weight, pltpu.HBM))

    parts = weight[None]
    for group in groups[:-1]:
        received = [exchange(parts, mask, devices) for mask in masks_of(group)]
        if group is groups[0]:
            near_slab, far_slab = exchange(halo, 1, devices), swap_far(halo)
        if group is groups[1]:
            flip = position_of(me & -2, groups) if direct else jnp.zeros((), jnp.int32)
            own = (own_rules, rule_counts[0], slab)
            scalars = jnp.broadcast_to(jnp.stack([slab & 1, flip]), (OFFS, 2))
            plan = jnp.concatenate(
                [codes_of(*own), codes_of(*tail_of(near_slab), slab), back_codes_of(*own), scalars], 1
            )
            sum_shapes = (shape((OFFS, OUT_BLK, BR, CI)), shape((OFFS, OUT_BLK, CI, BR)))
            sums = call(
                sum_kernel,
                "block_sums",
                [SMEM] + [VMEM] * 2,
                sum_shapes,
                [pltpu.VMEM((OUT_BLK + 1, BR, CI), jnp.float32)],
                0,
                1 << 23,
            )(plan, halo, near_slab)
            parts, sums = lax.optimization_barrier((parts, sums))
        if group is groups[0]:
            parts = own_weight[None]
        parts = jnp.concatenate([parts] + received, 0)
    far = exchange(parts, groups[-1][0], devices)
    far_plan = codes_of(*tail_of(far_slab), slab)

    if direct:
        near = parts
        positions = [position_of(2 * pair, groups) for pair in range(PAIRS)]
    else:
        ids = np.arange(devices, dtype=np.int32)
        order = position_of(ids ^ me, groups)
        whole = jnp.concatenate([parts, far], 0)[order].reshape(PAIRS, 2, ROWS, CO)
        swapped = jnp.where((slab & 1) == 0, whole, whole[:, ::-1])
        near, far = swapped[:, 0], swapped[:, 1]
        positions = list(range(PAIRS))

    rule_flops = 2 * OFFS * SLOTS * BR * CI * CO
    sums = call(
        far_sum_kernel,
        "far_sums",
        [SMEM] + [VMEM] * 3,
        sum_shapes,
        [],
        0,
        1 << 20,
        {2: 0, 3: 1},
    )(far_plan, far_slab, *sums)
    activated, grad_pre, near_grad, far_grad, keep, send, kernels = call(
        functools.partial(main_kernel, positions),
        "forward_and_weight_grad",
        [SMEM] + [VMEM] * 5,
        (
            pltpu.VMEM((OUT_BLK, BR, CO), jnp.bfloat16),
            shape((OUT_BLK, BR, CO)),
            shape((BND, BR, CO)),
            shape((BND, BR, CO)),
            shape((PAIRS, ROWS, CO), jnp.float32),
            shape((PAIRS, ROWS, CO)),
            shape((OFFS * CI, CO)),
        ),
        [],
        rule_flops,
        1 << 22,
    )(plan, *sums, near, far, cotangent[0].reshape(OUT_BLK, BR, CO))

    if not direct:
        terms = jnp.stack([keep, send.astype(jnp.float32)], 1)
        terms = jnp.where((slab & 1) == 0, terms, terms[:, ::-1]).reshape(devices, rows, CO)
        source = np.argsort(position_of(ids, groups)).astype(np.int32) ^ me
        ordered = terms[source]
        keep, send = ordered[: devices // 2], ordered[devices // 2 :].astype(jnp.bfloat16)
    total = keep + exchange(send, groups[-1][0], devices).astype(jnp.float32)

    near_rim = exchange(near_grad, 1, devices)
    far_rim = swap_far(far_grad)
    grad_in = call(
        feature_grad_kernel,
        "feature_grad",
        [SMEM] + [VMEM] * 4,
        shape((IN_BLK, BR, CI)),
        [
            pltpu.VMEM((EXT + 1, BR, CO), jnp.bfloat16),
            pltpu.VMEM((IN_BLK, BR, CI), jnp.float32),
        ],
        rule_flops,
        1 << 22,
    )(plan, grad_pre, near_rim, far_rim, kernels)

    for group in reversed(groups[:-1]):
        masks = masks_of(group)
        count = total.shape[0] // (len(masks) + 1)
        received = [
            exchange(total[(r + 1) * count : (r + 2) * count].astype(jnp.bfloat16), mask, devices)
            for r, mask in enumerate(masks)
        ]
        total = total[:count]
        for piece in received:
            total = total + piece.astype(jnp.float32)
    grad_weight = total[0] * grad_scale
    return (
        activated.reshape(1, OUT_BLK * BR, CO),
        grad_in.reshape(1, IN_ROWS, CI),
        grad_weight,
    )


def solution(mesh):
    in_specs = (
        P("dp", "space", None),
        P(("dp", "space"), None),
        P("dp", "space", None, None),
        P("dp", "space"),
        P("dp", "space", None),
    )
    out_specs = (P("dp", "space", None), P("dp", "space", None), P(("dp", "space"), None))
    return jax.shard_map(local, mesh=mesh, in_specs=in_specs, out_specs=out_specs, check_vma=False)
```

```python
import functools

import jax
import jax.numpy as jnp
import numpy as np
from jax import lax
from jax.experimental import pallas as pl
from jax.experimental.pallas import tpu as pltpu
from jax.sharding import PartitionSpec as P

CI = 256
CO = 256
OFFS = 8
BR = 128
BND = 2
SLOTS = 8
IN_BLK = 8
OUT_BLK = 4
EXT = OUT_BLK + 2 * BND
IN_ROWS = IN_BLK * BR
TAIL = 32
TOGETHER = 4
AXES = ("dp", "space")
BACK = 2 * SLOTS
CORE = BACK + SLOTS
FLIP = CORE + 1
PAIRS = 16
ROWS = OFFS * CI // (2 * PAIRS)

grad_scale = 1.0 / 2048.0

VMEM = pl.BlockSpec(memory_space=pltpu.VMEM)
SMEM = pl.BlockSpec(memory_space=pltpu.SMEM)


def phases_of(dp, space):
    space_bits = [1 << b for b in reversed(range(space.bit_length() - 1))]
    dp_bits = [space << b for b in reversed(range(dp.bit_length() - 1))]
    order = space_bits[:-1:2] + space_bits[1:-1:2] + dp_bits
    return [order[i : i + 2] for i in range(0, len(order), 2)] + [space_bits[-1:]]


def masks_of(group):
    if len(group) == 1:
        return list(group)
    return [group[0] | group[1], group[1], group[0]]


def position_of(index, groups):
    place, t = 0, 0
    for group in groups:
        bits = [(index >> (bit.bit_length() - 1)) & 1 for bit in group]
        digit = bits[0] if len(group) == 1 else bits[0] | ((bits[0] ^ bits[1]) << 1)
        place = place | (digit << t)
        t += len(group)
    return place


def exchange(value, mask, devices):
    return lax.ppermute(value, AXES, [(i, i ^ mask) for i in range(devices)])


def swap_far(value):
    count = lax.axis_size("space")
    pairs = [(s, s + 1) for s in range(1, count - 1, 2)]
    return lax.ppermute(value, "space", pairs + [(t, s) for s, t in pairs])


def pack_kernel(x_hbm, rules_hbm, counts_hbm, halo_ref, rules, counts, tail, sems):
    copies = [
        pltpu.make_async_copy(x_hbm, halo_ref.at[:IN_ROWS], sems.at[0]),
        pltpu.make_async_copy(rules_hbm, rules, sems.at[1]),
        pltpu.make_async_copy(counts_hbm, counts, sems.at[2]),
    ]
    for copy in copies:
        copy.start()
    tail[...] = jnp.zeros_like(tail)
    copies[1].wait()
    for part in range(3):
        tail[OFFS * part : OFFS * (part + 1), :SLOTS] = rules[part].astype(jnp.float32)
    copies[2].wait()
    tail[3 * OFFS : 3 * OFFS + 1, :OFFS] = counts[...].astype(jnp.float32)
    halo_ref[IN_ROWS:] = tail[...].astype(jnp.bfloat16)
    copies[0].wait()


def fetch_kernel(weight_hbm, weight_ref, sem):
    copy = pltpu.make_async_copy(weight_hbm, weight_ref, sem)
    copy.start()
    copy.wait()


def block_at(ref, index):
    return ref[pl.ds(pl.multiple_of(index * BR, BR), BR)]


def sum_kernel(plan_ref, x_ref, a_ref, s_ref, st_ref, acc):
    for offset in range(OFFS):
        acc[...] = jnp.zeros_like(acc)
        for ref, first in ((x_ref, 0), (a_ref, SLOTS)):

            @pl.loop(0, SLOTS)
            def _(j, ref=ref, first=first, offset=offset):
                code = plan_ref[offset, first + j]

                @pl.when((code & 7) != OUT_BLK)
                def _():
                    acc[code & 7] += block_at(ref, code >> 3).astype(jnp.float32)

        for t in range(OUT_BLK):
            block = acc[t].astype(jnp.bfloat16)
            s_ref[offset, t] = block
            st_ref[offset, t] = block.T


def far_sum_kernel(far_plan_ref, b_ref, _, __, s_ref, st_ref):
    for offset in range(OFFS):

        @pl.loop(0, SLOTS)
        def _(j, offset=offset):
            code = far_plan_ref[offset, j]

            @pl.when((code & 7) != OUT_BLK)
            def _():
                t = code & 7
                extra = block_at(b_ref, code >> 3).astype(jnp.float32)
                block = (s_ref[offset, t].astype(jnp.float32) + extra).astype(jnp.bfloat16)
                s_ref[offset, t] = block
                st_ref[offset, t] = block.T


def main_kernel(
    positions, plan_ref, s_ref, st_ref, near_ref, far_ref, cot_ref,
    act_ref, grad_ref, near_grad_ref, far_grad_ref, keep_ref, send_ref, w_ref,
):
    core, flip = plan_ref[0, CORE], plan_ref[0, FLIP]
    for pair, position in enumerate(positions):
        place = position ^ flip
        a, b = near_ref[place], far_ref[place]
        w_ref[2 * pair * ROWS : (2 * pair + 1) * ROWS] = jnp.where(core == 0, a, b)
        w_ref[(2 * pair + 1) * ROWS : (2 * pair + 2) * ROWS] = jnp.where(core == 0, b, a)
    sums = jnp.concatenate([s_ref[k].reshape(OUT_BLK * BR, CI) for k in range(OFFS)], 1)
    pre = jnp.dot(sums, w_ref[...], preferred_element_type=jnp.float32)
    pre = pre.reshape(OUT_BLK, BR, CO)
    sigma = jax.nn.sigmoid(pre)
    act_ref[...] = (pre * sigma).astype(jnp.bfloat16)
    upstream = cot_ref[...].astype(jnp.float32)
    grad = (upstream * sigma * (1.0 + pre * (1.0 - sigma))).astype(jnp.bfloat16)
    grad_ref[...] = grad
    low, high = grad[:BND], grad[OUT_BLK - BND :]
    near_grad_ref[...] = jnp.where(core == 0, high, low)
    far_grad_ref[...] = jnp.where(core == 0, low, high)
    grads = grad_ref[...].reshape(OUT_BLK * BR, CO)
    per = CI // (2 * ROWS)
    for first in range(0, OFFS, TOGETHER):
        left = [
            jnp.concatenate([st_ref[offset, t] for t in range(OUT_BLK)], 1)
            for offset in range(first, first + TOGETHER)
        ]
        term = jnp.dot(jnp.concatenate(left, 0), grads, preferred_element_type=jnp.float32)
        for pair in range(TOGETHER * per):
            place = positions[first * per + pair] ^ flip
            a = term[2 * pair * ROWS : (2 * pair + 1) * ROWS]
            b = term[(2 * pair + 1) * ROWS : (2 * pair + 2) * ROWS]
            keep_ref[place] = jnp.where(core == 0, a, b)
            send_ref[place] = jnp.where(core == 0, b, a).astype(jnp.bfloat16)


def feature_grad_kernel(plan_ref, grad_ref, near_ref, far_ref, w_ref, out_ref, g_all, acc):
    core = plan_ref[0, CORE]
    near, far = near_ref[...], far_ref[...]
    g_all[:BND] = jnp.where(core == 0, far, near)
    g_all[BND : BND + OUT_BLK] = grad_ref[...]
    g_all[BND + OUT_BLK : EXT] = jnp.where(core == 0, near, far)
    g_all[EXT] = jnp.zeros((BR, CO), jnp.bfloat16)
    acc[...] = jnp.zeros_like(acc)
    for offset in range(OFFS):
        codes = [plan_ref[offset, BACK + j] for j in range(SLOTS)]
        rules = [(code >> 4, code & 15) for code in codes]
        grads = jnp.concatenate([g_all[slot] for _, slot in rules], 0)
        kernel = w_ref[offset * CI : (offset + 1) * CI]
        back = lax.dot_general(
            grads, kernel, (((1,), (1,)), ((), ())), preferred_element_type=jnp.float32
        )
        for j, (i, _) in enumerate(rules):
            acc[i] += back[j * BR : (j + 1) * BR]
    out_ref[...] = acc[...].astype(jnp.bfloat16)


def call(kernel, name, in_specs, out_shape, scratch, flops, moved, aliases={}):
    return pl.pallas_call(
        kernel,
        name=name,
        out_shape=out_shape,
        in_specs=in_specs,
        out_specs=jax.tree.map(lambda _: VMEM, out_shape),
        scratch_shapes=scratch,
        input_output_aliases=aliases,
        compiler_params=pltpu.CompilerParams(vmem_limit_bytes=24 * 1024 * 1024),
        cost_estimate=pl.CostEstimate(flops=flops, bytes_accessed=moved, transcendentals=0),
    )


def shape(dims, dtype=jnp.bfloat16):
    return jax.ShapeDtypeStruct(dims, dtype)


def codes_of(tables, counts, slab):
    valid = jnp.arange(SLOTS, dtype=jnp.int32) < counts[:, None]
    return jnp.where(valid & (tables[2] == slab), tables[0] * 8 + tables[1], OUT_BLK)


def back_codes_of(tables, counts, slab):
    valid = jnp.arange(SLOTS, dtype=jnp.int32) < counts[:, None]
    slot = BND + tables[1] + (tables[2] - slab) * OUT_BLK
    return tables[0] * 16 + jnp.where(valid, slot, EXT)


def tail_of(halo):
    tail = halo[-TAIL:, :SLOTS].astype(jnp.int32)
    return tail[: 3 * OFFS].reshape(3, OFFS, SLOTS), tail[3 * OFFS]


def local(features, weight, rulebook, rule_counts, cotangent):
    dp, space = lax.axis_size("dp"), lax.axis_size("space")
    devices = dp * space
    groups = phases_of(dp, space)
    rows = weight.shape[0]
    slab = lax.axis_index("space").astype(jnp.int32)
    me = lax.axis_index("dp").astype(jnp.int32) * space + slab
    direct = rows == ROWS

    own_rules = jnp.swapaxes(rulebook[0], 0, 1)
    halo = pl.pallas_call(
        pack_kernel,
        name="pack",
        out_shape=pltpu.VMEM((IN_ROWS + TAIL, CI), jnp.bfloat16),
        in_specs=[pl.BlockSpec(memory_space=pltpu.HBM)] * 3,
        out_specs=VMEM,
        scratch_shapes=[
            pltpu.VMEM((3, OFFS, SLOTS), jnp.int32),
            pltpu.VMEM((1, OFFS), jnp.int32),
            pltpu.VMEM((TAIL, CI), jnp.float32),
            pltpu.SemaphoreType.DMA((3,)),
        ],
        cost_estimate=pl.CostEstimate(flops=0, bytes_accessed=1 << 20, transcendentals=0),
    )(*[pltpu.with_memory_space_constraint(v, pltpu.HBM) for v in (features[0], own_rules, rule_counts)])

    own_weight = pl.pallas_call(
        fetch_kernel,
        name="fetch",
        out_shape=pltpu.VMEM((rows, CO), jnp.bfloat16),
        in_specs=[pl.BlockSpec(memory_space=pltpu.HBM)],
        out_specs=VMEM,
        scratch_shapes=[pltpu.SemaphoreType.DMA],
        cost_estimate=pl.CostEstimate(flops=0, bytes_accessed=1 << 16, transcendentals=0),
    )(pltpu.with_memory_space_constraint(weight, pltpu.HBM))

    parts = weight[None]
    for group in groups[:-1]:
        received = [exchange(parts, mask, devices) for mask in masks_of(group)]
        if group is groups[0]:
            near_slab, far_slab = exchange(features[0], 1, devices), swap_far(halo)
            near_tail = exchange(halo[IN_ROWS:], 1, devices)
        if group is groups[1]:
            flip = position_of(me & -2, groups) if direct else jnp.zeros((), jnp.int32)
            own = (own_rules, rule_counts[0], slab)
            scalars = jnp.broadcast_to(jnp.stack([slab & 1, flip]), (OFFS, 2))
            plan = jnp.concatenate(
                [codes_of(*own), codes_of(*tail_of(near_tail), slab), back_codes_of(*own), scalars], 1
            )
            sum_shapes = (shape((OFFS, OUT_BLK, BR, CI)), shape((OFFS, OUT_BLK, CI, BR)))
            sums = call(
                sum_kernel,
                "block_sums",
                [SMEM] + [VMEM] * 2,
                sum_shapes,
                [pltpu.VMEM((OUT_BLK + 1, BR, CI), jnp.float32)],
                0,
                1 << 23,
            )(plan, halo, near_slab)
            parts, sums = lax.optimization_barrier((parts, sums))
        if group is groups[0]:
            parts = own_weight[None]
        parts = jnp.concatenate([parts] + received, 0)
    far = exchange(parts, groups[-1][0], devices)
    far_plan = codes_of(*tail_of(far_slab), slab)

    if direct:
        near = parts
        positions = [position_of(2 * pair, groups) for pair in range(PAIRS)]
    else:
        ids = np.arange(devices, dtype=np.int32)
        order = position_of(ids ^ me, groups)
        whole = jnp.concatenate([parts, far], 0)[order].reshape(PAIRS, 2, ROWS, CO)
        swapped = jnp.where((slab & 1) == 0, whole, whole[:, ::-1])
        near, far = swapped[:, 0], swapped[:, 1]
        positions = list(range(PAIRS))

    rule_flops = 2 * OFFS * SLOTS * BR * CI * CO
    sums = call(
        far_sum_kernel,
        "far_sums",
        [SMEM] + [VMEM] * 3,
        sum_shapes,
        [],
        0,
        1 << 20,
        {2: 0, 3: 1},
    )(far_plan, far_slab, *sums)
    activated, grad_pre, near_grad, far_grad, keep, send, kernels = call(
        functools.partial(main_kernel, positions),
        "forward_and_weight_grad",
        [SMEM] + [VMEM] * 5,
        (
            pltpu.VMEM((OUT_BLK, BR, CO), jnp.bfloat16),
            shape((OUT_BLK, BR, CO)),
            shape((BND, BR, CO)),
            shape((BND, BR, CO)),
            shape((PAIRS, ROWS, CO), jnp.float32),
            shape((PAIRS, ROWS, CO)),
            shape((OFFS * CI, CO)),
        ),
        [],
        rule_flops,
        1 << 22,
    )(plan, *sums, near, far, cotangent[0].reshape(OUT_BLK, BR, CO))

    if not direct:
        terms = jnp.stack([keep, send.astype(jnp.float32)], 1)
        terms = jnp.where((slab & 1) == 0, terms, terms[:, ::-1]).reshape(devices, rows, CO)
        source = np.argsort(position_of(ids, groups)).astype(np.int32) ^ me
        ordered = terms[source]
        keep, send = ordered[: devices // 2], ordered[devices // 2 :].astype(jnp.bfloat16)
    total = keep + exchange(send, groups[-1][0], devices).astype(jnp.float32)

    near_rim = exchange(near_grad, 1, devices)
    far_rim = swap_far(far_grad)
    grad_in = call(
        feature_grad_kernel,
        "feature_grad",
        [SMEM] + [VMEM] * 4,
        shape((IN_BLK, BR, CI)),
        [
            pltpu.VMEM((EXT + 1, BR, CO), jnp.bfloat16),
            pltpu.VMEM((IN_BLK, BR, CI), jnp.float32),
        ],
        rule_flops,
        1 << 22,
    )(plan, grad_pre, near_rim, far_rim, kernels)

    for group in reversed(groups[:-1]):
        masks = masks_of(group)
        count = total.shape[0] // (len(masks) + 1)
        received = [
            exchange(total[(r + 1) * count : (r + 2) * count].astype(jnp.bfloat16), mask, devices)
            for r, mask in enumerate(masks)
        ]
        total = total[:count]
        for piece in received:
            total = total + piece.astype(jnp.float32)
    grad_weight = total[0] * grad_scale
    return (
        activated.reshape(1, OUT_BLK * BR, CO),
        grad_in.reshape(1, IN_ROWS, CI),
        grad_weight,
    )


def solution(mesh):
    in_specs = (
        P("dp", "space", None),
        P(("dp", "space"), None),
        P("dp", "space", None, None),
        P("dp", "space"),
        P("dp", "space", None),
    )
    out_specs = (P("dp", "space", None), P("dp", "space", None), P(("dp", "space"), None))
    return jax.shard_map(local, mesh=mesh, in_specs=in_specs, out_specs=out_specs, check_vma=False)
```
